256 devices in a mesh: video: 8 (over y, core), audio: 16 (over z, x_hi), tp: 2 (over x_lo).
Axes of the slice: x: 4 (x_hi: 2, x_lo: 2; x = x_hi * 2 + x_lo), y: 4, z: 8, core: 2. Of those that a mesh axis runs over, the one named last changes fastest.
Arguments:
- query_video: bfloat16 [32768, 3072], P(('video', 'audio'), 'tp'), may hold values from -400 to 400
- key_video: bfloat16 [32768, 3072], P(('video', 'audio'), 'tp'), may hold values from -6 to 6
- value_video: bfloat16 [32768, 3072], P(('video', 'audio'), 'tp'), may hold values from -6 to 6
- query_audio: bfloat16 [4096, 3072], P(('video', 'audio'), 'tp'), may hold values from -400 to 400
- key_audio: bfloat16 [4096, 3072], P(('video', 'audio'), 'tp'), may hold values from -6 to 6
- value_audio: bfloat16 [4096, 3072], P(('video', 'audio'), 'tp'), may hold values from -6 to 6
- conv_video: float32 [3, 3072], P(None, 'tp'), may hold values from -3 to 3
- conv_audio: float32 [3, 3072], P(None, 'tp'), may hold values from -3 to 3
- gain_video: float32 [3072], P('tp'), may hold values from 0.1 to 1.9
- gain_audio: float32 [3072], P('tp'), may hold values from 0.1 to 1.9
- video_window: int32 [128, 2], replicated, may hold values from 0 to 4096, as said below
- audio_window: int32 [128, 2], replicated, may hold values from 0 to 32768, as said below
- video_valid: int32 [128], replicated, may hold values from 65 to 256
- audio_valid: int32 [128], replicated, may hold values from 9 to 32
- cotangent_video: bfloat16 [32768, 3072], P(('video', 'audio'), 'tp'), may hold values from -6 to 6
- cotangent_audio: bfloat16 [4096, 3072], P(('video', 'audio'), 'tp'), may hold values from -6 to 6
Outputs:
- output_video: bfloat16 [32768, 3072], P(('video', 'audio'), 'tp')
- output_audio: bfloat16 [4096, 3072], P(('video', 'audio'), 'tp')
- query_grad_video: bfloat16 [32768, 3072], P(('video', 'audio'), 'tp')
- key_grad_video: bfloat16 [32768, 3072], P(('video', 'audio'), 'tp')
- value_grad_video: bfloat16 [32768, 3072], P(('video', 'audio'), 'tp')
- query_grad_audio: bfloat16 [4096, 3072], P(('video', 'audio'), 'tp')
- key_grad_audio: bfloat16 [4096, 3072], P(('video', 'audio'), 'tp')
- value_grad_audio: bfloat16 [4096, 3072], P(('video', 'audio'), 'tp')
- taps_grad_video: float32 [3, 3072], P(None, 'tp')
- taps_grad_audio: float32 [3, 3072], P(None, 'tp')
- gain_grad_video: float32 [3072], P('tp')
- gain_grad_audio: float32 [3072], P('tp')
The draws below stay inside these ranges and needn't reach their ends.
Inputs may be any that keep to these rules, and one draw needn't show every extreme that they name: video_window[b] = [lower, upper) contains all audio tokens of block b; lower lies in block b - 1 (0 for b = 0) and upper - 1 in block b + 1 (upper = 4096 for the last block). audio_window[c] = [lower, upper) contains all video tokens of block c; lower lies in block c - 1 (0 for c = 0) and upper - 1 in block c + 1 (upper = 32768 for the last block).
All inputs are finite; a program needn't handle non-finite values.
Results may differ from the reference program's by a relative error of at most 0.022.
Values may be sent and summed in bfloat16 or wider, within the bound.
No kernel may reach another device: no remote copies, remote signals or barrier semaphores. Data moves between devices by JAX's collectives and lax.ppermute only.
A program may use at most 128 MiB of HBM per device.

```python
import jax
import jax.numpy as jnp
from jax import lax

HEAD_DIM = 128
D = 3072
TV_DEV = 256
TA_DEV = 32
STRIDE = 32
TAPS = 3
NB = 128
TV = 32768
TA = 4096


def scaled_rows(key, rows, width, reach):
    base = jax.random.normal(key, (rows, width), jnp.float32)
    boost = jnp.exp(jax.random.uniform(jax.random.fold_in(key, 7), (rows, 1), jnp.float32, 0.0, reach))
    return jnp.clip(base * boost, -400.0, 400.0)


def bound_pairs(key, key_rows):
    blocks = jnp.arange(NB, dtype=jnp.int32)
    before = jax.random.randint(jax.random.fold_in(key, 1), (NB,), key_rows - key_rows // 8, key_rows + 1, dtype=jnp.int32)
    beyond = jax.random.randint(jax.random.fold_in(key, 2), (NB,), 1, key_rows + 1, dtype=jnp.int32)
    lower = jnp.maximum(blocks * key_rows - before, 0)
    upper = jnp.minimum((blocks + 1) * key_rows + beyond, NB * key_rows)
    return jnp.stack([lower, upper], 1).astype(jnp.int32)


def full_counts(key, rows):
    counts = jax.random.randint(jax.random.fold_in(key, 1), (NB,), rows // 4 + 1, rows + 1, dtype=jnp.int32)
    chosen = jax.random.randint(jax.random.fold_in(key, 2), (), 0, NB, dtype=jnp.int32)
    return jnp.where(jnp.arange(NB, dtype=jnp.int32) == chosen, rows, counts).astype(jnp.int32)


def draw_query_video(key, part):
    key = jax.random.fold_in(key, 21)
    return scaled_rows(key, TV, D, 0.7).astype(jnp.bfloat16)


def draw_query_audio(key, part):
    key = jax.random.fold_in(key, 22)
    return scaled_rows(key, TA, D, 0.7).astype(jnp.bfloat16)


def draw_video_window(key, part):
    key = jax.random.fold_in(key, 31)
    return bound_pairs(key, TA_DEV)


def draw_audio_window(key, part):
    key = jax.random.fold_in(key, 32)
    return bound_pairs(key, TV_DEV)


def draw_video_valid(key, part):
    key = jax.random.fold_in(key, 41)
    return full_counts(key, TV_DEV)


def draw_audio_valid(key, part):
    key = jax.random.fold_in(key, 42)
    return full_counts(key, TA_DEV)


def steps_of(stream_key, shape, split, low, high):
    def one(axis_at, parts):
        steps = jax.random.uniform(jax.random.fold_in(jax.random.fold_in(stream_key, 6), axis_at), (parts,), jnp.float32, low / len(split), high / len(split))
        return jnp.repeat(jnp.exp(steps), shape[axis_at] // parts).reshape((-1,) + (1,) * (len(shape) - axis_at - 1))

    gain = one(*split[0])
    for cut in split[1:]:
        gain = gain * one(*cut)
    return gain


def scatter_about(stream_key, shape, scale, limit, split=(), held_as=jnp.bfloat16):
    gain = steps_of(stream_key, shape, split, -0.22, 0.18) if split else 1.0
    entries = jax.random.normal(stream_key, shape, jnp.float32) * scale * gain
    return jnp.minimum(jnp.maximum(entries, -limit), limit).astype(held_as)


def setup_inputs(seed: int = 0) -> dict:
    splits = jax.random.split(jax.random.key(seed), 17)
    query_video = draw_query_video(jax.random.fold_in(splits[16], 71), 0)
    key_video = scatter_about(splits[1], (TV, D), 1.0, 6.0, ((0, 128), (1, 2)))
    value_video = scatter_about(splits[2], (TV, D), 1.0, 6.0, ((0, 128), (1, 2)))
    query_audio = draw_query_audio(jax.random.fold_in(splits[16], 71), 0)
    key_audio = scatter_about(splits[4], (TA, D), 1.0, 6.0, ((0, 128), (1, 2)))
    value_audio = scatter_about(splits[5], (TA, D), 1.0, 6.0, ((0, 128), (1, 2)))
    conv_video = scatter_about(splits[6], (TAPS, D), 0.6, 3.0, ((1, 2),), jnp.float32)
    conv_audio = scatter_about(splits[7], (TAPS, D), 0.6, 3.0, ((1, 2),), jnp.float32)
    gain_video = jnp.clip(1.0 + 0.18 * jax.random.normal(splits[8], (D,), jnp.float32), 0.1, 1.9)
    gain_audio = jnp.clip(1.0 + 0.18 * jax.random.normal(splits[9], (D,), jnp.float32), 0.1, 1.9)
    video_window = draw_video_window(jax.random.fold_in(splits[16], 71), 0)
    audio_window = draw_audio_window(jax.random.fold_in(splits[16], 71), 0)
    video_valid = draw_video_valid(jax.random.fold_in(splits[16], 71), 0)
    audio_valid = draw_audio_valid(jax.random.fold_in(splits[16], 71), 0)
    cotangent_video = scatter_about(splits[14], (TV, D), 1.0, 6.0, ((0, 128), (1, 2)))
    cotangent_audio = scatter_about(splits[15], (TA, D), 1.0, 6.0, ((0, 128), (1, 2)))
    return dict(query_video=query_video, key_video=key_video, value_video=value_video, query_audio=query_audio, key_audio=key_audio, value_audio=value_audio, conv_video=conv_video, conv_audio=conv_audio, gain_video=gain_video, gain_audio=gain_audio, video_window=video_window, audio_window=audio_window, video_valid=video_valid, audio_valid=audio_valid, cotangent_video=cotangent_video, cotangent_audio=cotangent_audio)


NEGATIVE = -1e+30
EPSILON = 1e-06

def split_heads(rows):
    return rows.reshape(rows.shape[0], -1, HEAD_DIM).astype(jnp.float32)

def join_heads(heads):
    return heads.reshape(heads.shape[0], -1)

def padded_rows(array, width):
    return jnp.pad(array, ((width, width), (0, 0)))

def key_visible(window, valid, block, key_rows):
    zero_index = jnp.zeros((), jnp.int32)
    bounds = lax.dynamic_slice(window, (block, zero_index), (1, 2))
    valid_pad = jnp.concatenate([jnp.zeros((1,), jnp.int32), valid, jnp.zeros((1,), jnp.int32)])
    valid_three = jnp.repeat(lax.dynamic_slice(valid_pad, (block,), (3,)), key_rows)
    offsets = jnp.arange(3 * key_rows, dtype=jnp.int32)
    position = (block - 1) * key_rows + offsets
    return (position >= bounds[0, 0]) & (position < bounds[0, 1]) & (offsets % key_rows < valid_three)

def attend_forward(queries, keys, values, window, valid):
    query_rows = queries.shape[0] // NB
    key_rows = keys.shape[0] // NB
    keys_pad = padded_rows(keys, key_rows)
    values_pad = padded_rows(values, key_rows)
    factor = HEAD_DIM ** (-0.5)

    def one_block(block):
        rows = split_heads(lax.dynamic_slice_in_dim(queries, block * query_rows, query_rows, 0))
        near_keys = split_heads(lax.dynamic_slice_in_dim(keys_pad, block * key_rows, 3 * key_rows, 0))
        near_values = split_heads(lax.dynamic_slice_in_dim(values_pad, block * key_rows, 3 * key_rows, 0))
        visible = key_visible(window, valid, block, key_rows)
        scores = jnp.einsum('qhd,khd->hqk', rows, near_keys) * factor
        scores = jnp.where(visible[None, None, :], scores, NEGATIVE)
        peak = lax.optimization_barrier(jnp.max(scores, axis=-1, keepdims=True))
        log_total = peak[..., 0] + jnp.log(lax.optimization_barrier(jnp.sum(jnp.exp(scores - peak), axis=-1)))
        prob_round = jnp.exp(scores - log_total[..., None]).astype(jnp.bfloat16)
        attended = jnp.einsum('hqk,khd->qhd', prob_round.astype(jnp.float32), near_values)
        return (join_heads(attended).astype(jnp.bfloat16), log_total)
    attended, log_total = lax.map(one_block, jnp.arange(NB, dtype=jnp.int32))
    totals = jnp.transpose(log_total, (1, 0, 2)).reshape(log_total.shape[1], -1)
    return (attended.reshape(queries.shape), totals)

def query_grads(queries, keys, values, attended, upstream, totals, window, valid):
    query_rows = queries.shape[0] // NB
    key_rows = keys.shape[0] // NB
    keys_pad = padded_rows(keys, key_rows)
    values_pad = padded_rows(values, key_rows)
    factor = HEAD_DIM ** (-0.5)

    def one_block(block):
        rows = split_heads(lax.dynamic_slice_in_dim(queries, block * query_rows, query_rows, 0))
        grad_rows = split_heads(lax.dynamic_slice_in_dim(upstream, block * query_rows, query_rows, 0))
        out_rows = split_heads(lax.dynamic_slice_in_dim(attended, block * query_rows, query_rows, 0))
        total_rows = lax.dynamic_slice_in_dim(totals, block * query_rows, query_rows, 1)
        near_keys = split_heads(lax.dynamic_slice_in_dim(keys_pad, block * key_rows, 3 * key_rows, 0))
        near_values = split_heads(lax.dynamic_slice_in_dim(values_pad, block * key_rows, 3 * key_rows, 0))
        visible = key_visible(window, valid, block, key_rows)
        scores = jnp.einsum('qhd,khd->hqk', rows, near_keys) * factor
        scores = jnp.where(visible[None, None, :], scores, NEGATIVE)
        probability = jnp.exp(scores - total_rows[..., None])
        prob_grad = jnp.einsum('qhd,khd->hqk', grad_rows, near_values)
        row_dots = jnp.einsum('qhd,qhd->hq', grad_rows, out_rows)
        score_grad = (probability * (prob_grad - row_dots[..., None])).astype(jnp.bfloat16)
        query_grad = jnp.einsum('hqk,khd->qhd', score_grad.astype(jnp.float32), near_keys) * factor
        return (join_heads(query_grad).astype(jnp.bfloat16), row_dots)
    query_grad, row_dots = lax.map(one_block, jnp.arange(NB, dtype=jnp.int32))
    dots = jnp.transpose(row_dots, (1, 0, 2)).reshape(row_dots.shape[1], -1)
    return (query_grad.reshape(queries.shape), dots)

def key_grads(queries, keys, values, upstream, totals, dots, window, valid):
    query_rows = queries.shape[0] // NB
    key_rows = keys.shape[0] // NB
    factor = HEAD_DIM ** (-0.5)
    queries_pad = padded_rows(queries, query_rows)
    grads_pad = padded_rows(upstream, query_rows)
    totals_pad = jnp.pad(totals, ((0, 0), (query_rows, query_rows)))
    dots_pad = jnp.pad(dots, ((0, 0), (query_rows, query_rows)))
    window_pad = jnp.concatenate([jnp.zeros((1, 2), jnp.int32), window, jnp.zeros((1, 2), jnp.int32)], 0)

    def one_block(block):
        zero_index = jnp.zeros((), jnp.int32)
        near_rows = split_heads(lax.dynamic_slice_in_dim(queries_pad, block * query_rows, 3 * query_rows, 0))
        near_grads = split_heads(lax.dynamic_slice_in_dim(grads_pad, block * query_rows, 3 * query_rows, 0))
        near_totals = lax.dynamic_slice_in_dim(totals_pad, block * query_rows, 3 * query_rows, 1)
        near_dots = lax.dynamic_slice_in_dim(dots_pad, block * query_rows, 3 * query_rows, 1)
        own_keys = split_heads(lax.dynamic_slice_in_dim(keys, block * key_rows, key_rows, 0))
        own_values = split_heads(lax.dynamic_slice_in_dim(values, block * key_rows, key_rows, 0))
        bounds = lax.dynamic_slice(window_pad, (block, zero_index), (3, 2))
        lower = jnp.repeat(bounds[:, 0], query_rows)
        upper = jnp.repeat(bounds[:, 1], query_rows)
        offsets = jnp.arange(key_rows, dtype=jnp.int32)
        position = block * key_rows + offsets
        own_valid = lax.dynamic_slice(valid, (block,), (1,))[0]
        visible = (position[None, :] >= lower[:, None]) & (position[None, :] < upper[:, None]) & (offsets < own_valid)[None, :]
        scores = jnp.einsum('qhd,khd->hqk', near_rows, own_keys) * factor
        scores = jnp.where(visible[None], scores, NEGATIVE)
        probability = jnp.exp(scores - near_totals[..., None])
        prob_round = probability.astype(jnp.bfloat16)
        prob_grad = jnp.einsum('qhd,khd->hqk', near_grads, own_values)
        score_grad = (probability * (prob_grad - near_dots[..., None])).astype(jnp.bfloat16)
        key_grad = jnp.einsum('hqk,qhd->khd', score_grad.astype(jnp.float32), near_rows) * factor
        value_grad = jnp.einsum('hqk,qhd->khd', prob_round.astype(jnp.float32), near_grads)
        return (join_heads(key_grad).astype(jnp.bfloat16), join_heads(value_grad).astype(jnp.bfloat16))
    key_grad, value_grad = lax.map(one_block, jnp.arange(NB, dtype=jnp.int32))
    return (key_grad.reshape(keys.shape), value_grad.reshape(values.shape))

def shifted(rows, stride):
    zeros = jnp.zeros((stride, rows.shape[1]), rows.dtype)
    earlier = jnp.concatenate([zeros, rows[:-stride]], 0)
    later = jnp.concatenate([rows[stride:], zeros], 0)
    return (earlier, later)

def conv_norm(attended, taps, gains, cotangent, stride):
    signal = attended.astype(jnp.float32)
    earlier, later = shifted(signal, stride)
    mixed = taps[0] * earlier + taps[1] * signal + taps[2] * later
    inverse = lax.rsqrt(lax.optimization_barrier(jnp.sum(mixed * mixed, axis=-1)) / D + EPSILON)[:, None]
    output = (mixed * inverse * gains).astype(jnp.bfloat16)
    incoming = cotangent.astype(jnp.float32)
    scaled = incoming * gains
    gain_grad = lax.optimization_barrier(jnp.sum(incoming * mixed * inverse, axis=0))
    inner = lax.optimization_barrier(jnp.sum(scaled * mixed, axis=-1, keepdims=True))
    mixed_grad = inverse * scaled - mixed * inverse * inverse * inverse * inner / D
    grad_earlier, grad_later = shifted(mixed_grad, stride)
    upstream = (taps[0] * grad_later + taps[1] * mixed_grad + taps[2] * grad_earlier).astype(jnp.bfloat16)
    taps_grad = jnp.stack([lax.optimization_barrier(jnp.sum(mixed_grad * earlier, 0)), lax.optimization_barrier(jnp.sum(mixed_grad * signal, 0)), lax.optimization_barrier(jnp.sum(mixed_grad * later, 0))])
    return (output, upstream, taps_grad, gain_grad)

def reference(query_video, key_video, value_video, query_audio, key_audio, value_audio, conv_video, conv_audio, gain_video, gain_audio, video_window, audio_window, video_valid, audio_valid, cotangent_video, cotangent_audio):
    attended_video, total_video = attend_forward(query_video, key_audio, value_audio, video_window, audio_valid)
    attended_audio, total_audio = attend_forward(query_audio, key_video, value_video, audio_window, video_valid)
    output_video, upstream_video, taps_grad_video, gain_grad_video = conv_norm(attended_video, conv_video, gain_video, cotangent_video, STRIDE)
    output_audio, upstream_audio, taps_grad_audio, gain_grad_audio = conv_norm(attended_audio, conv_audio, gain_audio, cotangent_audio, 1)
    query_grad_video, dots_video = query_grads(query_video, key_audio, value_audio, attended_video, upstream_video, total_video, video_window, audio_valid)
    query_grad_audio, dots_audio = query_grads(query_audio, key_video, value_video, attended_audio, upstream_audio, total_audio, audio_window, video_valid)
    key_grad_audio, value_grad_audio = key_grads(query_video, key_audio, value_audio, upstream_video, total_video, dots_video, video_window, audio_valid)
    key_grad_video, value_grad_video = key_grads(query_audio, key_video, value_video, upstream_audio, total_audio, dots_audio, audio_window, video_valid)
    return (output_video, output_audio, query_grad_video, key_grad_video, value_grad_video, query_grad_audio, key_grad_audio, value_grad_audio, taps_grad_video, taps_grad_audio, gain_grad_video, gain_grad_audio)
```

```python
import jax
import jax.numpy as jnp
from jax import lax
from jax.experimental import pallas as pl
from jax.experimental.pallas import tpu as pltpu
from jax.sharding import PartitionSpec as P

HEAD_DIM = 128
STRIDE = 32
NEGATIVE = -1e30
EPSILON = 1e-06
FACTOR = HEAD_DIM ** (-0.5)
BLOCKS = ("video", "audio")
BF = jnp.bfloat16
F32 = jnp.float32
PAD = 128


def dot(a, b, over_a, over_b):
    return lax.dot_general(
        a, b, (((over_a,), (over_b,)), ((), ())), preferred_element_type=F32
    )


def call(kernel, outs, args, scalars, flops, scratch=()):
    vmem = pl.BlockSpec(memory_space=pltpu.VMEM)
    smem = pl.BlockSpec(memory_space=pltpu.SMEM)
    size = sum(a.size * a.dtype.itemsize for a in args)
    return pl.pallas_call(
        kernel,
        out_shape=[jax.ShapeDtypeStruct(s, d) for s, d in outs],
        in_specs=[smem] * len(scalars) + [vmem] * len(args),
        out_specs=[vmem] * len(outs),
        scratch_shapes=list(scratch),
        compiler_params=pltpu.CompilerParams(vmem_limit_bytes=48 * 1024 * 1024),
        cost_estimate=pl.CostEstimate(flops=flops, bytes_accessed=size, transcendentals=0),
    )(*scalars, *args)


def other(i, count):
    return (i + 2 * (i & 1) - 1 + count) & (count - 1)


def columns(h):
    return slice(h * HEAD_DIM, (h + 1) * HEAD_DIM)


def pack_stats(tile):
    high = tile.astype(BF).astype(F32)
    rest = tile - high
    middle = rest.astype(BF).astype(F32)
    low = rest - middle
    return (high + pltpu.roll(middle, 16, 1) + pltpu.roll(low, 32, 1)).astype(BF)


def unpack_stats(packed):
    wide = packed.astype(F32)
    return wide + (pltpu.roll(wide, PAD - 16, 1) + pltpu.roll(wide, PAD - 32, 1))


def audio_bias(i, count, window, valid, rows_q, rows_k):
    lane = lax.broadcasted_iota(jnp.int32, (rows_q, rows_k), 1)
    position = i * rows_k + lane
    parts = []
    for c in (i, i ^ 1, other(i, count)):
        seen = (position >= window[c, 0]) & (position < window[c, 1]) & (lane < valid[i])
        parts.append(jnp.where(seen, 0.0, NEGATIVE))
    return jnp.concatenate(parts, 0)


def video_bias(i, count, window, valid, rows_q, rows_k):
    row = lax.broadcasted_iota(jnp.int32, (rows_k, rows_q), 0)
    parts = []
    for c in (i, i ^ 1, other(i, count)):
        position = c * rows_k + row
        seen = (position >= window[i, 0]) & (position < window[i, 1]) & (row < valid[c])
        parts.append(jnp.where(seen, 0.0, NEGATIVE))
    return jnp.concatenate(parts, 0)


def audio_forward(count, idx, window, valid, q, qe, qo, k, v, send_e, send_o, own, own_lse):
    rows = q.shape[0]
    heads = q.shape[1] // HEAD_DIM
    bias = audio_bias(idx[0], count, window, valid, rows, k.shape[0])
    lane = lax.broadcasted_iota(jnp.int32, (3 * rows, PAD), 1)
    tile = jnp.zeros((3 * rows, PAD), F32)
    for h in range(heads):
        c = columns(h)
        near = jnp.concatenate([q[:, c], qe[:, c], qo[:, c]], 0)
        scores = dot(near, k[:, c], 1, 1) * FACTOR + bias
        peak = jnp.max(scores, 1, keepdims=True)
        weight = jnp.exp(scores - peak)
        total = jnp.sum(weight, 1, keepdims=True)
        part = dot(weight.astype(BF), v[:, c], 1, 0) / total
        tile = jnp.where(lane == h, peak + jnp.log(total), tile)
        own[:, c] = part[:rows]
        send_e[:, c] = part[rows : 2 * rows].astype(BF)
        send_o[:, c] = part[2 * rows :].astype(BF)
    own_lse[...] = tile[:rows]
    tail = slice(heads * HEAD_DIM, heads * HEAD_DIM + PAD)
    send_e[:, tail] = pack_stats(tile[rows : 2 * rows])
    send_o[:, tail] = pack_stats(tile[2 * rows :])


def video_forward(
    count, idx, window, valid, q, k, ke, ko, v, ve, vo, att, lse, send_e, send_o
):
    rows = q.shape[0]
    heads = q.shape[1] // HEAD_DIM
    i = idx[0]
    bias = video_bias(i, count, window, valid, rows, k.shape[0])
    lse[...] = jnp.zeros(lse.shape, F32)
    for h in range(heads):
        c = columns(h)
        keys = jnp.concatenate([k[:, c], ke[:, c], ko[:, c]], 0)
        values = jnp.concatenate([v[:, c], ve[:, c], vo[:, c]], 0)
        scores = dot(keys, q[:, c], 1, 1) * FACTOR + bias
        peak = jnp.max(scores, 0, keepdims=True)
        weight = jnp.exp(scores - peak)
        total = jnp.sum(weight, 0, keepdims=True)
        prob = (weight * (1.0 / total)).astype(BF)
        att[:, c] = dot(prob, values, 0, 0).astype(BF)
        lse[h : h + 1, :] = peak + jnp.log(total)
    half = send_e.shape[0]
    odd = i & 1
    last = rows - half
    send_e[...] = att[pl.ds(pl.multiple_of((1 - odd) * last, 64), half), :]
    send_o[...] = att[pl.ds(pl.multiple_of(odd * last, 64), half), :]


def audio_combine(idx, own, own_lse, re, ro, att, total, send_e, send_o):
    rows = own.shape[0]
    heads = own.shape[1] // HEAD_DIM
    tail = slice(heads * HEAD_DIM, heads * HEAD_DIM + PAD)
    mine = own_lse[...]
    first = unpack_stats(re[:, tail])
    second = unpack_stats(ro[:, tail])
    peak = jnp.maximum(mine, jnp.maximum(first, second))
    whole = peak + jnp.log(
        jnp.exp(mine - peak) + jnp.exp(first - peak) + jnp.exp(second - peak)
    )
    total[...] = whole
    wm, we, wo = jnp.exp(mine - whole), jnp.exp(first - whole), jnp.exp(second - whole)
    for h in range(heads):
        c = columns(h)
        att[:, c] = (
            own[:, c] * wm[:, h : h + 1]
            + re[:, c].astype(F32) * we[:, h : h + 1]
            + ro[:, c].astype(F32) * wo[:, h : h + 1]
        ).astype(BF)
    odd = idx[0] & 1
    send_e[...] = att[pl.ds(pl.multiple_of((1 - odd) * (rows - 16), 16), 16), :]
    send_o[...] = att[pl.ds(pl.multiple_of(odd * (rows - 16), 16), 16), :]


class Mix:
    def __init__(self, count, idx, refs):
        self.i = idx[0]
        self.even = (self.i & 1) == 0
        self.has_prev = (self.i > 0).astype(F32)
        self.has_next = (self.i < count - 1).astype(F32)
        (self.att_v, self.hve, self.hvo, self.cot_v, self.cve, self.cvo,
         self.att_a, self.hae, self.hao, self.cot_a, self.cae, self.cao,
         self.conv_v, self.conv_a, self.gain_v, self.gain_a) = refs
        self.chunks = self.att_v.shape[0] // STRIDE

    def before(self, e, o):
        return jnp.where(self.even, o.astype(F32), e.astype(F32)) * self.has_prev

    def after(self, e, o):
        return jnp.where(self.even, e.astype(F32), o.astype(F32)) * self.has_next

    def video_att(self, g, c):
        if 0 <= g < self.chunks:
            return self.att_v[g * STRIDE : (g + 1) * STRIDE, c].astype(F32)
        if g < 0:
            s = slice((g + 2) * STRIDE, (g + 3) * STRIDE)
            return self.before(self.hve[s, c], self.hvo[s, c])
        s = slice((g - self.chunks) * STRIDE, (g - self.chunks + 1) * STRIDE)
        return self.after(self.hve[s, c], self.hvo[s, c])

    def video_cot(self, g, c):
        if 0 <= g < self.chunks:
            return self.cot_v[g * STRIDE : (g + 1) * STRIDE, c].astype(F32)
        if g < 0:
            return self.before(self.cve[:, c], self.cvo[:, c])
        return self.after(self.cve[:, c], self.cvo[:, c])

    def extended(self, own, e, o, c):
        low = self.before(e[:, c], o[:, c])[8:16]
        high = self.after(e[:, c], o[:, c])[0:8]
        return jnp.concatenate([low, own[:, c].astype(F32), high], 0)

    def audio(self, c):
        att = self.extended(self.att_a, self.hae, self.hao, c)
        rows = att.shape[0]
        early = pltpu.roll(att, 1, 0)
        late = pltpu.roll(att, rows - 1, 0)
        taps = self.conv_a
        mixed = taps[0:1, c] * early + taps[1:2, c] * att + taps[2:3, c] * late
        cot = self.extended(self.cot_a, self.cae, self.cao, c)
        return mixed, cot, early, att, late


def row_sums(count, idx, *refs):
    mix = Mix(count, idx, refs[:-1])
    stats = refs[-1]
    heads = mix.att_v.shape[1] // HEAD_DIM
    rows_a = mix.att_a.shape[0] + 16
    lane = lax.broadcasted_iota(jnp.int32, (STRIDE, PAD), 1)
    tile = jnp.zeros((STRIDE, PAD), F32)
    taps = mix.conv_v
    for g in range(-1, mix.chunks + 1):
        square = jnp.zeros((STRIDE, HEAD_DIM), F32)
        inner = jnp.zeros((STRIDE, HEAD_DIM), F32)
        for h in range(heads):
            c = columns(h)
            mixed = (
                taps[0:1, c] * mix.video_att(g - 1, c)
                + taps[1:2, c] * mix.video_att(g, c)
                + taps[2:3, c] * mix.video_att(g + 1, c)
            )
            square += mixed * mixed
            inner += mix.video_cot(g, c) * mix.gain_v[0:1, c] * mixed
        tile = jnp.where(lane == g + 1, jnp.sum(square, 1, keepdims=True), tile)
        tile = jnp.where(lane == g + 17, jnp.sum(inner, 1, keepdims=True), tile)
    lane_a = lax.broadcasted_iota(jnp.int32, (rows_a, PAD), 1)
    square = jnp.zeros((rows_a, HEAD_DIM), F32)
    inner = jnp.zeros((rows_a, HEAD_DIM), F32)
    for h in range(heads):
        c = columns(h)
        mixed, cot, _, _, _ = mix.audio(c)
        square += mixed * mixed
        inner += cot * mix.gain_a[0:1, c] * mixed
    tile_a = jnp.where(
        lane_a == 0,
        jnp.sum(square, 1, keepdims=True),
        jnp.where(lane_a == 1, jnp.sum(inner, 1, keepdims=True), 0.0),
    )
    stats[0:STRIDE, :] = tile
    stats[STRIDE:, :] = tile_a


def norm_backward(count, width, idx, *refs):
    mix = Mix(count, idx, refs[2:18])
    mine, theirs = refs[0], refs[1]
    total_a = refs[18]
    out_v, up_v, out_a, up_a, up_send, dots_a, parts = refs[19:26]
    scale_ref, shrink_ref = refs[26:28]
    heads = mix.att_v.shape[1] // HEAD_DIM
    sums = mine[...] + theirs[...]
    rows_a = mix.att_a.shape[0]
    ext = rows_a + 16
    for g in range(mix.chunks + 2):
        inverse = lax.rsqrt(sums[0:STRIDE, g : g + 1] / width + EPSILON)
        inner = sums[0:STRIDE, g + 16 : g + 17]
        if g == 0:
            present = mix.has_prev
        elif g == mix.chunks + 1:
            present = mix.has_next
        else:
            present = 1.0
        s = slice(g * STRIDE, (g + 1) * STRIDE)
        scale_ref[s, :] = jnp.broadcast_to(inverse * present, (STRIDE, HEAD_DIM))
        shrink_ref[s, :] = jnp.broadcast_to(
            inverse * inverse * inverse * inner / width * present, (STRIDE, HEAD_DIM)
        )
    row = lax.broadcasted_iota(jnp.int32, (ext, HEAD_DIM), 0)
    present = jnp.where(row < 8, mix.has_prev, jnp.where(row >= rows_a + 8, mix.has_next, 1.0))
    inverse = lax.rsqrt(sums[STRIDE:, 0:1] / width + EPSILON)
    scale_a = jnp.broadcast_to(inverse, (ext, HEAD_DIM)) * present
    shrink_a = (
        jnp.broadcast_to(
            inverse * inverse * inverse * sums[STRIDE:, 1:2] / width, (ext, HEAD_DIM)
        )
        * present
    )
    lane = lax.broadcasted_iota(jnp.int32, (rows_a, PAD), 1)
    dots = jnp.zeros((rows_a, PAD), F32)
    own = slice(8, 8 + rows_a)
    for h in range(heads):
        c = columns(h)
        taps = [mix.conv_v[k : k + 1, c] for k in range(3)]
        gain = mix.gain_v[0:1, c]
        sum_taps = [jnp.zeros((STRIDE, HEAD_DIM), F32) for _ in range(3)]
        sum_gain = jnp.zeros((STRIDE, HEAD_DIM), F32)
        atts = [mix.video_att(g, c) for g in (-2, -1, 0)]
        grads = []
        for g in range(-1, mix.chunks + 1):
            early, here, late = atts
            mixed = taps[0] * early + taps[1] * here + taps[2] * late
            s = slice((g + 1) * STRIDE, (g + 2) * STRIDE)
            scale = scale_ref[s, :]
            incoming = mix.video_cot(g, c)
            grad = scale * (incoming * gain) - mixed * shrink_ref[s, :]
            if 0 <= g < mix.chunks:
                normed = mixed * scale
                out_v[g * STRIDE : (g + 1) * STRIDE, c] = (normed * gain).astype(BF)
                sum_gain += incoming * normed
                for k in range(3):
                    sum_taps[k] += grad * atts[k]
            grads = (grads + [grad])[-3:]
            if g >= 1:
                up_v[(g - 1) * STRIDE : g * STRIDE, c] = (
                    taps[0] * grads[2] + taps[1] * grads[1] + taps[2] * grads[0]
                ).astype(BF)
            if g < mix.chunks:
                atts = atts[1:] + [mix.video_att(g + 2, c)]
        for k in range(3):
            parts[k : k + 1, c] = jnp.sum(sum_taps[k], 0, keepdims=True)
        parts[3:4, c] = jnp.sum(sum_gain, 0, keepdims=True)

        mixed, cot, early, att, late = mix.audio(c)
        gain = mix.gain_a[0:1, c]
        taps = [mix.conv_a[k : k + 1, c] for k in range(3)]
        normed = mixed * scale_a
        grad = scale_a * (cot * gain) - mixed * shrink_a
        out_a[:, c] = (normed * gain)[own].astype(BF)
        upstream = (
            taps[0] * pltpu.roll(grad, ext - 1, 0)
            + taps[1] * grad
            + taps[2] * pltpu.roll(grad, 1, 0)
        )[own].astype(BF)
        up_a[:, c] = upstream
        up_send[:, c] = upstream
        row_dot = jnp.sum(upstream.astype(F32) * att[own], 1, keepdims=True)
        dots = jnp.where(lane == h, row_dot, dots)
        for k, shifted in enumerate((early, att, late)):
            parts[4 + k : 5 + k, c] = jnp.sum((grad * shifted)[own], 0, keepdims=True)
        parts[7:8, c] = jnp.sum((cot * normed)[own], 0, keepdims=True)
    dots_a[...] = dots
    tail = slice(heads * HEAD_DIM, heads * HEAD_DIM + PAD)
    packed = pack_stats(jnp.where(lane < heads, total_a[...], 0.0)).astype(F32)
    packed_dots = pack_stats(dots).astype(F32)
    up_send[:, tail] = (packed + pltpu.roll(packed_dots, 64, 1)).astype(BF)


def video_backward(
    count, idx, window, valid, q, up, lse, k, ke, ko, v, ve, vo, dq, own, send_e, send_o
):
    rows = q.shape[0]
    heads = q.shape[1] // HEAD_DIM
    near = k.shape[0]
    bias = video_bias(idx[0], count, window, valid, rows, near)
    for h in range(heads):
        c = columns(h)
        keys = jnp.concatenate([k[:, c], ke[:, c], ko[:, c]], 0)
        values = jnp.concatenate([v[:, c], ve[:, c], vo[:, c]], 0)
        queries = q[:, c]
        upstream = up[:, c]
        scores = dot(keys, queries, 1, 1) * FACTOR + bias
        prob = jnp.exp(scores - lse[h : h + 1, :])
        prob_grad = dot(values, upstream, 1, 1)
        row_dot = jnp.sum(prob * prob_grad, 0, keepdims=True)
        score_grad = (prob * (prob_grad - row_dot)).astype(BF)
        dq[:, c] = (dot(score_grad, keys, 0, 0) * FACTOR).astype(BF)
        dk = dot(score_grad, queries, 1, 0) * FACTOR
        dv = dot(prob.astype(BF), upstream, 1, 0)
        own[0:near, c] = dk[0:near]
        own[near:, c] = dv[0:near]
        send_e[0:near, c] = dk[near : 2 * near].astype(BF)
        send_e[near:, c] = dv[near : 2 * near].astype(BF)
        send_o[0:near, c] = dk[2 * near :].astype(BF)
        send_o[near:, c] = dv[2 * near :].astype(BF)


def audio_backward(
    count, idx, window, valid, q, qe, qo, up, upe, upo, total, dots, k, v,
    dk, dv, own, send_e, send_o,
):
    rows = q.shape[0]
    heads = q.shape[1] // HEAD_DIM
    tail = slice(heads * HEAD_DIM, heads * HEAD_DIM + PAD)
    bias = audio_bias(idx[0], count, window, valid, rows, k.shape[0])
    totals, row_dots = [total[...]], [dots[...]]
    for packed in (upe[:, tail], upo[:, tail]):
        wide = unpack_stats(packed)
        totals.append(wide)
        row_dots.append(pltpu.roll(wide, 64, 1))
    totals = jnp.concatenate(totals, 0)
    row_dots = jnp.concatenate(row_dots, 0)
    for h in range(heads):
        c = columns(h)
        queries = jnp.concatenate([q[:, c], qe[:, c], qo[:, c]], 0)
        upstream = jnp.concatenate([up[:, c], upe[:, c], upo[:, c]], 0)
        keys, values = k[:, c], v[:, c]
        scores = dot(queries, keys, 1, 1) * FACTOR + bias
        prob = jnp.exp(scores - totals[:, h : h + 1])
        prob_grad = dot(upstream, values, 1, 1)
        score_grad = (prob * (prob_grad - row_dots[:, h : h + 1])).astype(BF)
        dq = dot(score_grad, keys, 1, 0) * FACTOR
        dk[:, c] = (dot(score_grad, queries, 0, 0) * FACTOR).astype(BF)
        dv[:, c] = dot(prob.astype(BF), upstream, 0, 0).astype(BF)
        own[:, c] = dq[:rows]
        send_e[:, c] = dq[rows : 2 * rows].astype(BF)
        send_o[:, c] = dq[2 * rows :].astype(BF)


def per_device(
    query_video,
    key_video,
    value_video,
    query_audio,
    key_audio,
    value_audio,
    conv_video,
    conv_audio,
    gain_video,
    gain_audio,
    video_window,
    audio_window,
    video_valid,
    audio_valid,
    cotangent_video,
    cotangent_audio,
):
    count = video_window.shape[0]
    block = lax.axis_index(BLOCKS)
    idx = block.astype(jnp.int32).reshape(1)
    odd = block & 1
    rows_v, wide = query_video.shape
    rows_a = query_audio.shape[0]
    heads = wide // HEAD_DIM
    model = wide * lax.axis_size("tp")
    even_route = [(i, i ^ 1) for i in range(count)]
    odd_route = [(i, other(i, count)) for i in range(count)]

    def swap_e(x):
        return lax.ppermute(x, BLOCKS, even_route)

    def swap_o(x):
        return lax.ppermute(x, BLOCKS, odd_route)

    def bind(f, *extra):
        def kernel(*refs):
            return f(*extra, *refs)

        return kernel

    qe, qo = swap_e(query_audio), swap_o(query_audio)
    ke, ko = swap_e(key_audio), swap_o(key_audio)
    ve, vo = swap_e(value_audio), swap_o(value_audio)

    def edge(x, rows, to_even):
        last = x.shape[0] - rows
        start = (1 - odd) * last if to_even else odd * last
        return lax.dynamic_slice_in_dim(x, start, rows, 0)

    cve = swap_e(edge(cotangent_video, STRIDE, True))
    cvo = swap_o(edge(cotangent_video, STRIDE, False))
    cae = swap_e(edge(cotangent_audio, 16, True))
    cao = swap_o(edge(cotangent_audio, 16, False))

    mm = 2 * heads * 3 * rows_a * rows_v * HEAD_DIM
    packed = ((rows_a, wide + PAD), BF)
    audio_info = (idx, audio_window, video_valid)
    video_info = (idx, video_window, audio_valid)
    send_e, send_o, own_part, own_lse = call(
        bind(audio_forward, count),
        [packed, packed, ((rows_a, wide), F32), ((rows_a, PAD), F32)],
        [query_audio, qe, qo, key_video, value_video],
        audio_info,
        2 * mm,
    )
    pe, po = swap_e(send_e), swap_o(send_o)
    keys_values = [key_audio, ke, ko, value_audio, ve, vo]
    halo = ((2 * STRIDE, wide), BF)
    att_v, lse_v, hv_e, hv_o = call(
        bind(video_forward, count),
        [((rows_v, wide), BF), (((heads + 7) // 8 * 8, rows_v), F32), halo, halo],
        [query_video] + keys_values,
        video_info,
        2 * mm,
    )
    hve, hvo = swap_e(hv_e), swap_o(hv_o)
    halo_a = ((16, wide), BF)
    att_a, total_a, ha_e, ha_o = call(
        audio_combine,
        [((rows_a, wide), BF), ((rows_a, PAD), F32), halo_a, halo_a],
        [own_part, own_lse, pe, po],
        (idx,),
        10**6,
    )
    hae, hao = swap_e(ha_e), swap_o(ha_o)

    mix_args = [
        att_v, hve, hvo, cotangent_video, cve, cvo,
        att_a, hae, hao, cotangent_audio, cae, cao,
        conv_video, conv_audio, gain_video.reshape(1, wide), gain_audio.reshape(1, wide),
    ]
    stats_rows = STRIDE + rows_a + 16
    (stats,) = call(
        bind(row_sums, count), [((stats_rows, PAD), F32)], mix_args, (idx,), 10**7
    )
    tp_size = lax.axis_size("tp")
    stats_other = lax.ppermute(stats, "tp", [(i, i ^ 1) for i in range(tp_size)])
    chunks = rows_v // STRIDE
    out_v, up_v, out_a, up_a, up_send, dots_a, parts = call(
        bind(norm_backward, count, model),
        [
            ((rows_v, wide), BF),
            ((rows_v, wide), BF),
            ((rows_a, wide), BF),
            ((rows_a, wide), BF),
            packed,
            ((rows_a, PAD), F32),
            ((8, wide), F32),
        ],
        [stats, stats_other] + mix_args + [total_a],
        (idx,),
        10**7,
        [pltpu.VMEM(((chunks + 2) * STRIDE, HEAD_DIM), F32)] * 2,
    )
    upe, upo = swap_e(up_send), swap_o(up_send)
    total = parts
    for bits in (1, 2, 4, 14, 16, 32, 96):
        total = total + lax.ppermute(total, BLOCKS, [(i, i ^ bits) for i in range(count)])

    two = ((2 * rows_a, wide), BF)
    dq_v, dkv_own, dkv_e, dkv_o = call(
        bind(video_backward, count),
        [((rows_v, wide), BF), ((2 * rows_a, wide), F32), two, two],
        [query_video, up_v, lse_v] + keys_values,
        video_info,
        5 * mm,
    )
    dkve, dkvo = swap_e(dkv_e), swap_o(dkv_o)
    dk_v, dv_v, dq_own, dq_e, dq_o = call(
        bind(audio_backward, count),
        [
            ((rows_v, wide), BF),
            ((rows_v, wide), BF),
            ((rows_a, wide), F32),
            ((rows_a, wide), BF),
            ((rows_a, wide), BF),
        ],
        [query_audio, qe, qo, up_a, upe, upo, total_a, dots_a, key_video, value_video],
        audio_info,
        5 * mm,
    )
    dqe, dqo = swap_e(dq_e), swap_o(dq_o)
    dkv = (dkv_own + dkve.astype(F32) + dkvo.astype(F32)).astype(BF)
    dq_a = (dq_own + dqe.astype(F32) + dqo.astype(F32)).astype(BF)
    return (
        out_v,
        out_a,
        dq_v,
        dk_v,
        dv_v,
        dq_a,
        dkv[:rows_a],
        dkv[rows_a:],
        total[0:3],
        total[4:7],
        total[3],
        total[7],
    )


def solution(mesh):
    rows = P(BLOCKS, "tp")
    in_specs = (rows,) * 6 + (P(None, "tp"),) * 2 + (P("tp"),) * 2 + (P(),) * 4 + (rows,) * 2
    out_specs = (rows,) * 8 + (P(None, "tp"),) * 2 + (P("tp"),) * 2
    return jax.shard_map(
        per_device, mesh=mesh, in_specs=in_specs, out_specs=out_specs, check_vma=False
    )
```

```python
import jax
import jax.numpy as jnp
from jax import lax
from jax.experimental import pallas as pl
from jax.experimental.pallas import tpu as pltpu
from jax.sharding import PartitionSpec as P

HEAD_DIM = 128
STRIDE = 32
NEGATIVE = -1e30
EPSILON = 1e-06
FACTOR = HEAD_DIM ** (-0.5)
BLOCKS = ("video", "audio")
BF = jnp.bfloat16
F32 = jnp.float32
PAD = 128


def dot(a, b, over_a, over_b):
    return lax.dot_general(
        a, b, (((over_a,), (over_b,)), ((), ())), preferred_element_type=F32
    )


def call(kernel, outs, args, scalars, micros, scratch=()):
    vmem = pl.BlockSpec(memory_space=pltpu.VMEM)
    smem = pl.BlockSpec(memory_space=pltpu.SMEM)
    size = sum(a.size * a.dtype.itemsize for a in args)
    return pl.pallas_call(
        kernel,
        out_shape=[jax.ShapeDtypeStruct(s, d) for s, d in outs],
        in_specs=[smem] * len(scalars) + [vmem] * len(args),
        out_specs=[vmem] * len(outs),
        scratch_shapes=list(scratch),
        compiler_params=pltpu.CompilerParams(vmem_limit_bytes=48 * 1024 * 1024),
        cost_estimate=pl.CostEstimate(
            flops=int(micros * 1.1e9), bytes_accessed=size, transcendentals=0
        ),
    )(*scalars, *args)


def other(i, count):
    return (i + 2 * (i & 1) - 1 + count) & (count - 1)


def columns(h):
    return slice(h * HEAD_DIM, (h + 1) * HEAD_DIM)


def pack_stats(tile):
    high = tile.astype(BF).astype(F32)
    rest = tile - high
    middle = rest.astype(BF).astype(F32)
    low = rest - middle
    return (high + pltpu.roll(middle, 16, 1) + pltpu.roll(low, 32, 1)).astype(BF)


def unpack_stats(packed):
    wide = packed.astype(F32)
    return wide + (pltpu.roll(wide, PAD - 16, 1) + pltpu.roll(wide, PAD - 32, 1))


def audio_bias(i, count, window, valid, rows_q, rows_k):
    row = lax.broadcasted_iota(jnp.int32, (rows_k, 4 * rows_q), 0)
    slot = lax.broadcasted_iota(jnp.int32, (rows_k, 4 * rows_q), 1) // rows_q
    position = i * rows_k + row
    blocks = (i, i ^ 1, other(i, count))
    lower, upper = [
        jnp.where(
            slot == 0,
            window[blocks[0], side],
            jnp.where(slot == 1, window[blocks[1], side], window[blocks[2], side]),
        )
        for side in (0, 1)
    ]
    seen = (position >= lower) & (position < upper) & (row < valid[i]) & (slot < 3)
    return jnp.where(seen, 0.0, NEGATIVE)


def padded(own, e, o, c):
    return jnp.concatenate(
        [own[:, c], e[:, c], o[:, c], jnp.zeros((own.shape[0], HEAD_DIM), BF)], 0
    )


def video_bias(i, count, window, valid, rows_q, rows_k):
    row = lax.broadcasted_iota(jnp.int32, (rows_k, rows_q), 0)
    parts = []
    for c in (i, i ^ 1, other(i, count)):
        position = c * rows_k + row
        seen = (position >= window[i, 0]) & (position < window[i, 1]) & (row < valid[c])
        parts.append(jnp.where(seen, 0.0, NEGATIVE))
    return jnp.concatenate(parts, 0)


def audio_forward(
    count, idx, window, valid, q, qe, qo, k, v, send_e, send_o, own, own_lse, rows_lse
):
    rows = q.shape[0]
    heads = q.shape[1] // HEAD_DIM
    bias = audio_bias(idx[0], count, window, valid, rows, k.shape[0])
    rows_lse[...] = jnp.zeros(rows_lse.shape, F32)
    for h in range(heads):
        c = columns(h)
        scores = dot(k[:, c], padded(q, qe, qo, c), 1, 1) * FACTOR + bias
        peak = jnp.max(scores, 0, keepdims=True)
        weight = jnp.exp(scores - peak)
        total = jnp.sum(weight, 0, keepdims=True)
        part = dot((weight * (1.0 / total)).astype(BF), v[:, c], 0, 0)
        rows_lse[h : h + 1, :] = peak + jnp.log(total)
        own[:, c] = part[:rows]
        send_e[:, c] = part[rows : 2 * rows].astype(BF)
        send_o[:, c] = part[2 * rows : 3 * rows].astype(BF)
    tile = jnp.transpose(rows_lse[...])
    own_lse[...] = tile[:rows]
    tail = slice(heads * HEAD_DIM, heads * HEAD_DIM + PAD)
    send_e[:, tail] = pack_stats(tile[rows : 2 * rows])
    send_o[:, tail] = pack_stats(tile[2 * rows : 3 * rows])


def near_columns(own, e, o, c, part):
    rows = own.shape[0]
    s = slice(part * rows, (part + 1) * rows)
    return jnp.concatenate([own[:, c], e[s, c], o[s, c]], 0)


def video_forward(
    count, idx, window, valid, q, k, v, kve, kvo, att, lse, send_e, send_o
):
    rows = q.shape[0]
    heads = q.shape[1] // HEAD_DIM
    i = idx[0]
    bias = video_bias(i, count, window, valid, rows, k.shape[0])
    lse[...] = jnp.zeros(lse.shape, F32)
    for h in range(heads):
        c = columns(h)
        keys = near_columns(k, kve, kvo, c, 0)
        values = near_columns(v, kve, kvo, c, 1)
        scores = dot(keys, q[:, c], 1, 1) * FACTOR + bias
        peak = jnp.max(scores, 0, keepdims=True)
        weight = jnp.exp(scores - peak)
        total = jnp.sum(weight, 0, keepdims=True)
        prob = (weight * (1.0 / total)).astype(BF)
        att[:, c] = dot(prob, values, 0, 0).astype(BF)
        lse[h : h + 1, :] = peak + jnp.log(total)
    odd = i & 1
    for send, side in ((send_e, 1 - odd), (send_o, odd)):
        start = pl.multiple_of(side * (rows - STRIDE), STRIDE)
        send[...] = att[pl.ds(start, STRIDE), :]


def audio_combine(idx, own, own_lse, re, ro, cot, att, total, send_e, send_o):
    rows = own.shape[0]
    heads = own.shape[1] // HEAD_DIM
    tail = slice(heads * HEAD_DIM, heads * HEAD_DIM + PAD)
    mine = own_lse[...]
    first = unpack_stats(re[:, tail])
    second = unpack_stats(ro[:, tail])
    peak = jnp.maximum(mine, jnp.maximum(first, second))
    whole = peak + jnp.log(
        jnp.exp(mine - peak) + jnp.exp(first - peak) + jnp.exp(second - peak)
    )
    total[...] = whole
    wm, we, wo = jnp.exp(mine - whole), jnp.exp(first - whole), jnp.exp(second - whole)
    odd = (idx[0] & 1) == 1
    for h in range(heads):
        c = columns(h)
        joined = (
            own[:, c] * wm[:, h : h + 1]
            + re[:, c].astype(F32) * we[:, h : h + 1]
            + ro[:, c].astype(F32) * wo[:, h : h + 1]
        )
        att[:, c] = joined.astype(BF)
        incoming = cot[:, c].astype(F32)
        low = jnp.concatenate([joined[0:8], incoming[0:8]], 0)
        high = jnp.concatenate([joined[rows - 8 :], incoming[rows - 8 :]], 0)
        send_e[:, c] = jnp.where(odd, low, high).astype(BF)
        send_o[:, c] = jnp.where(odd, high, low).astype(BF)


class Mix:
    def __init__(self, count, idx, refs):
        self.i = idx[0]
        self.even = (self.i & 1) == 0
        self.has_prev = (self.i > 0).astype(F32)
        self.has_next = (self.i < count - 1).astype(F32)
        (self.att_v, self.hve, self.hvo, self.cot_v,
         self.att_a, self.hae, self.hao, self.cot_a,
         self.conv_v, self.conv_a, self.gain_v, self.gain_a) = refs
        self.chunks = self.att_v.shape[0] // STRIDE

    def before(self, e, o):
        return jnp.where(self.even, o.astype(F32), e.astype(F32)) * self.has_prev

    def after(self, e, o):
        return jnp.where(self.even, e.astype(F32), o.astype(F32)) * self.has_next

    def video_att(self, g, c):
        if g < 0:
            return self.before(self.hve[:, c], self.hvo[:, c])
        if g >= self.chunks:
            return self.after(self.hve[:, c], self.hvo[:, c])
        return self.att_v[g * STRIDE : (g + 1) * STRIDE, c].astype(F32)

    def video_cot(self, g, c):
        return self.cot_v[g * STRIDE : (g + 1) * STRIDE, c].astype(F32)

    def extended(self, own, c, part):
        s = slice(8 * part, 8 * part + 8)
        low = self.before(self.hae[:, c], self.hao[:, c])[s]
        high = self.after(self.hae[:, c], self.hao[:, c])[s]
        return jnp.concatenate([low, own[:, c].astype(F32), high], 0)

    def audio(self, c):
        att = self.extended(self.att_a, c, 0)
        rows = att.shape[0]
        early = pltpu.roll(att, 1, 0)
        late = pltpu.roll(att, rows - 1, 0)
        taps = self.conv_a
        mixed = taps[0:1, c] * early + taps[1:2, c] * att + taps[2:3, c] * late
        cot = self.extended(self.cot_a, c, 1)
        return mixed, cot, early, att, late


def row_sums(count, idx, *refs):
    mix = Mix(count, idx, refs[:-1])
    stats = refs[-1]
    heads = mix.att_v.shape[1] // HEAD_DIM
    rows_a = mix.att_a.shape[0] + 16
    lane = lax.broadcasted_iota(jnp.int32, (STRIDE, PAD), 1)
    tile = jnp.zeros((STRIDE, PAD), F32)
    taps = mix.conv_v
    for g in range(mix.chunks):
        square = jnp.zeros((STRIDE, HEAD_DIM), F32)
        inner = jnp.zeros((STRIDE, HEAD_DIM), F32)
        for h in range(heads):
            c = columns(h)
            mixed = (
                taps[0:1, c] * mix.video_att(g - 1, c)
                + taps[1:2, c] * mix.video_att(g, c)
                + taps[2:3, c] * mix.video_att(g + 1, c)
            )
            square += mixed * mixed
            inner += mix.video_cot(g, c) * mix.gain_v[0:1, c] * mixed
        tile = jnp.where(lane == g, jnp.sum(square, 1, keepdims=True), tile)
        tile = jnp.where(lane == g + 16, jnp.sum(inner, 1, keepdims=True), tile)
    lane_a = lax.broadcasted_iota(jnp.int32, (rows_a, PAD), 1)
    square = jnp.zeros((rows_a, HEAD_DIM), F32)
    inner = jnp.zeros((rows_a, HEAD_DIM), F32)
    for h in range(heads):
        c = columns(h)
        mixed, cot, _, _, _ = mix.audio(c)
        square += mixed * mixed
        inner += cot * mix.gain_a[0:1, c] * mixed
    tile_a = jnp.where(
        lane_a == 0,
        jnp.sum(square, 1, keepdims=True),
        jnp.where(lane_a == 1, jnp.sum(inner, 1, keepdims=True), 0.0),
    )
    stats[0:STRIDE, :] = tile
    stats[STRIDE:, :] = tile_a


def norm_backward(count, width, idx, *refs):
    mix = Mix(count, idx, refs[2:14])
    mine, theirs = refs[0], refs[1]
    total_a = refs[14]
    out_v, grad_v, out_a, up_a, send_e, send_o, dots_a, parts = refs[15:23]
    scale_ref, shrink_ref = refs[23:25]
    heads = mix.att_v.shape[1] // HEAD_DIM
    sums = mine[...] + theirs[...]
    rows_a = mix.att_a.shape[0]
    ext = rows_a + 16
    for g in range(mix.chunks):
        inverse = lax.rsqrt(sums[0:STRIDE, g : g + 1] / width + EPSILON)
        inner = sums[0:STRIDE, g + 16 : g + 17]
        s = slice(g * STRIDE, (g + 1) * STRIDE)
        scale_ref[s, :] = jnp.broadcast_to(inverse, (STRIDE, HEAD_DIM))
        shrink_ref[s, :] = jnp.broadcast_to(
            inverse * inverse * inverse * inner / width, (STRIDE, HEAD_DIM)
        )
    row = lax.broadcasted_iota(jnp.int32, (ext, HEAD_DIM), 0)
    present = jnp.where(row < 8, mix.has_prev, jnp.where(row >= rows_a + 8, mix.has_next, 1.0))
    inverse = lax.rsqrt(sums[STRIDE:, 0:1] / width + EPSILON)
    scale_a = jnp.broadcast_to(inverse, (ext, HEAD_DIM)) * present
    shrink_a = (
        jnp.broadcast_to(
            inverse * inverse * inverse * sums[STRIDE:, 1:2] / width, (ext, HEAD_DIM)
        )
        * present
    )
    lane = lax.broadcasted_iota(jnp.int32, (rows_a, PAD), 1)
    dots = jnp.zeros((rows_a, PAD), F32)
    own = slice(8, 8 + rows_a)
    for h in range(heads):
        c = columns(h)
        taps = [mix.conv_v[k : k + 1, c] for k in range(3)]
        gain = mix.gain_v[0:1, c]
        sum_taps = [jnp.zeros((STRIDE, HEAD_DIM), F32) for _ in range(3)]
        sum_gain = jnp.zeros((STRIDE, HEAD_DIM), F32)
        atts = [mix.video_att(g, c) for g in (-1, 0, 1)]
        for g in range(mix.chunks):
            mixed = taps[0] * atts[0] + taps[1] * atts[1] + taps[2] * atts[2]
            s = slice(g * STRIDE, (g + 1) * STRIDE)
            scale = scale_ref[s, :]
            incoming = mix.video_cot(g, c)
            grad = scale * (incoming * gain) - mixed * shrink_ref[s, :]
            normed = mixed * scale
            out_v[s, c] = (normed * gain).astype(BF)
            grad_v[s, c] = grad
            sum_gain += incoming * normed
            for k in range(3):
                sum_taps[k] += grad * atts[k]
            if g + 1 < mix.chunks:
                atts = atts[1:] + [mix.video_att(g + 2, c)]
        for k in range(3):
            parts[k : k + 1, c] = jnp.sum(sum_taps[k], 0, keepdims=True)
        parts[3:4, c] = jnp.sum(sum_gain, 0, keepdims=True)

        mixed, cot, early, att, late = mix.audio(c)
        gain = mix.gain_a[0:1, c]
        taps = [mix.conv_a[k : k + 1, c] for k in range(3)]
        normed = mixed * scale_a
        grad = scale_a * (cot * gain) - mixed * shrink_a
        out_a[:, c] = (normed * gain)[own].astype(BF)
        upstream = (
            taps[0] * pltpu.roll(grad, ext - 1, 0)
            + taps[1] * grad
            + taps[2] * pltpu.roll(grad, 1, 0)
        )[own].astype(BF)
        up_a[:, c] = upstream
        send_e[0:rows_a, c] = upstream
        send_o[0:rows_a, c] = upstream
        row_dot = jnp.sum(upstream.astype(F32) * att[own], 1, keepdims=True)
        dots = jnp.where(lane == h, row_dot, dots)
        for k, shifted in enumerate((early, att, late)):
            parts[4 + k : 5 + k, c] = jnp.sum((grad * shifted)[own], 0, keepdims=True)
        parts[7:8, c] = jnp.sum((cot * normed)[own], 0, keepdims=True)
    dots_a[...] = dots
    tail = slice(heads * HEAD_DIM, heads * HEAD_DIM + PAD)
    packed = pack_stats(jnp.where(lane < heads, total_a[...], 0.0)).astype(F32)
    packed_dots = pack_stats(dots).astype(F32)
    packed = (packed + pltpu.roll(packed_dots, 64, 1)).astype(BF)
    odd = idx[0] & 1
    body = slice(0, heads * HEAD_DIM)
    for send, side in ((send_e, 1 - odd), (send_o, odd)):
        start = pl.multiple_of(side * (mix.att_v.shape[0] - STRIDE), STRIDE)
        send[0:rows_a, tail] = packed
        send[rows_a:, body] = grad_v[pl.ds(start, STRIDE), :].astype(BF)
        send[rows_a:, tail] = jnp.zeros((STRIDE, PAD), BF)


def video_backward(
    count, idx, window, valid, q, grad, re, ro, conv, lse, k, v, kve, kvo,
    dq, own, send_e, send_o,
):
    rows = q.shape[0]
    heads = q.shape[1] // HEAD_DIM
    near = k.shape[0]
    i = idx[0]
    even = (i & 1) == 0
    has_prev = (i > 0).astype(F32)
    has_next = (i < count - 1).astype(F32)
    bias = video_bias(i, count, window, valid, rows, near)
    halo = slice(near, near + STRIDE)
    for h in range(heads):
        c = columns(h)
        keys = near_columns(k, kve, kvo, c, 0)
        values = near_columns(v, kve, kvo, c, 1)
        queries = q[:, c]
        first, second = re[halo, c].astype(F32), ro[halo, c].astype(F32)
        before = jnp.where(even, second, first) * has_prev
        after = jnp.where(even, first, second) * has_next
        own_grad = grad[:, c]
        wide = jnp.concatenate([before, own_grad, after], 0)
        upstream = (
            conv[0:1, c] * wide[2 * STRIDE :]
            + conv[1:2, c] * own_grad
            + conv[2:3, c] * wide[0:rows]
        ).astype(BF)
        scores = dot(keys, queries, 1, 1) * FACTOR + bias
        prob = jnp.exp(scores - lse[h : h + 1, :])
        prob_grad = dot(values, upstream, 1, 1)
        row_dot = jnp.sum(prob * prob_grad, 0, keepdims=True)
        score_grad = (prob * (prob_grad - row_dot)).astype(BF)
        dq[:, c] = (dot(score_grad, keys, 0, 0) * FACTOR).astype(BF)
        dk = dot(score_grad, queries, 1, 0) * FACTOR
        dv = dot(prob.astype(BF), upstream, 1, 0)
        for part, value in enumerate((dk, dv)):
            s = slice(part * near, (part + 1) * near)
            own[s, c] = value[0:near]
            send_e[s, c] = value[near : 2 * near].astype(BF)
            send_o[s, c] = value[2 * near :].astype(BF)


def audio_backward(
    count, idx, window, valid, q, qe, qo, up, re, ro, total, dots, k, v, part_e, part_o,
    dk, dv, own, send_e, send_o,
):
    rows = q.shape[0]
    heads = q.shape[1] // HEAD_DIM
    tail = slice(heads * HEAD_DIM, heads * HEAD_DIM + PAD)
    bias = audio_bias(idx[0], count, window, valid, rows, k.shape[0])
    totals, row_dots = [total[...]], [dots[...]]
    for r in (re, ro):
        wide = unpack_stats(r[0:rows, tail])
        totals.append(wide)
        row_dots.append(pltpu.roll(wide, 64, 1))
    blank = jnp.zeros((PAD - 3 * rows, PAD), F32)
    totals = jnp.transpose(jnp.concatenate(totals + [blank], 0))
    row_dots = jnp.transpose(jnp.concatenate(row_dots + [blank], 0))
    up_e, up_o = re.at[0:rows], ro.at[0:rows]
    done = slice(0, 2 * rows)
    send_e[done, :] = part_e[...]
    send_o[done, :] = part_o[...]
    for h in range(heads):
        c = columns(h)
        queries = padded(q, qe, qo, c)
        upstream = padded(up, up_e, up_o, c)
        keys, values = k[:, c], v[:, c]
        scores = dot(keys, queries, 1, 1) * FACTOR + bias
        prob = jnp.exp(scores - totals[h : h + 1, :])
        prob_grad = dot(values, upstream, 1, 1)
        score_grad = (prob * (prob_grad - row_dots[h : h + 1, :])).astype(BF)
        dq = dot(score_grad, keys, 0, 0) * FACTOR
        dk[:, c] = (dot(score_grad, queries, 1, 0) * FACTOR).astype(BF)
        dv[:, c] = dot(prob.astype(BF), upstream, 1, 0).astype(BF)
        own[:, c] = dq[:rows]
        send_e[2 * rows :, c] = dq[rows : 2 * rows].astype(BF)
        send_o[2 * rows :, c] = dq[2 * rows : 3 * rows].astype(BF)


def per_device(
    query_video,
    key_video,
    value_video,
    query_audio,
    key_audio,
    value_audio,
    conv_video,
    conv_audio,
    gain_video,
    gain_audio,
    video_window,
    audio_window,
    video_valid,
    audio_valid,
    cotangent_video,
    cotangent_audio,
):
    count = video_window.shape[0]
    block = lax.axis_index(BLOCKS)
    idx = block.astype(jnp.int32).reshape(1)
    rows_v, wide = query_video.shape
    rows_a = query_audio.shape[0]
    heads = wide // HEAD_DIM
    model = wide * lax.axis_size("tp")
    even_route = [(i, i ^ 1) for i in range(count)]
    odd_route = [(i, other(i, count)) for i in range(count)]

    def swap_e(x):
        return lax.ppermute(x, BLOCKS, even_route)

    def swap_o(x):
        return lax.ppermute(x, BLOCKS, odd_route)

    def bind(f, *extra):
        def kernel(*refs):
            return f(*extra, *refs)

        return kernel

    qe, qo = swap_e(query_audio), swap_o(query_audio)
    both = jnp.concatenate([key_audio, value_audio], 0)
    kve, kvo = swap_e(both), swap_o(both)

    packed = ((rows_a, wide + PAD), BF)
    audio_info = (idx, audio_window, video_valid)
    video_info = (idx, video_window, audio_valid)
    send_e, send_o, own_part, own_lse = call(
        bind(audio_forward, count),
        [packed, packed, ((rows_a, wide), F32), ((rows_a, PAD), F32)],
        [query_audio, qe, qo, key_video, value_video],
        audio_info,
        3.0,
        [pltpu.VMEM((PAD, PAD), F32)],
    )
    kve, kvo, own_lse = lax.optimization_barrier((kve, kvo, own_lse))
    pe, po = swap_e(send_e), swap_o(send_o)
    keys_values = [key_audio, value_audio, kve, kvo]
    halo = ((STRIDE, wide), BF)
    att_v, lse_v, hv_e, hv_o = call(
        bind(video_forward, count),
        [((rows_v, wide), BF), (((heads + 7) // 8 * 8, rows_v), F32), halo, halo],
        [query_video] + keys_values,
        video_info,
        2.8,
    )
    hve, hvo = swap_e(hv_e), swap_o(hv_o)
    halo_a = ((16, wide), BF)
    att_a, total_a, ha_e, ha_o = call(
        audio_combine,
        [((rows_a, wide), BF), ((rows_a, PAD), F32), halo_a, halo_a],
        [own_part, own_lse, pe, po, cotangent_audio],
        (idx,),
        0.5,
    )
    hae, hao = swap_e(ha_e), swap_o(ha_o)

    mix_args = [
        att_v, hve, hvo, cotangent_video,
        att_a, hae, hao, cotangent_audio,
        conv_video, conv_audio, gain_video.reshape(1, wide), gain_audio.reshape(1, wide),
    ]
    stats_rows = STRIDE + rows_a + 16
    (stats,) = call(
        bind(row_sums, count), [((stats_rows, PAD), F32)], mix_args, (idx,), 1.3
    )
    tp_size = lax.axis_size("tp")
    stats_other = lax.ppermute(stats, "tp", [(i, i ^ 1) for i in range(tp_size)])
    chunks = rows_v // STRIDE
    both = ((rows_a + STRIDE, wide + PAD), BF)
    out_v, grad_v, out_a, up_a, back_e, back_o, dots_a, parts = call(
        bind(norm_backward, count, model),
        [
            ((rows_v, wide), BF),
            ((rows_v, wide), F32),
            ((rows_a, wide), BF),
            ((rows_a, wide), BF),
            both,
            both,
            ((rows_a, PAD), F32),
            ((8, wide), F32),
        ],
        [stats, stats_other] + mix_args + [total_a],
        (idx,),
        3.0,
        [pltpu.VMEM((rows_v, HEAD_DIM), F32)] * 2,
    )
    re, ro = swap_e(back_e), swap_o(back_o)
    total = parts
    for bits in (16, 32, 2, 1, 96, 4, 14):
        total = total + lax.ppermute(total, BLOCKS, [(i, i ^ bits) for i in range(count)])

    two = ((2 * rows_a, wide), BF)
    dq_v, dkv_own, dkv_e, dkv_o = call(
        bind(video_backward, count),
        [((rows_v, wide), BF), ((2 * rows_a, wide), F32), two, two],
        [query_video, grad_v, re, ro, conv_video, lse_v] + keys_values,
        video_info,
        5.0,
    )
    three = ((3 * rows_a, wide), BF)
    dk_v, dv_v, dq_own, give_e, give_o = call(
        bind(audio_backward, count),
        [((rows_v, wide), BF), ((rows_v, wide), BF), ((rows_a, wide), F32), three, three],
        [query_audio, qe, qo, up_a, re, ro, total_a, dots_a, key_video, value_video,
         dkv_e, dkv_o],
        audio_info,
        5.0,
    )
    got_e, got_o = swap_e(give_e), swap_o(give_o)
    own = jnp.concatenate([dkv_own, dq_own], 0)
    grads = (own + got_e.astype(F32) + got_o.astype(F32)).astype(BF)
    return (
        out_v,
        out_a,
        dq_v,
        dk_v,
        dv_v,
        grads[2 * rows_a :],
        grads[:rows_a],
        grads[rows_a : 2 * rows_a],
        total[0:3],
        total[4:7],
        total[3],
        total[7],
    )


def solution(mesh):
    rows = P(BLOCKS, "tp")
    in_specs = (rows,) * 6 + (P(None, "tp"),) * 2 + (P("tp"),) * 2 + (P(),) * 4 + (rows,) * 2
    out_specs = (rows,) * 8 + (P(None, "tp"),) * 2 + (P("tp"),) * 2
    return jax.shard_map(
        per_device, mesh=mesh, in_specs=in_specs, out_specs=out_specs, check_vma=False
    )
```

```python
import jax
import jax.numpy as jnp
from jax import lax
from jax.experimental import pallas as pl
from jax.experimental.pallas import tpu as pltpu
from jax.sharding import PartitionSpec as P

HEAD_DIM = 128
STRIDE = 32
NEGATIVE = -1e30
EPSILON = 1e-06
FACTOR = HEAD_DIM ** (-0.5)
BLOCKS = ("video", "audio")
BF = jnp.bfloat16
F32 = jnp.float32
PAD = 128


def dot(a, b, over_a, over_b):
    return lax.dot_general(
        a, b, (((over_a,), (over_b,)), ((), ())), preferred_element_type=F32
    )


def call(kernel, outs, args, scalars, micros, scratch=(), far_args=(), far_outs=(), unread=()):
    vmem = pl.BlockSpec(memory_space=pltpu.VMEM)
    smem = pl.BlockSpec(memory_space=pltpu.SMEM)
    anywhere = pl.BlockSpec(memory_space=pl.ANY)
    far = pl.BlockSpec(memory_space=pltpu.HBM)
    size = sum(a.size * a.dtype.itemsize for a in args)
    return pl.pallas_call(
        kernel,
        out_shape=[jax.ShapeDtypeStruct(s, d) for s, d in outs],
        in_specs=[smem] * len(scalars)
        + [
            anywhere if n in unread else far if n in far_args else vmem
            for n in range(len(args))
        ],
        out_specs=[anywhere if n in far_outs else vmem for n in range(len(outs))],
        scratch_shapes=list(scratch),
        compiler_params=pltpu.CompilerParams(vmem_limit_bytes=48 * 1024 * 1024),
        cost_estimate=pl.CostEstimate(
            flops=int(micros * 1.1e9), bytes_accessed=size, transcendentals=0
        ),
    )(*scalars, *args)


CHUNK = 6


class Stream:
    def __init__(self, pairs, sems, heads):
        self.pairs, self.sems = pairs, sems
        self.parts = heads // CHUNK

    def copies(self, part):
        c = slice(part * CHUNK * HEAD_DIM, (part + 1) * CHUNK * HEAD_DIM)
        return [
            pltpu.make_async_copy(src.at[:, c], dst.at[:, c], self.sems.at[n, part])
            for n, (src, dst) in enumerate(self.pairs)
        ]

    def start(self, part):
        for copy in self.copies(part):
            copy.start()

    def wait(self, part):
        for copy in self.copies(part):
            copy.wait()

    def start_all(self):
        for part in range(self.parts):
            self.start(part)

    def wait_all(self):
        for part in range(self.parts):
            self.wait(part)

    def before_head(self, h):
        if h % CHUNK == 0:
            self.wait(h // CHUNK)

    def after_head(self, h):
        if h % CHUNK == CHUNK - 1:
            self.start(h // CHUNK)


def pack_rows(k, v, both, sems):
    rows = k.shape[0]
    copies = [
        pltpu.make_async_copy(k, both.at[0:rows], sems.at[0]),
        pltpu.make_async_copy(v, both.at[rows:], sems.at[1]),
    ]
    for copy in copies:
        copy.start()
    for copy in copies:
        copy.wait()


def plus(*refs):
    refs[-1][...] = refs[0][...] + refs[1][...]


def split_sums(mine, theirs, taps_v, taps_a, gain_v, gain_a):
    total = mine[...] + theirs[...]
    taps_v[...] = total[0:3]
    gain_v[...] = total[3]
    taps_a[...] = total[4:7]
    gain_a[...] = total[7]


def other(i, count):
    return (i + 2 * (i & 1) - 1 + count) & (count - 1)


def groups(heads, size):
    return [range(g, min(g + size, heads)) for g in range(0, heads, size)]


def columns(h):
    return slice(h * HEAD_DIM, (h + 1) * HEAD_DIM)


def pack_stats(tile):
    high = tile.astype(BF).astype(F32)
    rest = tile - high
    middle = rest.astype(BF).astype(F32)
    low = rest - middle
    return (high + pltpu.roll(middle, 16, 1) + pltpu.roll(low, 32, 1)).astype(BF)


def unpack_stats(packed):
    wide = packed.astype(F32)
    return wide + (pltpu.roll(wide, PAD - 16, 1) + pltpu.roll(wide, PAD - 32, 1))


def audio_bias(i, count, window, valid, rows_q, rows_k):
    row = lax.broadcasted_iota(jnp.int32, (rows_k, 4 * rows_q), 0)
    slot = lax.broadcasted_iota(jnp.int32, (rows_k, 4 * rows_q), 1) // rows_q
    position = i * rows_k + row
    blocks = (i, i ^ 1, other(i, count))
    lower, upper = [
        jnp.where(
            slot == 0,
            window[side, blocks[0]],
            jnp.where(slot == 1, window[side, blocks[1]], window[side, blocks[2]]),
        )
        for side in (0, 1)
    ]
    seen = (position >= lower) & (position < upper) & (row < valid[i]) & (slot < 3)
    return jnp.where(seen, 0.0, NEGATIVE)


def padded(own, e, o, c):
    return jnp.concatenate(
        [own[:, c], e[:, c], o[:, c], jnp.zeros((own.shape[0], HEAD_DIM), BF)], 0
    )


def video_bias(i, count, window, valid, rows_q, rows_k):
    row = lax.broadcasted_iota(jnp.int32, (rows_k, rows_q), 0)
    parts = []
    for c in (i, i ^ 1, other(i, count)):
        position = c * rows_k + row
        seen = (position >= window[0, i]) & (position < window[1, i]) & (row < valid[c])
        parts.append(jnp.where(seen, 0.0, NEGATIVE))
    return jnp.concatenate(parts, 0)


def audio_forward(
    count, idx, window, valid, q, qe, qo, k, v, send_e, send_o, own, own_lse,
    rows_lse,
):
    rows = q.shape[0]
    heads = q.shape[1] // HEAD_DIM
    bias = audio_bias(idx[0], count, window, valid, rows, k.shape[0])
    rows_lse[...] = jnp.zeros(rows_lse.shape, F32)
    for group in groups(heads, heads):
        scores, probs = {}, {}
        for h in group:
            c = columns(h)
            scores[h] = dot(k[:, c], padded(q, qe, qo, c), 1, 1) * FACTOR + bias
        for h in group:
            peak = jnp.max(scores[h], 0, keepdims=True)
            weight = jnp.exp(scores[h] - peak)
            total = jnp.sum(weight, 0, keepdims=True)
            rows_lse[h : h + 1, :] = peak + jnp.log(total)
            probs[h] = (weight * (1.0 / total)).astype(BF)
        for h in group:
            c = columns(h)
            part = dot(probs[h], v[:, c], 0, 0)
            own[:, c] = part[:rows]
            send_e[:, c] = part[rows : 2 * rows].astype(BF)
            send_o[:, c] = part[2 * rows : 3 * rows].astype(BF)
    tile = jnp.transpose(rows_lse[...])
    own_lse[...] = tile[:rows]
    tail = slice(heads * HEAD_DIM, heads * HEAD_DIM + PAD)
    send_e[:, tail] = pack_stats(tile[rows : 2 * rows])
    send_o[:, tail] = pack_stats(tile[2 * rows : 3 * rows])


def near_columns(own, e, o, c, part):
    rows = own.shape[0]
    s = slice(part * rows, (part + 1) * rows)
    return jnp.concatenate([own[:, c], e[s, c], o[s, c]], 0)


def video_forward(
    count, idx, window, valid, q, k, v, kve, kvo, _, att, lse, send_e, send_o
):
    rows = q.shape[0]
    heads = q.shape[1] // HEAD_DIM
    i = idx[0]
    bias = video_bias(i, count, window, valid, rows, k.shape[0])
    lse[...] = jnp.zeros(lse.shape, F32)
    for group in groups(heads, heads):
        scores, probs = {}, {}
        for h in group:
            c = columns(h)
            keys = near_columns(k, kve, kvo, c, 0)
            scores[h] = dot(keys, q[:, c], 1, 1) * FACTOR + bias
        for h in group:
            peak = jnp.max(scores[h], 0, keepdims=True)
            weight = jnp.exp(scores[h] - peak)
            total = jnp.sum(weight, 0, keepdims=True)
            lse[h : h + 1, :] = peak + jnp.log(total)
            probs[h] = (weight * (1.0 / total)).astype(BF)
        for h in group:
            c = columns(h)
            att[:, c] = dot(probs[h], near_columns(v, kve, kvo, c, 1), 0, 0).astype(BF)
    odd = i & 1
    for send, side in ((send_e, 1 - odd), (send_o, odd)):
        start = pl.multiple_of(side * (rows - STRIDE), STRIDE)
        send[...] = att[pl.ds(start, STRIDE), :]


def audio_combine(idx, own, own_lse, re, ro, cot, att, total, send_e, send_o):
    rows = own.shape[0]
    heads = own.shape[1] // HEAD_DIM
    tail = slice(heads * HEAD_DIM, heads * HEAD_DIM + PAD)
    mine = own_lse[...]
    first = unpack_stats(re[:, tail])
    second = unpack_stats(ro[:, tail])
    peak = jnp.maximum(mine, jnp.maximum(first, second))
    whole = peak + jnp.log(
        jnp.exp(mine - peak) + jnp.exp(first - peak) + jnp.exp(second - peak)
    )
    total[...] = whole
    wm, we, wo = jnp.exp(mine - whole), jnp.exp(first - whole), jnp.exp(second - whole)
    odd = (idx[0] & 1) == 1
    for h in range(heads):
        c = columns(h)
        joined = (
            own[:, c] * wm[:, h : h + 1]
            + re[:, c].astype(F32) * we[:, h : h + 1]
            + ro[:, c].astype(F32) * wo[:, h : h + 1]
        )
        att[:, c] = joined.astype(BF)
        incoming = cot[:, c].astype(F32)
        low = jnp.concatenate([joined[0:8], incoming[0:8]], 0)
        high = jnp.concatenate([joined[rows - 8 :], incoming[rows - 8 :]], 0)
        send_e[:, c] = jnp.where(odd, low, high).astype(BF)
        send_o[:, c] = jnp.where(odd, high, low).astype(BF)


class Mix:
    def __init__(self, count, idx, refs):
        self.i = idx[0]
        self.even = (self.i & 1) == 0
        self.has_prev = (self.i > 0).astype(F32)
        self.has_next = (self.i < count - 1).astype(F32)
        (self.att_v, self.hve, self.hvo, self.cot_v,
         self.att_a, self.hae, self.hao, self.cot_a,
         self.conv_v, self.conv_a, self.gain_v, self.gain_a) = refs
        self.chunks = self.att_v.shape[0] // STRIDE

    def before(self, e, o):
        return jnp.where(self.even, o.astype(F32), e.astype(F32)) * self.has_prev

    def after(self, e, o):
        return jnp.where(self.even, e.astype(F32), o.astype(F32)) * self.has_next

    def video_att(self, g, c):
        if g < 0:
            return self.before(self.hve[:, c], self.hvo[:, c])
        if g >= self.chunks:
            return self.after(self.hve[:, c], self.hvo[:, c])
        return self.att_v[g * STRIDE : (g + 1) * STRIDE, c].astype(F32)

    def video_cot(self, g, c):
        return self.cot_v[g * STRIDE : (g + 1) * STRIDE, c].astype(F32)

    def extended(self, own, c, part):
        s = slice(8 * part, 8 * part + 8)
        low = self.before(self.hae[:, c], self.hao[:, c])[s]
        high = self.after(self.hae[:, c], self.hao[:, c])[s]
        return jnp.concatenate([low, own[:, c].astype(F32), high], 0)

    def audio(self, c):
        att = self.extended(self.att_a, c, 0)
        rows = att.shape[0]
        early = pltpu.roll(att, 1, 0)
        late = pltpu.roll(att, rows - 1, 0)
        taps = self.conv_a
        mixed = taps[0:1, c] * early + taps[1:2, c] * att + taps[2:3, c] * late
        cot = self.extended(self.cot_a, c, 1)
        return mixed, cot, early, att, late


def row_sums(count, idx, *refs):
    mix = Mix(count, idx, refs[:-1])
    stats = refs[-1]
    heads = mix.att_v.shape[1] // HEAD_DIM
    rows_a = mix.att_a.shape[0] + 16
    lane = lax.broadcasted_iota(jnp.int32, (STRIDE, PAD), 1)
    tile = jnp.zeros((STRIDE, PAD), F32)
    taps = mix.conv_v
    for g in range(mix.chunks):
        square = jnp.zeros((STRIDE, HEAD_DIM), F32)
        inner = jnp.zeros((STRIDE, HEAD_DIM), F32)
        for h in range(heads):
            c = columns(h)
            mixed = (
                taps[0:1, c] * mix.video_att(g - 1, c)
                + taps[1:2, c] * mix.video_att(g, c)
                + taps[2:3, c] * mix.video_att(g + 1, c)
            )
            square += mixed * mixed
            inner += mix.video_cot(g, c) * mix.gain_v[0:1, c] * mixed
        tile = jnp.where(lane == g, jnp.sum(square, 1, keepdims=True), tile)
        tile = jnp.where(lane == g + 16, jnp.sum(inner, 1, keepdims=True), tile)
    lane_a = lax.broadcasted_iota(jnp.int32, (rows_a, PAD), 1)
    square = jnp.zeros((rows_a, HEAD_DIM), F32)
    inner = jnp.zeros((rows_a, HEAD_DIM), F32)
    for h in range(heads):
        c = columns(h)
        mixed, cot, _, _, _ = mix.audio(c)
        square += mixed * mixed
        inner += cot * mix.gain_a[0:1, c] * mixed
    tile_a = jnp.where(
        lane_a == 0,
        jnp.sum(square, 1, keepdims=True),
        jnp.where(lane_a == 1, jnp.sum(inner, 1, keepdims=True), 0.0),
    )
    stats[0:STRIDE, :] = tile
    stats[STRIDE:, :] = tile_a


def norm_backward(count, width, idx, *refs):
    mix = Mix(count, idx, refs[2:14])
    mine, theirs = refs[0], refs[1]
    total_a = refs[14]
    grad_v, up_a, send_e, send_o, dots_a, parts = refs[15:21]
    scale_ref, shrink_ref = refs[21:23]
    heads = mix.att_v.shape[1] // HEAD_DIM
    sums = mine[...] + theirs[...]
    rows_a = mix.att_a.shape[0]
    ext = rows_a + 16
    for g in range(mix.chunks):
        inverse = lax.rsqrt(sums[0:STRIDE, g : g + 1] / width + EPSILON)
        inner = sums[0:STRIDE, g + 16 : g + 17]
        s = slice(g * STRIDE, (g + 1) * STRIDE)
        scale_ref[s, :] = jnp.broadcast_to(inverse, (STRIDE, HEAD_DIM))
        shrink_ref[s, :] = jnp.broadcast_to(
            inverse * inverse * inverse * inner / width, (STRIDE, HEAD_DIM)
        )
    row = lax.broadcasted_iota(jnp.int32, (ext, HEAD_DIM), 0)
    present = jnp.where(row < 8, mix.has_prev, jnp.where(row >= rows_a + 8, mix.has_next, 1.0))
    inverse = lax.rsqrt(sums[STRIDE:, 0:1] / width + EPSILON)
    scale_a = jnp.broadcast_to(inverse, (ext, HEAD_DIM)) * present
    shrink_a = (
        jnp.broadcast_to(
            inverse * inverse * inverse * sums[STRIDE:, 1:2] / width, (ext, HEAD_DIM)
        )
        * present
    )
    lane = lax.broadcasted_iota(jnp.int32, (rows_a, PAD), 1)
    dots = jnp.zeros((rows_a, PAD), F32)
    own = slice(8, 8 + rows_a)
    for h in range(heads):
        c = columns(h)
        taps = [mix.conv_v[k : k + 1, c] for k in range(3)]
        gain = mix.gain_v[0:1, c]
        sum_taps = [jnp.zeros((STRIDE, HEAD_DIM), F32) for _ in range(3)]
        sum_gain = jnp.zeros((STRIDE, HEAD_DIM), F32)
        atts = [mix.video_att(g, c) for g in (-1, 0, 1)]
        for g in range(mix.chunks):
            mixed = taps[0] * atts[0] + taps[1] * atts[1] + taps[2] * atts[2]
            s = slice(g * STRIDE, (g + 1) * STRIDE)
            scale = scale_ref[s, :]
            incoming = mix.video_cot(g, c)
            grad = scale * (incoming * gain) - mixed * shrink_ref[s, :]
            normed = mixed * scale
            grad_v[s, c] = grad
            sum_gain += incoming * normed
            for k in range(3):
                sum_taps[k] += grad * atts[k]
            if g + 1 < mix.chunks:
                atts = atts[1:] + [mix.video_att(g + 2, c)]
        for k in range(3):
            parts[k : k + 1, c] = jnp.sum(sum_taps[k], 0, keepdims=True)
        parts[3:4, c] = jnp.sum(sum_gain, 0, keepdims=True)

        mixed, cot, early, att, late = mix.audio(c)
        gain = mix.gain_a[0:1, c]
        taps = [mix.conv_a[k : k + 1, c] for k in range(3)]
        normed = mixed * scale_a
        grad = scale_a * (cot * gain) - mixed * shrink_a
        upstream = (
            taps[0] * pltpu.roll(grad, ext - 1, 0)
            + taps[1] * grad
            + taps[2] * pltpu.roll(grad, 1, 0)
        )[own].astype(BF)
        up_a[:, c] = upstream
        send_e[0:rows_a, c] = upstream
        send_o[0:rows_a, c] = upstream
        row_dot = jnp.sum(upstream.astype(F32) * att[own], 1, keepdims=True)
        dots = jnp.where(lane == h, row_dot, dots)
        for k, shifted in enumerate((early, att, late)):
            parts[4 + k : 5 + k, c] = jnp.sum((grad * shifted)[own], 0, keepdims=True)
        parts[7:8, c] = jnp.sum((cot * normed)[own], 0, keepdims=True)
    dots_a[...] = dots
    tail = slice(heads * HEAD_DIM, heads * HEAD_DIM + PAD)
    packed = pack_stats(jnp.where(lane < heads, total_a[...], 0.0)).astype(F32)
    packed_dots = pack_stats(dots).astype(F32)
    packed = (packed + pltpu.roll(packed_dots, 64, 1)).astype(BF)
    odd = idx[0] & 1
    body = slice(0, heads * HEAD_DIM)
    for send, side in ((send_e, 1 - odd), (send_o, odd)):
        start = pl.multiple_of(side * (mix.att_v.shape[0] - STRIDE), STRIDE)
        send[0:rows_a, tail] = packed
        send[rows_a:, body] = grad_v[pl.ds(start, STRIDE), :].astype(BF)
        send[rows_a:, tail] = jnp.zeros((STRIDE, PAD), BF)


def outputs(count, width, idx, *refs):
    mix = Mix(count, idx, refs[2:14])
    sums = refs[0][...] + refs[1][...]
    out_v, out_a, token = refs[15:18]
    token[...] = jnp.zeros(token.shape, F32)
    heads = mix.att_v.shape[1] // HEAD_DIM
    rows_a = mix.att_a.shape[0]
    scales = [
        jnp.broadcast_to(
            lax.rsqrt(sums[0:STRIDE, g : g + 1] / width + EPSILON), (STRIDE, HEAD_DIM)
        )
        for g in range(mix.chunks)
    ]
    scale_a = jnp.broadcast_to(
        lax.rsqrt(sums[STRIDE:, 0:1] / width + EPSILON), (rows_a + 16, HEAD_DIM)
    )
    for h in range(heads):
        c = columns(h)
        taps = [mix.conv_v[k : k + 1, c] for k in range(3)]
        gain = mix.gain_v[0:1, c]
        for g in range(mix.chunks):
            mixed = sum(taps[k] * mix.video_att(g + k - 1, c) for k in range(3))
            s = slice(g * STRIDE, (g + 1) * STRIDE)
            out_v[s, c] = (mixed * scales[g] * gain).astype(BF)
        normed = mix.audio(c)[0] * scale_a
        out_a[:, c] = (normed * mix.gain_a[0:1, c])[8 : 8 + rows_a].astype(BF)


def video_backward(
    count, idx, window, valid, q, grad, re, ro, conv, lse, k, v, kve, kvo,
    dq_far, own, send_e, send_o, dq, sems_out,
):
    rows = q.shape[0]
    heads = q.shape[1] // HEAD_DIM
    back = Stream([(dq, dq_far)], sems_out, heads)
    near = k.shape[0]
    i = idx[0]
    even = (i & 1) == 0
    has_prev = (i > 0).astype(F32)
    has_next = (i < count - 1).astype(F32)
    bias = video_bias(i, count, window, valid, rows, near)
    halo = slice(near, near + STRIDE)
    for group in groups(heads, CHUNK):
        upstream, scores, prob_grad, prob, score_grad = {}, {}, {}, {}, {}
        for h in group:
            c = columns(h)
            keys = near_columns(k, kve, kvo, c, 0)
            scores[h] = dot(keys, q[:, c], 1, 1) * FACTOR + bias
        for h in group:
            c = columns(h)
            first, second = re[halo, c].astype(F32), ro[halo, c].astype(F32)
            before = jnp.where(even, second, first) * has_prev
            after = jnp.where(even, first, second) * has_next
            own_grad = grad[:, c]
            wide = jnp.concatenate([before, own_grad, after], 0)
            upstream[h] = (
                conv[0:1, c] * wide[2 * STRIDE :]
                + conv[1:2, c] * own_grad
                + conv[2:3, c] * wide[0:rows]
            ).astype(BF)
            prob_grad[h] = dot(near_columns(v, kve, kvo, c, 1), upstream[h], 1, 1)
        for h in group:
            p = jnp.exp(scores[h] - lse[h : h + 1, :])
            row_dot = jnp.sum(p * prob_grad[h], 0, keepdims=True)
            score_grad[h] = (p * (prob_grad[h] - row_dot)).astype(BF)
            prob[h] = p.astype(BF)
        for h in group:
            c = columns(h)
            keys = near_columns(k, kve, kvo, c, 0)
            dq[:, c] = (dot(score_grad[h], keys, 0, 0) * FACTOR).astype(BF)
            dk = dot(score_grad[h], q[:, c], 1, 0) * FACTOR
            dv = dot(prob[h], upstream[h], 1, 0)
            for part, value in enumerate((dk, dv)):
                s = slice(part * near, (part + 1) * near)
                own[s, c] = value[0:near]
                send_e[s, c] = value[near : 2 * near].astype(BF)
                send_o[s, c] = value[2 * near :].astype(BF)
            back.after_head(h)
    back.wait_all()


def audio_backward(
    count, idx, window, valid, q, qe, qo, up, re, ro, total, dots, k, v,
    part_e, part_o, dk_far, dv_far, own, send_e, send_o, dk, dv, sems_out,
):
    rows = q.shape[0]
    heads = q.shape[1] // HEAD_DIM
    back = Stream([(dk, dk_far), (dv, dv_far)], sems_out, heads)
    tail = slice(heads * HEAD_DIM, heads * HEAD_DIM + PAD)
    bias = audio_bias(idx[0], count, window, valid, rows, k.shape[0])
    totals, row_dots = [total[...]], [dots[...]]
    for r in (re, ro):
        wide = unpack_stats(r[0:rows, tail])
        totals.append(wide)
        row_dots.append(pltpu.roll(wide, 64, 1))
    blank = jnp.zeros((PAD - 3 * rows, PAD), F32)
    totals = jnp.transpose(jnp.concatenate(totals + [blank], 0))
    row_dots = jnp.transpose(jnp.concatenate(row_dots + [blank], 0))
    up_e, up_o = re.at[0:rows], ro.at[0:rows]
    done = slice(0, 2 * rows)
    send_e[done, :] = part_e[...]
    send_o[done, :] = part_o[...]
    for group in groups(heads, CHUNK):
        scores, prob_grad, prob, score_grad = {}, {}, {}, {}
        for h in group:
            c = columns(h)
            scores[h] = dot(k[:, c], padded(q, qe, qo, c), 1, 1) * FACTOR + bias
            prob_grad[h] = dot(v[:, c], padded(up, up_e, up_o, c), 1, 1)
        for h in group:
            p = jnp.exp(scores[h] - totals[h : h + 1, :])
            score_grad[h] = (p * (prob_grad[h] - row_dots[h : h + 1, :])).astype(BF)
            prob[h] = p.astype(BF)
        for h in group:
            c = columns(h)
            grad = dot(score_grad[h], k[:, c], 0, 0) * FACTOR
            dk[:, c] = (dot(score_grad[h], padded(q, qe, qo, c), 1, 0) * FACTOR).astype(BF)
            dv[:, c] = dot(prob[h], padded(up, up_e, up_o, c), 1, 0).astype(BF)
            own[:, c] = grad[:rows]
            send_e[2 * rows :, c] = grad[rows : 2 * rows].astype(BF)
            send_o[2 * rows :, c] = grad[2 * rows : 3 * rows].astype(BF)
            back.after_head(h)
    back.wait_all()


def per_device(
    query_video,
    key_video,
    value_video,
    query_audio,
    key_audio,
    value_audio,
    conv_video,
    conv_audio,
    gain_video,
    gain_audio,
    video_window,
    audio_window,
    video_valid,
    audio_valid,
    cotangent_video,
    cotangent_audio,
):
    count = video_window.shape[0]
    block = lax.axis_index(BLOCKS)
    idx = block.astype(jnp.int32).reshape(1)
    rows_v, wide = query_video.shape
    rows_a = query_audio.shape[0]
    heads = wide // HEAD_DIM
    model = wide * lax.axis_size("tp")
    even_route = [(i, i ^ 1) for i in range(count)]
    odd_route = [(i, other(i, count)) for i in range(count)]

    def swap_e(x):
        return lax.ppermute(x, BLOCKS, even_route)

    def swap_o(x):
        return lax.ppermute(x, BLOCKS, odd_route)

    def bind(f, *extra):
        def kernel(*refs):
            return f(*extra, *refs)

        return kernel

    qe, qo = swap_e(query_audio), swap_o(query_audio)
    (both,) = call(
        pack_rows, [((2 * rows_a, wide), BF)], [key_audio, value_audio], (), 0.5,
        [pltpu.SemaphoreType.DMA((2,))], (0, 1),
    )
    kve, kvo = swap_e(both), swap_o(both)
    big = pltpu.VMEM((rows_v, wide), BF)

    def sems(count):
        return pltpu.SemaphoreType.DMA((count, heads // CHUNK))

    packed = ((rows_a, wide + PAD), BF)
    audio_info = (idx, audio_window.T, video_valid)
    video_info = (idx, video_window.T, audio_valid)
    send_e, send_o, own_part, own_lse = call(
        bind(audio_forward, count),
        [packed, packed, ((rows_a, wide), F32), ((rows_a, PAD), F32)],
        [query_audio, qe, qo, key_video, value_video],
        audio_info,
        3.0,
        [pltpu.VMEM((PAD, PAD), F32)],
    )
    pe, po = swap_e(send_e), swap_o(send_o)
    keys_values = [key_audio, value_audio, kve, kvo]
    halo = ((STRIDE, wide), BF)
    att_v, lse_v, hv_e, hv_o = call(
        bind(video_forward, count),
        [((rows_v, wide), BF), (((heads + 7) // 8 * 8, rows_v), F32), halo, halo],
        [query_video] + keys_values + [own_lse],
        video_info,
        2.5,
        (),
        (),
        (),
        (5,),
    )
    hve, hvo = swap_e(hv_e), swap_o(hv_o)
    halo_a = ((16, wide), BF)
    att_a, total_a, ha_e, ha_o = call(
        audio_combine,
        [((rows_a, wide), BF), ((rows_a, PAD), F32), halo_a, halo_a],
        [own_part, own_lse, pe, po, cotangent_audio],
        (idx,),
        0.5,
    )
    hae, hao = swap_e(ha_e), swap_o(ha_o)

    mix_args = [
        att_v, hve, hvo, cotangent_video,
        att_a, hae, hao, cotangent_audio,
        conv_video, conv_audio, gain_video.reshape(1, wide), gain_audio.reshape(1, wide),
    ]
    stats_rows = STRIDE + rows_a + 16
    (stats,) = call(
        bind(row_sums, count), [((stats_rows, PAD), F32)], mix_args, (idx,), 1.3
    )
    tp_size = lax.axis_size("tp")
    stats_other = lax.ppermute(stats, "tp", [(i, i ^ 1) for i in range(tp_size)])
    chunks = rows_v // STRIDE
    both = ((rows_a + STRIDE, wide + PAD), BF)
    grad_v, up_a, back_e, back_o, dots_a, parts = call(
        bind(norm_backward, count, model),
        [
            ((rows_v, wide), F32),
            ((rows_a, wide), BF),
            both,
            both,
            ((rows_a, PAD), F32),
            ((8, wide), F32),
        ],
        [stats, stats_other] + mix_args + [total_a],
        (idx,),
        2.5,
        [pltpu.VMEM((rows_v, HEAD_DIM), F32)] * 2,
    )
    re, ro = swap_e(back_e), swap_o(back_o)

    def moved(x, bits):
        return lax.ppermute(x, BLOCKS, [(i, i ^ bits) for i in range(count)])

    def summed(x, bits, *after):
        (y,) = call(
            plus, [((8, wide), F32)], [x, moved(x, bits)] + list(after), (), 0.5,
            (), (), (), range(2, 2 + len(after)),
        )
        return y

    total = summed(parts, 16)
    out_v, out_a, token = call(
        bind(outputs, count, model),
        [((rows_v, wide), BF), ((rows_a, wide), BF), ((8, PAD), F32)],
        [stats, stats_other] + mix_args + [total],
        (idx,),
        1.5,
        (),
        (),
        (),
        (14,),
    )
    total = summed(total, 32, token)
    total = summed(total, 2, re, ro)

    two = ((2 * rows_a, wide), BF)
    dq_v, dkv_own, dkv_e, dkv_o = call(
        bind(video_backward, count),
        [((rows_v, wide), BF), ((2 * rows_a, wide), F32), two, two],
        [query_video, grad_v, re, ro, conv_video, lse_v] + keys_values,
        video_info,
        4.5,
        [big, sems(1)],
        (),
        (0,),
    )
    total = summed(total, 1, dkv_own)
    three = ((3 * rows_a, wide), BF)
    dk_v, dv_v, dq_own, give_e, give_o = call(
        bind(audio_backward, count),
        [((rows_v, wide), BF), ((rows_v, wide), BF), ((rows_a, wide), F32), three, three],
        [query_audio, qe, qo, up_a, re, ro, total_a, dots_a, key_video, value_video,
         dkv_e, dkv_o],
        audio_info,
        4.5,
        [big] * 2 + [sems(2)],
        (),
        (0, 1),
    )
    got_e, got_o = swap_e(give_e), swap_o(give_o)
    total = summed(total, 96, dq_own)
    total = summed(total, 4)
    taps_v, taps_a, gain_v, gain_a = call(
        split_sums,
        [((3, wide), F32), ((3, wide), F32), ((wide,), F32), ((wide,), F32)],
        [total, moved(total, 14)],
        (),
        0.5,
    )
    own = jnp.concatenate([dkv_own, dq_own], 0)
    grads = (own + got_e.astype(F32) + got_o.astype(F32)).astype(BF)
    return (
        out_v,
        out_a,
        dq_v,
        dk_v,
        dv_v,
        grads[2 * rows_a :],
        grads[:rows_a],
        grads[rows_a : 2 * rows_a],
        taps_v,
        taps_a,
        gain_v,
        gain_a,
    )


def solution(mesh):
    rows = P(BLOCKS, "tp")
    in_specs = (rows,) * 6 + (P(None, "tp"),) * 2 + (P("tp"),) * 2 + (P(),) * 4 + (rows,) * 2
    out_specs = (rows,) * 8 + (P(None, "tp"),) * 2 + (P("tp"),) * 2
    return jax.shard_map(
        per_device, mesh=mesh, in_specs=in_specs, out_specs=out_specs, check_vma=False
    )
```

```python
import jax
import jax.numpy as jnp
from jax import lax
from jax.experimental import pallas as pl
from jax.experimental.pallas import tpu as pltpu
from jax.sharding import PartitionSpec as P

HEAD_DIM = 128
STRIDE = 32
NEGATIVE = -1e30
EPSILON = 1e-06
FACTOR = HEAD_DIM ** (-0.5)
BLOCKS = ("video", "audio")
BF = jnp.bfloat16
F32 = jnp.float32
PAD = 128


def dot(a, b, over_a, over_b):
    return lax.dot_general(
        a, b, (((over_a,), (over_b,)), ((), ())), preferred_element_type=F32
    )


def call(kernel, outs, args, scalars, micros, scratch=(), far_args=(), far_outs=(), unread=()):
    vmem = pl.BlockSpec(memory_space=pltpu.VMEM)
    smem = pl.BlockSpec(memory_space=pltpu.SMEM)
    anywhere = pl.BlockSpec(memory_space=pl.ANY)
    far = pl.BlockSpec(memory_space=pltpu.HBM)
    size = sum(a.size * a.dtype.itemsize for a in args)
    return pl.pallas_call(
        kernel,
        out_shape=[jax.ShapeDtypeStruct(s, d) for s, d in outs],
        in_specs=[smem] * len(scalars)
        + [
            anywhere if n in unread else far if n in far_args else vmem
            for n in range(len(args))
        ],
        out_specs=[anywhere if n in far_outs else vmem for n in range(len(outs))],
        scratch_shapes=list(scratch),
        compiler_params=pltpu.CompilerParams(vmem_limit_bytes=48 * 1024 * 1024),
        cost_estimate=pl.CostEstimate(
            flops=int(micros * 1.1e9), bytes_accessed=size, transcendentals=0
        ),
    )(*scalars, *args)


CHUNK = 6


class Stream:
    def __init__(self, pairs, sems, heads):
        self.pairs, self.sems = pairs, sems
        self.parts = heads // CHUNK

    def copies(self, part):
        c = slice(part * CHUNK * HEAD_DIM, (part + 1) * CHUNK * HEAD_DIM)
        return [
            pltpu.make_async_copy(src.at[:, c], dst.at[:, c], self.sems.at[n, part])
            for n, (src, dst) in enumerate(self.pairs)
        ]

    def start(self, part):
        for copy in self.copies(part):
            copy.start()

    def wait(self, part):
        for copy in self.copies(part):
            copy.wait()

    def start_all(self):
        for part in range(self.parts):
            self.start(part)

    def wait_all(self):
        for part in range(self.parts):
            self.wait(part)

    def before_head(self, h):
        if h % CHUNK == 0:
            self.wait(h // CHUNK)

    def after_head(self, h):
        if h % CHUNK == CHUNK - 1:
            self.start(h // CHUNK)


def pack_rows(k, v, both, sems):
    rows = k.shape[0]
    copies = [
        pltpu.make_async_copy(k, both.at[0:rows], sems.at[0]),
        pltpu.make_async_copy(v, both.at[rows:], sems.at[1]),
    ]
    for copy in copies:
        copy.start()
    for copy in copies:
        copy.wait()


def plus(*refs):
    refs[-1][...] = refs[0][...] + refs[1][...]


def settle(dkv, dq, e, o, dk_out, dv_out, dq_out, token):
    rows = dq.shape[0]
    token[...] = jnp.zeros(token.shape, F32)
    for n, out in enumerate((dk_out, dv_out, dq_out)):
        s = slice(n * rows, (n + 1) * rows)
        mine = dkv[s, :] if n < 2 else dq[...]
        out[...] = (mine + e[s, :].astype(F32) + o[s, :].astype(F32)).astype(BF)


def split_sums(mine, theirs, _, taps_v, taps_a, gain_v, gain_a):
    total = mine[...] + theirs[...]
    taps_v[...] = total[0:3]
    gain_v[...] = total[3]
    taps_a[...] = total[4:7]
    gain_a[...] = total[7]


def other(i, count):
    return (i + 2 * (i & 1) - 1 + count) & (count - 1)


def groups(heads, size):
    return [range(g, min(g + size, heads)) for g in range(0, heads, size)]


def columns(h):
    return slice(h * HEAD_DIM, (h + 1) * HEAD_DIM)


def pack_stats(tile):
    high = tile.astype(BF).astype(F32)
    rest = tile - high
    middle = rest.astype(BF).astype(F32)
    low = rest - middle
    return (high + pltpu.roll(middle, 16, 1) + pltpu.roll(low, 32, 1)).astype(BF)


def unpack_stats(packed):
    wide = packed.astype(F32)
    return wide + (pltpu.roll(wide, PAD - 16, 1) + pltpu.roll(wide, PAD - 32, 1))


def audio_bias(i, count, window, valid, rows_q, rows_k):
    row = lax.broadcasted_iota(jnp.int32, (rows_k, 4 * rows_q), 0)
    slot = lax.broadcasted_iota(jnp.int32, (rows_k, 4 * rows_q), 1) // rows_q
    position = i * rows_k + row
    blocks = (i, i ^ 1, other(i, count))
    lower, upper = [
        jnp.where(
            slot == 0,
            window[side, blocks[0]],
            jnp.where(slot == 1, window[side, blocks[1]], window[side, blocks[2]]),
        )
        for side in (0, 1)
    ]
    seen = (position >= lower) & (position < upper) & (row < valid[i]) & (slot < 3)
    return jnp.where(seen, 0.0, NEGATIVE)


def padded(own, e, o, c):
    return jnp.concatenate(
        [own[:, c], e[:, c], o[:, c], jnp.zeros((own.shape[0], HEAD_DIM), BF)], 0
    )


def video_bias(i, count, window, valid, rows_q, rows_k):
    row = lax.broadcasted_iota(jnp.int32, (rows_k, rows_q), 0)
    parts = []
    for c in (i, i ^ 1, other(i, count)):
        position = c * rows_k + row
        seen = (position >= window[0, i]) & (position < window[1, i]) & (row < valid[c])
        parts.append(jnp.where(seen, 0.0, NEGATIVE))
    return jnp.concatenate(parts, 0)


def audio_forward(
    count, idx, window, valid, q, qe, qo, k, v, send_e, send_o, own, own_lse,
    rows_lse,
):
    rows = q.shape[0]
    heads = q.shape[1] // HEAD_DIM
    bias = audio_bias(idx[0], count, window, valid, rows, k.shape[0])
    rows_lse[...] = jnp.zeros(rows_lse.shape, F32)
    for group in groups(heads, heads):
        scores, probs = {}, {}
        for h in group:
            c = columns(h)
            scores[h] = dot(k[:, c], padded(q, qe, qo, c), 1, 1) * FACTOR + bias
        for h in group:
            peak = jnp.max(scores[h], 0, keepdims=True)
            weight = jnp.exp(scores[h] - peak)
            total = jnp.sum(weight, 0, keepdims=True)
            rows_lse[h : h + 1, :] = peak + jnp.log(total)
            probs[h] = (weight * (1.0 / total)).astype(BF)
        for h in group:
            c = columns(h)
            part = dot(probs[h], v[:, c], 0, 0)
            own[:, c] = part[:rows]
            send_e[:, c] = part[rows : 2 * rows].astype(BF)
            send_o[:, c] = part[2 * rows : 3 * rows].astype(BF)
    tile = jnp.transpose(rows_lse[...])
    own_lse[...] = tile[:rows]
    tail = slice(heads * HEAD_DIM, heads * HEAD_DIM + PAD)
    send_e[:, tail] = pack_stats(tile[rows : 2 * rows])
    send_o[:, tail] = pack_stats(tile[2 * rows : 3 * rows])


def near_columns(own, e, o, c, part):
    rows = own.shape[0]
    s = slice(part * rows, (part + 1) * rows)
    return jnp.concatenate([own[:, c], e[s, c], o[s, c]], 0)


def video_forward(
    count, idx, window, valid, q, k, v, kve, kvo, _, att, lse
):
    rows = q.shape[0]
    heads = q.shape[1] // HEAD_DIM
    i = idx[0]
    bias = video_bias(i, count, window, valid, rows, k.shape[0])
    lse[...] = jnp.zeros(lse.shape, F32)
    for group in groups(heads, heads):
        scores, probs = {}, {}
        for h in group:
            c = columns(h)
            keys = near_columns(k, kve, kvo, c, 0)
            scores[h] = dot(keys, q[:, c], 1, 1) * FACTOR + bias
        for h in group:
            peak = jnp.max(scores[h], 0, keepdims=True)
            weight = jnp.exp(scores[h] - peak)
            total = jnp.sum(weight, 0, keepdims=True)
            lse[h : h + 1, :] = peak + jnp.log(total)
            probs[h] = (weight * (1.0 / total)).astype(BF)
        for h in group:
            c = columns(h)
            att[:, c] = dot(probs[h], near_columns(v, kve, kvo, c, 1), 0, 0).astype(BF)


def audio_combine(
    idx, own, own_lse, re, ro, cot, att_v, att, total, send_e, send_o, first, last
):
    rows = own.shape[0]
    heads = own.shape[1] // HEAD_DIM
    tail = slice(heads * HEAD_DIM, heads * HEAD_DIM + PAD)
    mine = own_lse[...]
    lse_e = unpack_stats(re[:, tail])
    lse_o = unpack_stats(ro[:, tail])
    peak = jnp.maximum(mine, jnp.maximum(lse_e, lse_o))
    whole = peak + jnp.log(
        jnp.exp(mine - peak) + jnp.exp(lse_e - peak) + jnp.exp(lse_o - peak)
    )
    total[...] = whole
    wm, we, wo = jnp.exp(mine - whole), jnp.exp(lse_e - whole), jnp.exp(lse_o - whole)
    first[...] = jnp.zeros(first.shape, F32)
    last[...] = jnp.zeros(last.shape, F32)
    for h in range(heads):
        c = columns(h)
        joined = (
            own[:, c] * wm[:, h : h + 1]
            + re[:, c].astype(F32) * we[:, h : h + 1]
            + ro[:, c].astype(F32) * wo[:, h : h + 1]
        )
        att[:, c] = joined.astype(BF)
        incoming = cot[:, c].astype(F32)
        for edge, pair, only in ((first, 0, 0), (last, rows - 2, rows - 1)):
            edge[h : h + 1, 0:PAD] = joined[pair : pair + 1]
            edge[16 + h : 17 + h, 0:PAD] = joined[pair + 1 : pair + 2]
            edge[h : h + 1, PAD:] = incoming[only : only + 1]
    odd = idx[0] & 1
    for send, side in ((send_e, 1 - odd), (send_o, odd)):
        start = pl.multiple_of(side * (att_v.shape[0] - STRIDE), STRIDE)
        send[:, 0 : heads * HEAD_DIM] = att_v[pl.ds(start, STRIDE), :]
        send[:, heads * HEAD_DIM :] = jnp.where(side == 1, last[...], first[...]).astype(BF)


class Mix:
    def __init__(self, count, idx, refs):
        self.i = idx[0]
        self.even = (self.i & 1) == 0
        self.has_prev = (self.i > 0).astype(F32)
        self.has_next = (self.i < count - 1).astype(F32)
        (self.att_v, self.he, self.ho, self.cot_v, self.att_a, self.cot_a,
         self.conv_v, self.conv_a, self.gain_v, self.gain_a) = refs
        self.chunks = self.att_v.shape[0] // STRIDE
        edges = slice(self.att_v.shape[1], self.att_v.shape[1] + 2 * PAD)
        self.low = self.before(self.he[:, edges], self.ho[:, edges])
        self.high = self.after(self.he[:, edges], self.ho[:, edges])
        self.row = lax.broadcasted_iota(jnp.int32, (8, HEAD_DIM), 0)

    def before(self, e, o):
        return jnp.where(self.even, o.astype(F32), e.astype(F32)) * self.has_prev

    def after(self, e, o):
        return jnp.where(self.even, e.astype(F32), o.astype(F32)) * self.has_next

    def video_att(self, g, c):
        if g < 0:
            return self.before(self.he[:, c], self.ho[:, c])
        if g >= self.chunks:
            return self.after(self.he[:, c], self.ho[:, c])
        return self.att_v[g * STRIDE : (g + 1) * STRIDE, c].astype(F32)

    def video_cot(self, g, c):
        return self.cot_v[g * STRIDE : (g + 1) * STRIDE, c].astype(F32)

    def placed(self, at, value):
        return jnp.where(self.row == at, value, 0.0)

    def audio_att(self, c):
        h = c.start // HEAD_DIM
        low, high = self.low[:, 0:PAD], self.high[:, 0:PAD]
        return jnp.concatenate(
            [
                self.placed(6, low[h : h + 1]) + self.placed(7, low[16 + h : 17 + h]),
                self.att_a[:, c].astype(F32),
                self.placed(0, high[h : h + 1]) + self.placed(1, high[16 + h : 17 + h]),
            ],
            0,
        )

    def audio_cot(self, c):
        h = c.start // HEAD_DIM
        return jnp.concatenate(
            [
                self.placed(7, self.low[h : h + 1, PAD:]),
                self.cot_a[:, c].astype(F32),
                self.placed(0, self.high[h : h + 1, PAD:]),
            ],
            0,
        )

    def audio(self, c):
        att = self.audio_att(c)
        rows = att.shape[0]
        early = pltpu.roll(att, 1, 0)
        late = pltpu.roll(att, rows - 1, 0)
        taps = self.conv_a
        mixed = taps[0:1, c] * early + taps[1:2, c] * att + taps[2:3, c] * late
        cot = self.audio_cot(c)
        return mixed, cot, early, att, late


def row_sums(count, idx, *refs):
    mix = Mix(count, idx, refs[:-1])
    stats = refs[-1]
    heads = mix.att_v.shape[1] // HEAD_DIM
    rows_a = mix.att_a.shape[0] + 16
    lane = lax.broadcasted_iota(jnp.int32, (STRIDE, PAD), 1)
    tile = jnp.zeros((STRIDE, PAD), F32)
    taps = mix.conv_v
    for g in range(mix.chunks):
        square = jnp.zeros((STRIDE, HEAD_DIM), F32)
        inner = jnp.zeros((STRIDE, HEAD_DIM), F32)
        for h in range(heads):
            c = columns(h)
            mixed = (
                taps[0:1, c] * mix.video_att(g - 1, c)
                + taps[1:2, c] * mix.video_att(g, c)
                + taps[2:3, c] * mix.video_att(g + 1, c)
            )
            square += mixed * mixed
            inner += mix.video_cot(g, c) * mix.gain_v[0:1, c] * mixed
        tile = jnp.where(lane == g, jnp.sum(square, 1, keepdims=True), tile)
        tile = jnp.where(lane == g + 16, jnp.sum(inner, 1, keepdims=True), tile)
    lane_a = lax.broadcasted_iota(jnp.int32, (rows_a, PAD), 1)
    square = jnp.zeros((rows_a, HEAD_DIM), F32)
    inner = jnp.zeros((rows_a, HEAD_DIM), F32)
    for h in range(heads):
        c = columns(h)
        mixed, cot, _, _, _ = mix.audio(c)
        square += mixed * mixed
        inner += cot * mix.gain_a[0:1, c] * mixed
    tile_a = jnp.where(
        lane_a == 0,
        jnp.sum(square, 1, keepdims=True),
        jnp.where(lane_a == 1, jnp.sum(inner, 1, keepdims=True), 0.0),
    )
    stats[0:STRIDE, :] = tile
    stats[STRIDE:, :] = tile_a


def norm_backward(count, width, idx, *refs):
    mix = Mix(count, idx, refs[2:12])
    mine, theirs = refs[0], refs[1]
    total_a = refs[12]
    grad_v, up_a, send_e, send_o, dots_a, parts = refs[13:19]
    scale_ref, shrink_ref = refs[19:21]
    heads = mix.att_v.shape[1] // HEAD_DIM
    sums = mine[...] + theirs[...]
    rows_a = mix.att_a.shape[0]
    ext = rows_a + 16
    for g in range(mix.chunks):
        inverse = lax.rsqrt(sums[0:STRIDE, g : g + 1] / width + EPSILON)
        inner = sums[0:STRIDE, g + 16 : g + 17]
        s = slice(g * STRIDE, (g + 1) * STRIDE)
        scale_ref[s, :] = jnp.broadcast_to(inverse, (STRIDE, HEAD_DIM))
        shrink_ref[s, :] = jnp.broadcast_to(
            inverse * inverse * inverse * inner / width, (STRIDE, HEAD_DIM)
        )
    row = lax.broadcasted_iota(jnp.int32, (ext, HEAD_DIM), 0)
    present = jnp.where(row < 8, mix.has_prev, jnp.where(row >= rows_a + 8, mix.has_next, 1.0))
    inverse = lax.rsqrt(sums[STRIDE:, 0:1] / width + EPSILON)
    scale_a = jnp.broadcast_to(inverse, (ext, HEAD_DIM)) * present
    shrink_a = (
        jnp.broadcast_to(
            inverse * inverse * inverse * sums[STRIDE:, 1:2] / width, (ext, HEAD_DIM)
        )
        * present
    )
    lane = lax.broadcasted_iota(jnp.int32, (rows_a, PAD), 1)
    dots = jnp.zeros((rows_a, PAD), F32)
    own = slice(8, 8 + rows_a)
    for h in range(heads):
        c = columns(h)
        taps = [mix.conv_v[k : k + 1, c] for k in range(3)]
        gain = mix.gain_v[0:1, c]
        sum_taps = [jnp.zeros((STRIDE, HEAD_DIM), F32) for _ in range(3)]
        sum_gain = jnp.zeros((STRIDE, HEAD_DIM), F32)
        atts = [mix.video_att(g, c) for g in (-1, 0, 1)]
        for g in range(mix.chunks):
            mixed = taps[0] * atts[0] + taps[1] * atts[1] + taps[2] * atts[2]
            s = slice(g * STRIDE, (g + 1) * STRIDE)
            scale = scale_ref[s, :]
            incoming = mix.video_cot(g, c)
            grad = scale * (incoming * gain) - mixed * shrink_ref[s, :]
            normed = mixed * scale
            grad_v[s, c] = grad
            sum_gain += incoming * normed
            for k in range(3):
                sum_taps[k] += grad * atts[k]
            if g + 1 < mix.chunks:
                atts = atts[1:] + [mix.video_att(g + 2, c)]
        for k in range(3):
            parts[k : k + 1, c] = jnp.sum(sum_taps[k], 0, keepdims=True)
        parts[3:4, c] = jnp.sum(sum_gain, 0, keepdims=True)

        mixed, cot, early, att, late = mix.audio(c)
        gain = mix.gain_a[0:1, c]
        taps = [mix.conv_a[k : k + 1, c] for k in range(3)]
        normed = mixed * scale_a
        grad = scale_a * (cot * gain) - mixed * shrink_a
        upstream = (
            taps[0] * pltpu.roll(grad, ext - 1, 0)
            + taps[1] * grad
            + taps[2] * pltpu.roll(grad, 1, 0)
        )[own].astype(BF)
        up_a[:, c] = upstream
        send_e[0:rows_a, c] = upstream
        send_o[0:rows_a, c] = upstream
        row_dot = jnp.sum(upstream.astype(F32) * att[own], 1, keepdims=True)
        dots = jnp.where(lane == h, row_dot, dots)
        for k, shifted in enumerate((early, att, late)):
            parts[4 + k : 5 + k, c] = jnp.sum((grad * shifted)[own], 0, keepdims=True)
        parts[7:8, c] = jnp.sum((cot * normed)[own], 0, keepdims=True)
    dots_a[...] = dots
    tail = slice(heads * HEAD_DIM, heads * HEAD_DIM + PAD)
    packed = pack_stats(jnp.where(lane < heads, total_a[...], 0.0)).astype(F32)
    packed_dots = pack_stats(dots).astype(F32)
    packed = (packed + pltpu.roll(packed_dots, 64, 1)).astype(BF)
    odd = idx[0] & 1
    body = slice(0, heads * HEAD_DIM)
    for send, side in ((send_e, 1 - odd), (send_o, odd)):
        start = pl.multiple_of(side * (mix.att_v.shape[0] - STRIDE), STRIDE)
        send[0:rows_a, tail] = packed
        send[rows_a:, body] = grad_v[pl.ds(start, STRIDE), :].astype(BF)
        send[rows_a:, tail] = jnp.zeros((STRIDE, PAD), BF)


def outputs(count, width, idx, *refs):
    mix = Mix(count, idx, refs[2:12])
    sums = refs[0][...] + refs[1][...]
    out_v, out_a, token = refs[13:16]
    token[...] = jnp.zeros(token.shape, F32)
    heads = mix.att_v.shape[1] // HEAD_DIM
    rows_a = mix.att_a.shape[0]
    scales = [
        jnp.broadcast_to(
            lax.rsqrt(sums[0:STRIDE, g : g + 1] / width + EPSILON), (STRIDE, HEAD_DIM)
        )
        for g in range(mix.chunks)
    ]
    scale_a = jnp.broadcast_to(
        lax.rsqrt(sums[STRIDE:, 0:1] / width + EPSILON), (rows_a + 16, HEAD_DIM)
    )
    for h in range(heads):
        c = columns(h)
        taps = [mix.conv_v[k : k + 1, c] for k in range(3)]
        gain = mix.gain_v[0:1, c]
        for g in range(mix.chunks):
            mixed = sum(taps[k] * mix.video_att(g + k - 1, c) for k in range(3))
            s = slice(g * STRIDE, (g + 1) * STRIDE)
            out_v[s, c] = (mixed * scales[g] * gain).astype(BF)
        normed = mix.audio(c)[0] * scale_a
        out_a[:, c] = (normed * mix.gain_a[0:1, c])[8 : 8 + rows_a].astype(BF)


def video_backward(
    count, idx, window, valid, q, grad, re, ro, conv, lse, k, v, kve, kvo, _,
    dq_far, own, send_e, send_o, dq, sems_out,
):
    rows = q.shape[0]
    heads = q.shape[1] // HEAD_DIM
    back = Stream([(dq, dq_far)], sems_out, heads)
    near = k.shape[0]
    i = idx[0]
    even = (i & 1) == 0
    has_prev = (i > 0).astype(F32)
    has_next = (i < count - 1).astype(F32)
    bias = video_bias(i, count, window, valid, rows, near)
    halo = slice(near, near + STRIDE)
    for group in groups(heads, CHUNK):
        upstream, scores, prob_grad, prob, score_grad = {}, {}, {}, {}, {}
        for h in group:
            c = columns(h)
            keys = near_columns(k, kve, kvo, c, 0)
            scores[h] = dot(keys, q[:, c], 1, 1) * FACTOR + bias
        for h in group:
            c = columns(h)
            first, second = re[halo, c].astype(F32), ro[halo, c].astype(F32)
            before = jnp.where(even, second, first) * has_prev
            after = jnp.where(even, first, second) * has_next
            own_grad = grad[:, c]
            wide = jnp.concatenate([before, own_grad, after], 0)
            upstream[h] = (
                conv[0:1, c] * wide[2 * STRIDE :]
                + conv[1:2, c] * own_grad
                + conv[2:3, c] * wide[0:rows]
            ).astype(BF)
            prob_grad[h] = dot(near_columns(v, kve, kvo, c, 1), upstream[h], 1, 1)
        for h in group:
            p = jnp.exp(scores[h] - lse[h : h + 1, :])
            row_dot = jnp.sum(p * prob_grad[h], 0, keepdims=True)
            score_grad[h] = (p * (prob_grad[h] - row_dot)).astype(BF)
            prob[h] = p.astype(BF)
        for h in group:
            c = columns(h)
            keys = near_columns(k, kve, kvo, c, 0)
            dq[:, c] = (dot(score_grad[h], keys, 0, 0) * FACTOR).astype(BF)
            dk = dot(score_grad[h], q[:, c], 1, 0) * FACTOR
            dv = dot(prob[h], upstream[h], 1, 0)
            for part, value in enumerate((dk, dv)):
                s = slice(part * near, (part + 1) * near)
                own[s, c] = value[0:near]
                send_e[s, c] = value[near : 2 * near].astype(BF)
                send_o[s, c] = value[2 * near :].astype(BF)
            back.after_head(h)
    back.wait_all()


def audio_backward(
    count, idx, window, valid, q, qe, qo, up, re, ro, total, dots, k, v,
    part_e, part_o, _, dk_far, dv_far, own, send_e, send_o, dk, dv, sems_out,
):
    rows = q.shape[0]
    heads = q.shape[1] // HEAD_DIM
    back = Stream([(dk, dk_far), (dv, dv_far)], sems_out, heads)
    tail = slice(heads * HEAD_DIM, heads * HEAD_DIM + PAD)
    bias = audio_bias(idx[0], count, window, valid, rows, k.shape[0])
    totals, row_dots = [total[...]], [dots[...]]
    for r in (re, ro):
        wide = unpack_stats(r[0:rows, tail])
        totals.append(wide)
        row_dots.append(pltpu.roll(wide, 64, 1))
    blank = jnp.zeros((PAD - 3 * rows, PAD), F32)
    totals = jnp.transpose(jnp.concatenate(totals + [blank], 0))
    row_dots = jnp.transpose(jnp.concatenate(row_dots + [blank], 0))
    up_e, up_o = re.at[0:rows], ro.at[0:rows]
    done = slice(0, 2 * rows)
    send_e[done, :] = part_e[...]
    send_o[done, :] = part_o[...]
    for group in groups(heads, CHUNK):
        scores, prob_grad, prob, score_grad = {}, {}, {}, {}
        for h in group:
            c = columns(h)
            scores[h] = dot(k[:, c], padded(q, qe, qo, c), 1, 1) * FACTOR + bias
            prob_grad[h] = dot(v[:, c], padded(up, up_e, up_o, c), 1, 1)
        for h in group:
            p = jnp.exp(scores[h] - totals[h : h + 1, :])
            score_grad[h] = (p * (prob_grad[h] - row_dots[h : h + 1, :])).astype(BF)
            prob[h] = p.astype(BF)
        for h in group:
            c = columns(h)
            grad = dot(score_grad[h], k[:, c], 0, 0) * FACTOR
            dk[:, c] = (dot(score_grad[h], padded(q, qe, qo, c), 1, 0) * FACTOR).astype(BF)
            dv[:, c] = dot(prob[h], padded(up, up_e, up_o, c), 1, 0).astype(BF)
            own[:, c] = grad[:rows]
            send_e[2 * rows :, c] = grad[rows : 2 * rows].astype(BF)
            send_o[2 * rows :, c] = grad[2 * rows : 3 * rows].astype(BF)
            back.after_head(h)
    back.wait_all()


def per_device(
    query_video,
    key_video,
    value_video,
    query_audio,
    key_audio,
    value_audio,
    conv_video,
    conv_audio,
    gain_video,
    gain_audio,
    video_window,
    audio_window,
    video_valid,
    audio_valid,
    cotangent_video,
    cotangent_audio,
):
    count = video_window.shape[0]
    block = lax.axis_index(BLOCKS)
    idx = block.astype(jnp.int32).reshape(1)
    rows_v, wide = query_video.shape
    rows_a = query_audio.shape[0]
    heads = wide // HEAD_DIM
    model = wide * lax.axis_size("tp")
    even_route = [(i, i ^ 1) for i in range(count)]
    odd_route = [(i, other(i, count)) for i in range(count)]

    def swap_e(x):
        return lax.ppermute(x, BLOCKS, even_route)

    def swap_o(x):
        return lax.ppermute(x, BLOCKS, odd_route)

    def bind(f, *extra):
        def kernel(*refs):
            return f(*extra, *refs)

        return kernel

    qe, qo = swap_e(query_audio), swap_o(query_audio)
    (both,) = call(
        pack_rows, [((2 * rows_a, wide), BF)], [key_audio, value_audio], (), 0.5,
        [pltpu.SemaphoreType.DMA((2,))], (0, 1),
    )
    kve, kvo = swap_e(both), swap_o(both)
    big = pltpu.VMEM((rows_v, wide), BF)

    def sems(count):
        return pltpu.SemaphoreType.DMA((count, heads // CHUNK))

    packed = ((rows_a, wide + PAD), BF)
    audio_info = (idx, audio_window.T, video_valid)
    video_info = (idx, video_window.T, audio_valid)
    send_e, send_o, own_part, own_lse = call(
        bind(audio_forward, count),
        [packed, packed, ((rows_a, wide), F32), ((rows_a, PAD), F32)],
        [query_audio, qe, qo, key_video, value_video],
        audio_info,
        1.5,
        [pltpu.VMEM((PAD, PAD), F32)],
    )
    pe, po = swap_e(send_e), swap_o(send_o)
    keys_values = [key_audio, value_audio, kve, kvo]
    att_v, lse_v = call(
        bind(video_forward, count),
        [((rows_v, wide), BF), (((heads + 7) // 8 * 8, rows_v), F32)],
        [query_video] + keys_values + [own_lse],
        video_info,
        1.5,
        (),
        (),
        (),
        (5,),
    )
    halo = ((STRIDE, wide + 2 * PAD), BF)
    att_a, total_a, give_e, give_o = call(
        audio_combine,
        [((rows_a, wide), BF), ((rows_a, PAD), F32), halo, halo],
        [own_part, own_lse, pe, po, cotangent_audio, att_v],
        (idx,),
        0.5,
        [pltpu.VMEM((STRIDE, 2 * PAD), F32)] * 2,
    )
    he, ho = swap_e(give_e), swap_o(give_o)

    mix_args = [
        att_v, he, ho, cotangent_video, att_a, cotangent_audio,
        conv_video, conv_audio, gain_video.reshape(1, wide), gain_audio.reshape(1, wide),
    ]
    stats_rows = STRIDE + rows_a + 16
    (stats,) = call(
        bind(row_sums, count), [((stats_rows, PAD), F32)], mix_args, (idx,), 1.3
    )
    tp_size = lax.axis_size("tp")
    stats_other = lax.ppermute(stats, "tp", [(i, i ^ 1) for i in range(tp_size)])
    chunks = rows_v // STRIDE
    both = ((rows_a + STRIDE, wide + PAD), BF)
    grad_v, up_a, back_e, back_o, dots_a, parts = call(
        bind(norm_backward, count, model),
        [
            ((rows_v, wide), F32),
            ((rows_a, wide), BF),
            both,
            both,
            ((rows_a, PAD), F32),
            ((8, wide), F32),
        ],
        [stats, stats_other] + mix_args + [total_a],
        (idx,),
        2.5,
        [pltpu.VMEM((rows_v, HEAD_DIM), F32)] * 2,
    )
    re, ro = swap_e(back_e), swap_o(back_o)

    def moved(x, bits):
        return lax.ppermute(x, BLOCKS, [(i, i ^ bits) for i in range(count)])

    def summed(x, bits, *after):
        (y,) = call(
            plus, [((8, wide), F32)], [x, moved(x, bits)] + list(after), (), 0.5,
            (), (), (), range(2, 2 + len(after)),
        )
        return y

    total = summed(parts, 16)
    out_v, out_a, token = call(
        bind(outputs, count, model),
        [((rows_v, wide), BF), ((rows_a, wide), BF), ((8, PAD), F32)],
        [stats, stats_other] + mix_args + [total],
        (idx,),
        1.5,
        (),
        (),
        (),
        (12,),
    )
    total = summed(total, 32, token)
    total = summed(total, 2)

    two = ((2 * rows_a, wide), BF)
    dq_v, dkv_own, dkv_e, dkv_o = call(
        bind(video_backward, count),
        [((rows_v, wide), BF), ((2 * rows_a, wide), F32), two, two],
        [query_video, grad_v, re, ro, conv_video, lse_v] + keys_values + [total],
        video_info,
        3.0,
        [big, sems(1)],
        (),
        (0,),
        (10,),
    )
    three = ((3 * rows_a, wide), BF)
    total = summed(total, 1, dkv_own)
    dk_v, dv_v, dq_own, give_e, give_o = call(
        bind(audio_backward, count),
        [((rows_v, wide), BF), ((rows_v, wide), BF), ((rows_a, wide), F32), three, three],
        [query_audio, qe, qo, up_a, re, ro, total_a, dots_a, key_video, value_video,
         dkv_e, dkv_o, total],
        audio_info,
        3.0,
        [big] * 2 + [sems(2)],
        (),
        (0, 1),
        (12,),
    )
    got_e, got_o = swap_e(give_e), swap_o(give_o)
    total = summed(total, 96, dq_own)
    total = summed(total, 14)
    one = ((rows_a, wide), BF)
    dk_a, dv_a, dq_a, token = call(
        settle,
        [one, one, one, ((8, PAD), F32)],
        [dkv_own, dq_own, got_e, got_o],
        (),
        0.5,
    )
    taps_v, taps_a, gain_v, gain_a = call(
        split_sums,
        [((3, wide), F32), ((3, wide), F32), ((wide,), F32), ((wide,), F32)],
        [total, moved(total, 4), token],
        (),
        0.5,
        (),
        (),
        (),
        (2,),
    )
    return (
        out_v,
        out_a,
        dq_v,
        dk_v,
        dv_v,
        dq_a,
        dk_a,
        dv_a,
        taps_v,
        taps_a,
        gain_v,
        gain_a,
    )


def solution(mesh):
    rows = P(BLOCKS, "tp")
    in_specs = (rows,) * 6 + (P(None, "tp"),) * 2 + (P("tp"),) * 2 + (P(),) * 4 + (rows,) * 2
    out_specs = (rows,) * 8 + (P(None, "tp"),) * 2 + (P("tp"),) * 2
    return jax.shard_map(
        per_device, mesh=mesh, in_specs=in_specs, out_specs=out_specs, check_vma=False
    )
```

```python
import jax
import jax.numpy as jnp
from jax import lax
from jax.experimental import pallas as pl
from jax.experimental.pallas import tpu as pltpu
from jax.sharding import PartitionSpec as P

HEAD_DIM = 128
STRIDE = 32
NEGATIVE = -1e30
EPSILON = 1e-06
FACTOR = HEAD_DIM ** (-0.5)
BLOCKS = ("video", "audio")
BF = jnp.bfloat16
F32 = jnp.float32
PAD = 128


def dot(a, b, over_a, over_b):
    return lax.dot_general(
        a, b, (((over_a,), (over_b,)), ((), ())), preferred_element_type=F32
    )


def call(kernel, outs, args, scalars, micros, scratch=(), far_args=(), far_outs=(), unread=()):
    vmem = pl.BlockSpec(memory_space=pltpu.VMEM)
    smem = pl.BlockSpec(memory_space=pltpu.SMEM)
    anywhere = pl.BlockSpec(memory_space=pl.ANY)
    far = pl.BlockSpec(memory_space=pltpu.HBM)
    size = sum(a.size * a.dtype.itemsize for a in args)
    return pl.pallas_call(
        kernel,
        out_shape=[jax.ShapeDtypeStruct(s, d) for s, d in outs],
        in_specs=[smem] * len(scalars)
        + [
            anywhere if n in unread else far if n in far_args else vmem
            for n in range(len(args))
        ],
        out_specs=[anywhere if n in far_outs else vmem for n in range(len(outs))],
        scratch_shapes=list(scratch),
        compiler_params=pltpu.CompilerParams(vmem_limit_bytes=48 * 1024 * 1024),
        cost_estimate=pl.CostEstimate(
            flops=int(micros * 1.1e9), bytes_accessed=size, transcendentals=0
        ),
    )(*scalars, *args)


CHUNK = 6


class Stream:
    def __init__(self, pairs, sems, heads):
        self.pairs, self.sems = pairs, sems
        self.parts = heads // CHUNK

    def copies(self, part):
        c = slice(part * CHUNK * HEAD_DIM, (part + 1) * CHUNK * HEAD_DIM)
        return [
            pltpu.make_async_copy(src.at[:, c], dst.at[:, c], self.sems.at[n, part])
            for n, (src, dst) in enumerate(self.pairs)
        ]

    def start(self, part):
        for copy in self.copies(part):
            copy.start()

    def wait(self, part):
        for copy in self.copies(part):
            copy.wait()

    def start_all(self):
        for part in range(self.parts):
            self.start(part)

    def wait_all(self):
        for part in range(self.parts):
            self.wait(part)

    def before_head(self, h):
        if h % CHUNK == 0:
            self.wait(h // CHUNK)

    def after_head(self, h):
        if h % CHUNK == CHUNK - 1:
            self.start(h // CHUNK)


def pack_rows(k, v, both, sems):
    rows = k.shape[0]
    copies = [
        pltpu.make_async_copy(k, both.at[0:rows], sems.at[0]),
        pltpu.make_async_copy(v, both.at[rows:], sems.at[1]),
    ]
    for copy in copies:
        copy.start()
    for copy in copies:
        copy.wait()


def plus(*refs):
    refs[-1][...] = refs[0][...] + refs[1][...]


def settle(dkv, dq, e, o, dk_out, dv_out, dq_out, token):
    rows = dq.shape[0]
    token[...] = jnp.zeros(token.shape, F32)
    for n, out in enumerate((dk_out, dv_out, dq_out)):
        s = slice(n * rows, (n + 1) * rows)
        mine = dkv[s, :] if n < 2 else dq[...]
        out[...] = (mine + e[s, :].astype(F32) + o[s, :].astype(F32)).astype(BF)


def split_sums(mine, theirs, _, taps_v, taps_a, gain_v, gain_a):
    total = mine[...] + theirs[...]
    taps_v[...] = total[0:3]
    gain_v[...] = total[3]
    taps_a[...] = total[4:7]
    gain_a[...] = total[7]


def other(i, count):
    return (i + 2 * (i & 1) - 1 + count) & (count - 1)


def groups(heads, size):
    return [range(g, min(g + size, heads)) for g in range(0, heads, size)]


def columns(h):
    return slice(h * HEAD_DIM, (h + 1) * HEAD_DIM)


def pack_stats(tile):
    high = tile.astype(BF).astype(F32)
    rest = tile - high
    middle = rest.astype(BF).astype(F32)
    low = rest - middle
    return (high + pltpu.roll(middle, 16, 1) + pltpu.roll(low, 32, 1)).astype(BF)


def unpack_stats(packed):
    wide = packed.astype(F32)
    return wide + (pltpu.roll(wide, PAD - 16, 1) + pltpu.roll(wide, PAD - 32, 1))


def audio_bias(i, count, window, valid, rows_q, rows_k):
    row = lax.broadcasted_iota(jnp.int32, (rows_k, 4 * rows_q), 0)
    slot = lax.broadcasted_iota(jnp.int32, (rows_k, 4 * rows_q), 1) // rows_q
    position = i * rows_k + row
    blocks = (i, i ^ 1, other(i, count))
    lower, upper = [
        jnp.where(
            slot == 0,
            window[side, blocks[0]],
            jnp.where(slot == 1, window[side, blocks[1]], window[side, blocks[2]]),
        )
        for side in (0, 1)
    ]
    seen = (position >= lower) & (position < upper) & (row < valid[i]) & (slot < 3)
    return jnp.where(seen, 0.0, NEGATIVE)


def padded(own, e, o, c):
    return jnp.concatenate(
        [own[:, c], e[:, c], o[:, c], jnp.zeros((own.shape[0], HEAD_DIM), BF)], 0
    )


def video_bias(i, count, window, valid, rows_q, rows_k):
    row = lax.broadcasted_iota(jnp.int32, (rows_k, rows_q), 0)
    parts = []
    for c in (i, i ^ 1, other(i, count)):
        position = c * rows_k + row
        seen = (position >= window[0, i]) & (position < window[1, i]) & (row < valid[c])
        parts.append(jnp.where(seen, 0.0, NEGATIVE))
    return jnp.concatenate(parts, 0)


def audio_forward(
    count, idx, window, valid, q, qe, qo, k, v, send_e, send_o, own, own_lse, rows_lse, kept,
):
    rows = q.shape[0]
    heads = q.shape[1] // HEAD_DIM
    bias = audio_bias(idx[0], count, window, valid, rows, k.shape[0])
    rows_lse[...] = jnp.zeros(rows_lse.shape, F32)
    for group in groups(heads, heads):
        scores, probs = {}, {}
        for h in group:
            c = columns(h)
            scores[h] = dot(k[:, c], padded(q, qe, qo, c), 1, 1) * FACTOR + bias
        for h in group:
            peak = jnp.max(scores[h], 0, keepdims=True)
            weight = jnp.exp(scores[h] - peak)
            total = jnp.sum(weight, 0, keepdims=True)
            rows_lse[h : h + 1, :] = peak + jnp.log(total)
            probs[h] = (weight * (1.0 / total)).astype(BF)
        for h in group:
            c = columns(h)
            kept[h * k.shape[0] : (h + 1) * k.shape[0], :] = probs[h]
            part = dot(probs[h], v[:, c], 0, 0)
            own[:, c] = part[:rows]
            send_e[:, c] = part[rows : 2 * rows].astype(BF)
            send_o[:, c] = part[2 * rows : 3 * rows].astype(BF)
    tile = jnp.transpose(rows_lse[...])
    own_lse[...] = tile[:rows]
    tail = slice(heads * HEAD_DIM, heads * HEAD_DIM + PAD)
    send_e[:, tail] = pack_stats(tile[rows : 2 * rows])
    send_o[:, tail] = pack_stats(tile[2 * rows : 3 * rows])


def near_columns(own, e, o, c, part):
    rows = own.shape[0]
    s = slice(part * rows, (part + 1) * rows)
    return jnp.concatenate([own[:, c], e[s, c], o[s, c]], 0)


def video_forward(
    count, idx, window, valid, q, k, v, kve, kvo, _, att, kept
):
    rows = q.shape[0]
    heads = q.shape[1] // HEAD_DIM
    i = idx[0]
    bias = video_bias(i, count, window, valid, rows, k.shape[0])
    for group in groups(heads, heads):
        scores, probs = {}, {}
        for h in group:
            c = columns(h)
            keys = near_columns(k, kve, kvo, c, 0)
            scores[h] = dot(keys, q[:, c], 1, 1) * FACTOR + bias
        for h in group:
            peak = jnp.max(scores[h], 0, keepdims=True)
            weight = jnp.exp(scores[h] - peak)
            total = jnp.sum(weight, 0, keepdims=True)
            probs[h] = (weight * (1.0 / total)).astype(BF)
            kept[h * weight.shape[0] : (h + 1) * weight.shape[0], :] = probs[h]
        for h in group:
            c = columns(h)
            att[:, c] = dot(probs[h], near_columns(v, kve, kvo, c, 1), 0, 0).astype(BF)


def audio_combine(
    idx, own, own_lse, re, ro, cot, att_v, att, total, send_e, send_o, first, last
):
    rows = own.shape[0]
    heads = own.shape[1] // HEAD_DIM
    tail = slice(heads * HEAD_DIM, heads * HEAD_DIM + PAD)
    mine = own_lse[...]
    lse_e = unpack_stats(re[:, tail])
    lse_o = unpack_stats(ro[:, tail])
    peak = jnp.maximum(mine, jnp.maximum(lse_e, lse_o))
    whole = peak + jnp.log(
        jnp.exp(mine - peak) + jnp.exp(lse_e - peak) + jnp.exp(lse_o - peak)
    )
    total[...] = whole
    wm, we, wo = jnp.exp(mine - whole), jnp.exp(lse_e - whole), jnp.exp(lse_o - whole)
    first[...] = jnp.zeros(first.shape, F32)
    last[...] = jnp.zeros(last.shape, F32)
    for h in range(heads):
        c = columns(h)
        joined = (
            own[:, c] * wm[:, h : h + 1]
            + re[:, c].astype(F32) * we[:, h : h + 1]
            + ro[:, c].astype(F32) * wo[:, h : h + 1]
        )
        att[:, c] = joined.astype(BF)
        incoming = cot[:, c].astype(F32)
        for edge, pair, only in ((first, 0, 0), (last, rows - 2, rows - 1)):
            edge[h : h + 1, 0:PAD] = joined[pair : pair + 1]
            edge[16 + h : 17 + h, 0:PAD] = joined[pair + 1 : pair + 2]
            edge[h : h + 1, PAD:] = incoming[only : only + 1]
    odd = idx[0] & 1
    for send, side in ((send_e, 1 - odd), (send_o, odd)):
        start = pl.multiple_of(side * (att_v.shape[0] - STRIDE), STRIDE)
        send[:, 0 : heads * HEAD_DIM] = att_v[pl.ds(start, STRIDE), :]
        send[:, heads * HEAD_DIM :] = jnp.where(side == 1, last[...], first[...]).astype(BF)


class Mix:
    def __init__(self, count, idx, refs):
        self.i = idx[0]
        self.even = (self.i & 1) == 0
        self.has_prev = (self.i > 0).astype(F32)
        self.has_next = (self.i < count - 1).astype(F32)
        (self.att_v, self.he, self.ho, self.cot_v, self.att_a, self.cot_a,
         self.conv_v, self.conv_a, self.gain_v, self.gain_a) = refs
        self.chunks = self.att_v.shape[0] // STRIDE
        edges = slice(self.att_v.shape[1], self.att_v.shape[1] + 2 * PAD)
        self.low = self.before(self.he[:, edges], self.ho[:, edges])
        self.high = self.after(self.he[:, edges], self.ho[:, edges])
        self.row = lax.broadcasted_iota(jnp.int32, (8, HEAD_DIM), 0)

    def before(self, e, o):
        return jnp.where(self.even, o.astype(F32), e.astype(F32)) * self.has_prev

    def after(self, e, o):
        return jnp.where(self.even, e.astype(F32), o.astype(F32)) * self.has_next

    def video_att(self, g, c):
        if g < 0:
            return self.before(self.he[:, c], self.ho[:, c])
        if g >= self.chunks:
            return self.after(self.he[:, c], self.ho[:, c])
        return self.att_v[g * STRIDE : (g + 1) * STRIDE, c].astype(F32)

    def video_cot(self, g, c):
        return self.cot_v[g * STRIDE : (g + 1) * STRIDE, c].astype(F32)

    def placed(self, at, value):
        return jnp.where(self.row == at, value, 0.0)

    def audio_att(self, c):
        h = c.start // HEAD_DIM
        low, high = self.low[:, 0:PAD], self.high[:, 0:PAD]
        return jnp.concatenate(
            [
                self.placed(6, low[h : h + 1]) + self.placed(7, low[16 + h : 17 + h]),
                self.att_a[:, c].astype(F32),
                self.placed(0, high[h : h + 1]) + self.placed(1, high[16 + h : 17 + h]),
            ],
            0,
        )

    def audio_cot(self, c):
        h = c.start // HEAD_DIM
        return jnp.concatenate(
            [
                self.placed(7, self.low[h : h + 1, PAD:]),
                self.cot_a[:, c].astype(F32),
                self.placed(0, self.high[h : h + 1, PAD:]),
            ],
            0,
        )

    def audio(self, c):
        att = self.audio_att(c)
        rows = att.shape[0]
        early = pltpu.roll(att, 1, 0)
        late = pltpu.roll(att, rows - 1, 0)
        taps = self.conv_a
        mixed = taps[0:1, c] * early + taps[1:2, c] * att + taps[2:3, c] * late
        cot = self.audio_cot(c)
        return mixed, cot, early, att, late


def video_sums(chunks, att, cot, conv, gain, heads, tile):
    lane = lax.broadcasted_iota(jnp.int32, (STRIDE, PAD), 1)
    for g in chunks:
        square = jnp.zeros((STRIDE, HEAD_DIM), F32)
        inner = jnp.zeros((STRIDE, HEAD_DIM), F32)
        for h in range(heads):
            c = columns(h)
            mixed = (
                conv[0:1, c] * att(g - 1, c)
                + conv[1:2, c] * att(g, c)
                + conv[2:3, c] * att(g + 1, c)
            )
            square += mixed * mixed
            inner += cot(g, c) * gain[0:1, c] * mixed
        tile = jnp.where(lane == g, jnp.sum(square, 1, keepdims=True), tile)
        tile = jnp.where(lane == g + 16, jnp.sum(inner, 1, keepdims=True), tile)
    return tile


def middle_sums(att_v, cot_v, conv, gain, out):
    def chunk(ref):
        return lambda g, c: ref[g * STRIDE : (g + 1) * STRIDE, c].astype(F32)

    chunks = att_v.shape[0] // STRIDE
    heads = att_v.shape[1] // HEAD_DIM
    out[...] = video_sums(
        range(1, chunks - 1), chunk(att_v), chunk(cot_v), conv, gain, heads,
        jnp.zeros((STRIDE, PAD), F32),
    )


def row_sums(count, idx, *refs):
    mix = Mix(count, idx, refs[1:-1])
    stats = refs[-1]
    heads = mix.att_v.shape[1] // HEAD_DIM
    rows_a = mix.att_a.shape[0] + 16
    tile = video_sums(
        (0, mix.chunks - 1), mix.video_att, mix.video_cot, mix.conv_v, mix.gain_v, heads,
        refs[0][...],
    )
    lane_a = lax.broadcasted_iota(jnp.int32, (rows_a, PAD), 1)
    square = jnp.zeros((rows_a, HEAD_DIM), F32)
    inner = jnp.zeros((rows_a, HEAD_DIM), F32)
    for h in range(heads):
        c = columns(h)
        mixed, cot, _, _, _ = mix.audio(c)
        square += mixed * mixed
        inner += cot * mix.gain_a[0:1, c] * mixed
    tile_a = jnp.where(
        lane_a == 0,
        jnp.sum(square, 1, keepdims=True),
        jnp.where(lane_a == 1, jnp.sum(inner, 1, keepdims=True), 0.0),
    )
    stats[0:STRIDE, :] = tile
    stats[STRIDE:, :] = tile_a


def norm_backward(count, width, idx, *refs):
    mix = Mix(count, idx, refs[2:12])
    mine, theirs = refs[0], refs[1]
    total_a = refs[12]
    grad_v, up_a, send_e, send_o, dots_a, parts = refs[13:19]
    scale_ref, shrink_ref = refs[19:21]
    heads = mix.att_v.shape[1] // HEAD_DIM
    sums = mine[...] + theirs[...]
    rows_a = mix.att_a.shape[0]
    ext = rows_a + 16
    for g in range(mix.chunks):
        inverse = lax.rsqrt(sums[0:STRIDE, g : g + 1] / width + EPSILON)
        inner = sums[0:STRIDE, g + 16 : g + 17]
        s = slice(g * STRIDE, (g + 1) * STRIDE)
        scale_ref[s, :] = jnp.broadcast_to(inverse, (STRIDE, HEAD_DIM))
        shrink_ref[s, :] = jnp.broadcast_to(
            inverse * inverse * inverse * inner / width, (STRIDE, HEAD_DIM)
        )
    row = lax.broadcasted_iota(jnp.int32, (ext, HEAD_DIM), 0)
    present = jnp.where(row < 8, mix.has_prev, jnp.where(row >= rows_a + 8, mix.has_next, 1.0))
    inverse = lax.rsqrt(sums[STRIDE:, 0:1] / width + EPSILON)
    scale_a = jnp.broadcast_to(inverse, (ext, HEAD_DIM)) * present
    shrink_a = (
        jnp.broadcast_to(
            inverse * inverse * inverse * sums[STRIDE:, 1:2] / width, (ext, HEAD_DIM)
        )
        * present
    )
    lane = lax.broadcasted_iota(jnp.int32, (rows_a, PAD), 1)
    dots = jnp.zeros((rows_a, PAD), F32)
    own = slice(8, 8 + rows_a)
    for h in range(heads):
        c = columns(h)
        taps = [mix.conv_v[k : k + 1, c] for k in range(3)]
        gain = mix.gain_v[0:1, c]
        sum_taps = [jnp.zeros((STRIDE, HEAD_DIM), F32) for _ in range(3)]
        sum_gain = jnp.zeros((STRIDE, HEAD_DIM), F32)
        atts = [mix.video_att(g, c) for g in (-1, 0, 1)]
        for g in range(mix.chunks):
            mixed = taps[0] * atts[0] + taps[1] * atts[1] + taps[2] * atts[2]
            s = slice(g * STRIDE, (g + 1) * STRIDE)
            scale = scale_ref[s, :]
            incoming = mix.video_cot(g, c)
            grad = scale * (incoming * gain) - mixed * shrink_ref[s, :]
            normed = mixed * scale
            grad_v[s, c] = grad
            sum_gain += incoming * normed
            for k in range(3):
                sum_taps[k] += grad * atts[k]
            if g + 1 < mix.chunks:
                atts = atts[1:] + [mix.video_att(g + 2, c)]
        for k in range(3):
            parts[k : k + 1, c] = jnp.sum(sum_taps[k], 0, keepdims=True)
        parts[3:4, c] = jnp.sum(sum_gain, 0, keepdims=True)

        mixed, cot, early, att, late = mix.audio(c)
        gain = mix.gain_a[0:1, c]
        taps = [mix.conv_a[k : k + 1, c] for k in range(3)]
        normed = mixed * scale_a
        grad = scale_a * (cot * gain) - mixed * shrink_a
        upstream = (
            taps[0] * pltpu.roll(grad, ext - 1, 0)
            + taps[1] * grad
            + taps[2] * pltpu.roll(grad, 1, 0)
        )[own].astype(BF)
        up_a[:, c] = upstream
        send_e[0:rows_a, c] = upstream
        send_o[0:rows_a, c] = upstream
        row_dot = jnp.sum(upstream.astype(F32) * att[own], 1, keepdims=True)
        dots = jnp.where(lane == h, row_dot, dots)
        for k, shifted in enumerate((early, att, late)):
            parts[4 + k : 5 + k, c] = jnp.sum((grad * shifted)[own], 0, keepdims=True)
        parts[7:8, c] = jnp.sum((cot * normed)[own], 0, keepdims=True)
    dots_a[...] = dots
    tail = slice(heads * HEAD_DIM, heads * HEAD_DIM + PAD)
    packed = pack_stats(jnp.where(lane < heads, total_a[...], 0.0)).astype(F32)
    packed_dots = pack_stats(dots).astype(F32)
    packed = (packed + pltpu.roll(packed_dots, 64, 1)).astype(BF)
    odd = idx[0] & 1
    body = slice(0, heads * HEAD_DIM)
    for send, side in ((send_e, 1 - odd), (send_o, odd)):
        start = pl.multiple_of(side * (mix.att_v.shape[0] - STRIDE), STRIDE)
        send[0:rows_a, tail] = packed
        send[rows_a:, body] = grad_v[pl.ds(start, STRIDE), :].astype(BF)
        send[rows_a:, tail] = jnp.zeros((STRIDE, PAD), BF)


def outputs(count, width, idx, *refs):
    mix = Mix(count, idx, refs[2:12])
    sums = refs[0][...] + refs[1][...]
    out_v, out_a, token = refs[13:16]
    token[...] = jnp.zeros(token.shape, F32)
    heads = mix.att_v.shape[1] // HEAD_DIM
    rows_a = mix.att_a.shape[0]
    scales = [
        jnp.broadcast_to(
            lax.rsqrt(sums[0:STRIDE, g : g + 1] / width + EPSILON), (STRIDE, HEAD_DIM)
        )
        for g in range(mix.chunks)
    ]
    scale_a = jnp.broadcast_to(
        lax.rsqrt(sums[STRIDE:, 0:1] / width + EPSILON), (rows_a + 16, HEAD_DIM)
    )
    for h in range(heads):
        c = columns(h)
        taps = [mix.conv_v[k : k + 1, c] for k in range(3)]
        gain = mix.gain_v[0:1, c]
        for g in range(mix.chunks):
            mixed = sum(taps[k] * mix.video_att(g + k - 1, c) for k in range(3))
            s = slice(g * STRIDE, (g + 1) * STRIDE)
            out_v[s, c] = (mixed * scales[g] * gain).astype(BF)
        normed = mix.audio(c)[0] * scale_a
        out_a[:, c] = (normed * mix.gain_a[0:1, c])[8 : 8 + rows_a].astype(BF)


def video_backward(
    count, idx, q, grad, re, ro, conv, kept, k, v, kve, kvo, _,
    dq_far, own, send_e, send_o, dq, sems_out,
):
    rows = q.shape[0]
    heads = q.shape[1] // HEAD_DIM
    back = Stream([(dq, dq_far)], sems_out, heads)
    near = k.shape[0]
    i = idx[0]
    even = (i & 1) == 0
    has_prev = (i > 0).astype(F32)
    has_next = (i < count - 1).astype(F32)
    halo = slice(near, near + STRIDE)
    for group in groups(heads, CHUNK):
        upstream, prob_grad, prob, score_grad = {}, {}, {}, {}
        for h in group:
            c = columns(h)
            first, second = re[halo, c].astype(F32), ro[halo, c].astype(F32)
            before = jnp.where(even, second, first) * has_prev
            after = jnp.where(even, first, second) * has_next
            own_grad = grad[:, c]
            wide = jnp.concatenate([before, own_grad, after], 0)
            upstream[h] = (
                conv[0:1, c] * wide[2 * STRIDE :]
                + conv[1:2, c] * own_grad
                + conv[2:3, c] * wide[0:rows]
            ).astype(BF)
            prob_grad[h] = dot(near_columns(v, kve, kvo, c, 1), upstream[h], 1, 1)
        for h in group:
            prob[h] = kept[h * 3 * near : (h + 1) * 3 * near, :]
            p = prob[h].astype(F32)
            row_dot = jnp.sum(p * prob_grad[h], 0, keepdims=True)
            score_grad[h] = (p * (prob_grad[h] - row_dot)).astype(BF)
        for h in group:
            c = columns(h)
            keys = near_columns(k, kve, kvo, c, 0)
            dq[:, c] = (dot(score_grad[h], keys, 0, 0) * FACTOR).astype(BF)
            dk = dot(score_grad[h], q[:, c], 1, 0) * FACTOR
            dv = dot(prob[h], upstream[h], 1, 0)
            for part, value in enumerate((dk, dv)):
                s = slice(part * near, (part + 1) * near)
                own[s, c] = value[0:near]
                send_e[s, c] = value[near : 2 * near].astype(BF)
                send_o[s, c] = value[2 * near :].astype(BF)
            back.after_head(h)
    back.wait_all()


def audio_backward(
    q, qe, qo, up, re, ro, total, dots, k, v, rows_lse, kept,
    part_e, part_o, dk_far, dv_far, own, send_e, send_o, dk, dv, sems_out,
):
    rows = q.shape[0]
    heads = q.shape[1] // HEAD_DIM
    back = Stream([(dk, dk_far), (dv, dv_far)], sems_out, heads)
    tail = slice(heads * HEAD_DIM, heads * HEAD_DIM + PAD)
    totals, row_dots = [total[...]], [dots[...]]
    for r in (re, ro):
        wide = unpack_stats(r[0:rows, tail])
        totals.append(wide)
        row_dots.append(pltpu.roll(wide, 64, 1))
    blank = jnp.zeros((PAD - 3 * rows, PAD), F32)
    totals = jnp.transpose(jnp.concatenate(totals + [blank], 0))
    share = jnp.exp(rows_lse[...] - totals)
    row_dots = jnp.transpose(jnp.concatenate(row_dots + [blank], 0))
    up_e, up_o = re.at[0:rows], ro.at[0:rows]
    done = slice(0, 2 * rows)
    send_e[done, :] = part_e[...]
    send_o[done, :] = part_o[...]
    for group in groups(heads, CHUNK):
        prob_grad, prob, score_grad = {}, {}, {}
        for h in group:
            c = columns(h)
            prob_grad[h] = dot(v[:, c], padded(up, up_e, up_o, c), 1, 1)
        for h in group:
            p = kept[h * k.shape[0] : (h + 1) * k.shape[0], :].astype(F32) * share[h : h + 1, :]
            score_grad[h] = (p * (prob_grad[h] - row_dots[h : h + 1, :])).astype(BF)
            prob[h] = p.astype(BF)
        for h in group:
            c = columns(h)
            grad = dot(score_grad[h], k[:, c], 0, 0) * FACTOR
            dk[:, c] = (dot(score_grad[h], padded(q, qe, qo, c), 1, 0) * FACTOR).astype(BF)
            dv[:, c] = dot(prob[h], padded(up, up_e, up_o, c), 1, 0).astype(BF)
            own[:, c] = grad[:rows]
            send_e[2 * rows :, c] = grad[rows : 2 * rows].astype(BF)
            send_o[2 * rows :, c] = grad[2 * rows : 3 * rows].astype(BF)
            back.after_head(h)
    back.wait_all()


def per_device(
    query_video,
    key_video,
    value_video,
    query_audio,
    key_audio,
    value_audio,
    conv_video,
    conv_audio,
    gain_video,
    gain_audio,
    video_window,
    audio_window,
    video_valid,
    audio_valid,
    cotangent_video,
    cotangent_audio,
):
    count = video_window.shape[0]
    block = lax.axis_index(BLOCKS)
    idx = block.astype(jnp.int32).reshape(1)
    rows_v, wide = query_video.shape
    rows_a = query_audio.shape[0]
    heads = wide // HEAD_DIM
    model = wide * lax.axis_size("tp")
    even_route = [(i, i ^ 1) for i in range(count)]
    odd_route = [(i, other(i, count)) for i in range(count)]

    def swap_e(x):
        return lax.ppermute(x, BLOCKS, even_route)

    def swap_o(x):
        return lax.ppermute(x, BLOCKS, odd_route)

    def bind(f, *extra):
        def kernel(*refs):
            return f(*extra, *refs)

        return kernel

    qe, qo = swap_e(query_audio), swap_o(query_audio)
    (both,) = call(
        pack_rows, [((2 * rows_a, wide), BF)], [key_audio, value_audio], (), 0.5,
        [pltpu.SemaphoreType.DMA((2,))], (0, 1),
    )
    kve, kvo = swap_e(both), swap_o(both)
    big = pltpu.VMEM((rows_v, wide), BF)

    def sems(count):
        return pltpu.SemaphoreType.DMA((count, heads // CHUNK))

    packed = ((rows_a, wide + PAD), BF)
    audio_info = (idx, audio_window.T, video_valid)
    video_info = (idx, video_window.T, audio_valid)
    rows_shape = ((PAD, PAD), F32)
    send_e, send_o, own_part, own_lse, rows_lse, kept_a = call(
        bind(audio_forward, count),
        [packed, packed, ((rows_a, wide), F32), ((rows_a, PAD), F32), rows_shape,
         ((heads * rows_v, 4 * rows_a), BF)],
        [query_audio, qe, qo, key_video, value_video],
        audio_info,
        1.6,
    )
    pe, po = swap_e(send_e), swap_o(send_o)
    keys_values = [key_audio, value_audio, kve, kvo]
    att_v, kept_v = call(
        bind(video_forward, count),
        [((rows_v, wide), BF), ((heads * 3 * rows_a, rows_v), BF)],
        [query_video] + keys_values + [own_lse],
        video_info,
        1.5,
        (),
        (),
        (),
        (5,),
    )
    halo = ((STRIDE, wide + 2 * PAD), BF)
    att_a, total_a, give_e, give_o = call(
        audio_combine,
        [((rows_a, wide), BF), ((rows_a, PAD), F32), halo, halo],
        [own_part, own_lse, pe, po, cotangent_audio, att_v],
        (idx,),
        0.5,
        [pltpu.VMEM((STRIDE, 2 * PAD), F32)] * 2,
    )
    he, ho = swap_e(give_e), swap_o(give_o)

    mix_args = [
        att_v, he, ho, cotangent_video, att_a, cotangent_audio,
        conv_video, conv_audio, gain_video.reshape(1, wide), gain_audio.reshape(1, wide),
    ]
    stats_rows = STRIDE + rows_a + 16
    (middle,) = call(
        middle_sums,
        [((STRIDE, PAD), F32)],
        [att_v, cotangent_video, conv_video, mix_args[8]],
        (),
        0.7,
    )
    (stats,) = call(
        bind(row_sums, count),
        [((stats_rows, PAD), F32)],
        [middle] + mix_args,
        (idx,),
        0.5,
    )
    tp_size = lax.axis_size("tp")
    stats_other = lax.ppermute(stats, "tp", [(i, i ^ 1) for i in range(tp_size)])
    chunks = rows_v // STRIDE
    both = ((rows_a + STRIDE, wide + PAD), BF)
    grad_v, up_a, back_e, back_o, dots_a, parts = call(
        bind(norm_backward, count, model),
        [
            ((rows_v, wide), F32),
            ((rows_a, wide), BF),
            both,
            both,
            ((rows_a, PAD), F32),
            ((8, wide), F32),
        ],
        [stats, stats_other] + mix_args + [total_a],
        (idx,),
        2.5,
        [pltpu.VMEM((rows_v, HEAD_DIM), F32)] * 2,
    )
    re, ro = swap_e(back_e), swap_o(back_o)

    def moved(x, bits):
        return lax.ppermute(x, BLOCKS, [(i, i ^ bits) for i in range(count)])

    def summed(x, bits, *after):
        (y,) = call(
            plus, [((8, wide), F32)], [x, moved(x, bits)] + list(after), (), 0.5,
            (), (), (), range(2, 2 + len(after)),
        )
        return y

    total = summed(parts, 16)
    out_v, out_a, token = call(
        bind(outputs, count, model),
        [((rows_v, wide), BF), ((rows_a, wide), BF), ((8, PAD), F32)],
        [stats, stats_other] + mix_args + [total],
        (idx,),
        1.5,
        (),
        (),
        (),
        (12,),
    )
    total = summed(total, 32, token)
    total = summed(total, 2)

    two = ((2 * rows_a, wide), BF)
    dq_v, dkv_own, dkv_e, dkv_o = call(
        bind(video_backward, count),
        [((rows_v, wide), BF), ((2 * rows_a, wide), F32), two, two],
        [query_video, grad_v, re, ro, conv_video, kept_v] + keys_values + [total],
        (idx,),
        3.0,
        [big, sems(1)],
        (),
        (0,),
        (10,),
    )
    three = ((3 * rows_a, wide), BF)
    dk_v, dv_v, dq_own, give_e, give_o = call(
        audio_backward,
        [((rows_v, wide), BF), ((rows_v, wide), BF), ((rows_a, wide), F32), three, three],
        [query_audio, qe, qo, up_a, re, ro, total_a, dots_a, key_video, value_video,
         rows_lse, kept_a, dkv_e, dkv_o],
        (),
        3.0,
        [big] * 2 + [sems(2)],
        (),
        (0, 1),
    )
    got_e, got_o = swap_e(give_e), swap_o(give_o)
    total = summed(total, 1, dq_own)
    total = summed(total, 96)
    total = summed(total, 14)
    one = ((rows_a, wide), BF)
    dk_a, dv_a, dq_a, token = call(
        settle,
        [one, one, one, ((8, PAD), F32)],
        [dkv_own, dq_own, got_e, got_o],
        (),
        0.5,
    )
    taps_v, taps_a, gain_v, gain_a = call(
        split_sums,
        [((3, wide), F32), ((3, wide), F32), ((wide,), F32), ((wide,), F32)],
        [total, moved(total, 4), token],
        (),
        0.5,
        (),
        (),
        (),
        (2,),
    )
    return (
        out_v,
        out_a,
        dq_v,
        dk_v,
        dv_v,
        dq_a,
        dk_a,
        dv_a,
        taps_v,
        taps_a,
        gain_v,
        gain_a,
    )


def solution(mesh):
    rows = P(BLOCKS, "tp")
    in_specs = (rows,) * 6 + (P(None, "tp"),) * 2 + (P("tp"),) * 2 + (P(),) * 4 + (rows,) * 2
    out_specs = (rows,) * 8 + (P(None, "tp"),) * 2 + (P("tp"),) * 2
    return jax.shard_map(
        per_device, mesh=mesh, in_specs=in_specs, out_specs=out_specs, check_vma=False
    )
```

```python
import jax
import jax.numpy as jnp
from jax import lax
from jax.experimental import pallas as pl
from jax.experimental.pallas import tpu as pltpu
from jax.sharding import PartitionSpec as P

HEAD_DIM = 128
STRIDE = 32
NEGATIVE = -1e30
EPSILON = 1e-06
FACTOR = HEAD_DIM ** (-0.5)
BLOCKS = ("video", "audio")
BF = jnp.bfloat16
F32 = jnp.float32
PAD = 128


def dot(a, b, over_a, over_b):
    return lax.dot_general(
        a, b, (((over_a,), (over_b,)), ((), ())), preferred_element_type=F32
    )


def call(kernel, outs, args, scalars, micros, scratch=(), far_args=(), far_outs=(), unread=()):
    vmem = pl.BlockSpec(memory_space=pltpu.VMEM)
    smem = pl.BlockSpec(memory_space=pltpu.SMEM)
    anywhere = pl.BlockSpec(memory_space=pl.ANY)
    far = pl.BlockSpec(memory_space=pltpu.HBM)
    size = sum(a.size * a.dtype.itemsize for a in args)
    return pl.pallas_call(
        kernel,
        out_shape=[jax.ShapeDtypeStruct(s, d) for s, d in outs],
        in_specs=[smem] * len(scalars)
        + [
            anywhere if n in unread else far if n in far_args else vmem
            for n in range(len(args))
        ],
        out_specs=[anywhere if n in far_outs else vmem for n in range(len(outs))],
        scratch_shapes=list(scratch),
        compiler_params=pltpu.CompilerParams(vmem_limit_bytes=48 * 1024 * 1024),
        cost_estimate=pl.CostEstimate(
            flops=int(micros * 1.1e9), bytes_accessed=size, transcendentals=0
        ),
    )(*scalars, *args)


CHUNK = 6


class Stream:
    def __init__(self, pairs, sems, heads):
        self.pairs, self.sems = pairs, sems
        self.parts = heads // CHUNK

    def copies(self, part):
        c = slice(part * CHUNK * HEAD_DIM, (part + 1) * CHUNK * HEAD_DIM)
        return [
            pltpu.make_async_copy(src.at[:, c], dst.at[:, c], self.sems.at[n, part])
            for n, (src, dst) in enumerate(self.pairs)
        ]

    def start(self, part):
        for copy in self.copies(part):
            copy.start()

    def wait(self, part):
        for copy in self.copies(part):
            copy.wait()

    def start_all(self):
        for part in range(self.parts):
            self.start(part)

    def wait_all(self):
        for part in range(self.parts):
            self.wait(part)

    def before_head(self, h):
        if h % CHUNK == 0:
            self.wait(h // CHUNK)

    def after_head(self, h):
        if h % CHUNK == CHUNK - 1:
            self.start(h // CHUNK)


def pack_rows(k, v, both, sems):
    rows = k.shape[0]
    copies = [
        pltpu.make_async_copy(k, both.at[0:rows], sems.at[0]),
        pltpu.make_async_copy(v, both.at[rows:], sems.at[1]),
    ]
    for copy in copies:
        copy.start()
    for copy in copies:
        copy.wait()


def plus(*refs):
    refs[-1][...] = refs[0][...] + refs[1][...]


def join(kv_e, q_e, kv_o, q_o, _, send_e, send_o):
    rows = kv_e.shape[0]
    for send, kv, q in ((send_e, kv_e, q_e), (send_o, kv_o, q_o)):
        send[0:rows, :] = kv[...]
        send[rows:, :] = q[...]


def settle(dkv, dq, e, o, dk_out, dv_out, dq_out, token):
    rows = dq.shape[0]
    token[...] = jnp.zeros(token.shape, F32)
    for n, out in enumerate((dk_out, dv_out, dq_out)):
        s = slice(n * rows, (n + 1) * rows)
        mine = dkv[s, :] if n < 2 else dq[...]
        out[...] = (mine + e[s, :].astype(F32) + o[s, :].astype(F32)).astype(BF)


def split_sums(mine, theirs, _, taps_v, taps_a, gain_v, gain_a):
    total = mine[...] + theirs[...]
    taps_v[...] = total[0:3]
    gain_v[...] = total[3]
    taps_a[...] = total[4:7]
    gain_a[...] = total[7]


def other(i, count):
    return (i + 2 * (i & 1) - 1 + count) & (count - 1)


def groups(heads, size):
    return [range(g, min(g + size, heads)) for g in range(0, heads, size)]


def columns(h):
    return slice(h * HEAD_DIM, (h + 1) * HEAD_DIM)


def pack_stats(tile):
    high = tile.astype(BF).astype(F32)
    rest = tile - high
    middle = rest.astype(BF).astype(F32)
    low = rest - middle
    return (high + pltpu.roll(middle, 16, 1) + pltpu.roll(low, 32, 1)).astype(BF)


def unpack_stats(packed):
    wide = packed.astype(F32)
    return wide + (pltpu.roll(wide, PAD - 16, 1) + pltpu.roll(wide, PAD - 32, 1))


def audio_bias(i, count, window, valid, rows_q, rows_k):
    row = lax.broadcasted_iota(jnp.int32, (rows_k, 4 * rows_q), 0)
    slot = lax.broadcasted_iota(jnp.int32, (rows_k, 4 * rows_q), 1) // rows_q
    position = i * rows_k + row
    blocks = (i, i ^ 1, other(i, count))
    lower, upper = [
        jnp.where(
            slot == 0,
            window[side, blocks[0]],
            jnp.where(slot == 1, window[side, blocks[1]], window[side, blocks[2]]),
        )
        for side in (0, 1)
    ]
    seen = (position >= lower) & (position < upper) & (row < valid[i]) & (slot < 3)
    return jnp.where(seen, 0.0, NEGATIVE)


def padded(own, e, o, c):
    return jnp.concatenate(
        [own[:, c], e[:, c], o[:, c], jnp.zeros((own.shape[0], HEAD_DIM), BF)], 0
    )


def video_bias(i, count, window, valid, rows_q, rows_k):
    row = lax.broadcasted_iota(jnp.int32, (rows_k, rows_q), 0)
    parts = []
    for c in (i, i ^ 1, other(i, count)):
        position = c * rows_k + row
        seen = (position >= window[0, i]) & (position < window[1, i]) & (row < valid[c])
        parts.append(jnp.where(seen, 0.0, NEGATIVE))
    return jnp.concatenate(parts, 0)


def audio_forward(
    count, idx, window, valid, q, qe, qo, k, v, send_e, send_o, own, own_lse, rows_lse, kept,
):
    rows = q.shape[0]
    heads = q.shape[1] // HEAD_DIM
    bias = audio_bias(idx[0], count, window, valid, rows, k.shape[0])
    rows_lse[...] = jnp.zeros(rows_lse.shape, F32)
    for group in groups(heads, heads):
        scores, probs = {}, {}
        for h in group:
            c = columns(h)
            scores[h] = dot(k[:, c], padded(q, qe, qo, c), 1, 1) * FACTOR + bias
        for h in group:
            peak = jnp.max(scores[h], 0, keepdims=True)
            weight = jnp.exp(scores[h] - peak)
            total = jnp.sum(weight, 0, keepdims=True)
            rows_lse[h : h + 1, :] = peak + jnp.log(total)
            probs[h] = (weight * (1.0 / total)).astype(BF)
        for h in group:
            c = columns(h)
            kept[h * k.shape[0] : (h + 1) * k.shape[0], :] = probs[h]
            part = dot(probs[h], v[:, c], 0, 0)
            own[:, c] = part[:rows]
            send_e[:, c] = part[rows : 2 * rows].astype(BF)
            send_o[:, c] = part[2 * rows : 3 * rows].astype(BF)
    tile = jnp.transpose(rows_lse[...])
    own_lse[...] = tile[:rows]
    tail = slice(heads * HEAD_DIM, heads * HEAD_DIM + PAD)
    send_e[:, tail] = pack_stats(tile[rows : 2 * rows])
    send_o[:, tail] = pack_stats(tile[2 * rows : 3 * rows])


def near_columns(own, e, o, c, part):
    rows = own.shape[0]
    s = slice(part * rows, (part + 1) * rows)
    return jnp.concatenate([own[:, c], e[s, c], o[s, c]], 0)


def video_forward(
    count, idx, window, valid, q, k, v, kve, kvo, _, att, kept
):
    rows = q.shape[0]
    heads = q.shape[1] // HEAD_DIM
    i = idx[0]
    bias = video_bias(i, count, window, valid, rows, k.shape[0])
    for group in groups(heads, heads):
        scores, probs = {}, {}
        for h in group:
            c = columns(h)
            keys = near_columns(k, kve, kvo, c, 0)
            scores[h] = dot(keys, q[:, c], 1, 1) * FACTOR + bias
        for h in group:
            peak = jnp.max(scores[h], 0, keepdims=True)
            weight = jnp.exp(scores[h] - peak)
            total = jnp.sum(weight, 0, keepdims=True)
            probs[h] = (weight * (1.0 / total)).astype(BF)
            kept[h * weight.shape[0] : (h + 1) * weight.shape[0], :] = probs[h]
        for h in group:
            c = columns(h)
            att[:, c] = dot(probs[h], near_columns(v, kve, kvo, c, 1), 0, 0).astype(BF)


def audio_combine(
    idx, own, own_lse, re, ro, cot, att_v, att, total, send_e, send_o, first, last
):
    rows = own.shape[0]
    heads = own.shape[1] // HEAD_DIM
    tail = slice(heads * HEAD_DIM, heads * HEAD_DIM + PAD)
    mine = own_lse[...]
    lse_e = unpack_stats(re[:, tail])
    lse_o = unpack_stats(ro[:, tail])
    peak = jnp.maximum(mine, jnp.maximum(lse_e, lse_o))
    whole = peak + jnp.log(
        jnp.exp(mine - peak) + jnp.exp(lse_e - peak) + jnp.exp(lse_o - peak)
    )
    total[...] = whole
    wm, we, wo = jnp.exp(mine - whole), jnp.exp(lse_e - whole), jnp.exp(lse_o - whole)
    first[...] = jnp.zeros(first.shape, F32)
    last[...] = jnp.zeros(last.shape, F32)
    for h in range(heads):
        c = columns(h)
        joined = (
            own[:, c] * wm[:, h : h + 1]
            + re[:, c].astype(F32) * we[:, h : h + 1]
            + ro[:, c].astype(F32) * wo[:, h : h + 1]
        )
        att[:, c] = joined.astype(BF)
        incoming = cot[:, c].astype(F32)
        for edge, pair, only in ((first, 0, 0), (last, rows - 2, rows - 1)):
            edge[h : h + 1, 0:PAD] = joined[pair : pair + 1]
            edge[16 + h : 17 + h, 0:PAD] = joined[pair + 1 : pair + 2]
            edge[h : h + 1, PAD:] = incoming[only : only + 1]
    odd = idx[0] & 1
    for send, side in ((send_e, 1 - odd), (send_o, odd)):
        start = pl.multiple_of(side * (att_v.shape[0] - STRIDE), STRIDE)
        send[:, 0 : heads * HEAD_DIM] = att_v[pl.ds(start, STRIDE), :]
        send[:, heads * HEAD_DIM :] = jnp.where(side == 1, last[...], first[...]).astype(BF)


class Mix:
    def __init__(self, count, idx, refs):
        self.i = idx[0]
        self.even = (self.i & 1) == 0
        self.has_prev = (self.i > 0).astype(F32)
        self.has_next = (self.i < count - 1).astype(F32)
        (self.att_v, self.he, self.ho, self.cot_v, self.att_a, self.cot_a,
         self.conv_v, self.conv_a, self.gain_v, self.gain_a) = refs
        self.chunks = self.att_v.shape[0] // STRIDE
        edges = slice(self.att_v.shape[1], self.att_v.shape[1] + 2 * PAD)
        self.low = self.before(self.he[:, edges], self.ho[:, edges])
        self.high = self.after(self.he[:, edges], self.ho[:, edges])
        self.row = lax.broadcasted_iota(jnp.int32, (8, HEAD_DIM), 0)

    def before(self, e, o):
        return jnp.where(self.even, o.astype(F32), e.astype(F32)) * self.has_prev

    def after(self, e, o):
        return jnp.where(self.even, e.astype(F32), o.astype(F32)) * self.has_next

    def video_att(self, g, c):
        if g < 0:
            return self.before(self.he[:, c], self.ho[:, c])
        if g >= self.chunks:
            return self.after(self.he[:, c], self.ho[:, c])
        return self.att_v[g * STRIDE : (g + 1) * STRIDE, c].astype(F32)

    def video_cot(self, g, c):
        return self.cot_v[g * STRIDE : (g + 1) * STRIDE, c].astype(F32)

    def placed(self, at, value):
        return jnp.where(self.row == at, value, 0.0)

    def audio_att(self, c):
        h = c.start // HEAD_DIM
        low, high = self.low[:, 0:PAD], self.high[:, 0:PAD]
        return jnp.concatenate(
            [
                self.placed(6, low[h : h + 1]) + self.placed(7, low[16 + h : 17 + h]),
                self.att_a[:, c].astype(F32),
                self.placed(0, high[h : h + 1]) + self.placed(1, high[16 + h : 17 + h]),
            ],
            0,
        )

    def audio_cot(self, c):
        h = c.start // HEAD_DIM
        return jnp.concatenate(
            [
                self.placed(7, self.low[h : h + 1, PAD:]),
                self.cot_a[:, c].astype(F32),
                self.placed(0, self.high[h : h + 1, PAD:]),
            ],
            0,
        )

    def audio(self, c):
        att = self.audio_att(c)
        rows = att.shape[0]
        early = pltpu.roll(att, 1, 0)
        late = pltpu.roll(att, rows - 1, 0)
        taps = self.conv_a
        mixed = taps[0:1, c] * early + taps[1:2, c] * att + taps[2:3, c] * late
        cot = self.audio_cot(c)
        return mixed, cot, early, att, late


def video_sums(chunks, att, cot, conv, gain, heads, tile):
    lane = lax.broadcasted_iota(jnp.int32, (STRIDE, PAD), 1)
    for g in chunks:
        square = jnp.zeros((STRIDE, HEAD_DIM), F32)
        inner = jnp.zeros((STRIDE, HEAD_DIM), F32)
        for h in range(heads):
            c = columns(h)
            mixed = (
                conv[0:1, c] * att(g - 1, c)
                + conv[1:2, c] * att(g, c)
                + conv[2:3, c] * att(g + 1, c)
            )
            square += mixed * mixed
            inner += cot(g, c) * gain[0:1, c] * mixed
        tile = jnp.where(lane == g, jnp.sum(square, 1, keepdims=True), tile)
        tile = jnp.where(lane == g + 16, jnp.sum(inner, 1, keepdims=True), tile)
    return tile


def middle_sums(att_v, cot_v, conv, gain, out):
    def chunk(ref):
        return lambda g, c: ref[g * STRIDE : (g + 1) * STRIDE, c].astype(F32)

    chunks = att_v.shape[0] // STRIDE
    heads = att_v.shape[1] // HEAD_DIM
    out[...] = video_sums(
        range(1, chunks - 1), chunk(att_v), chunk(cot_v), conv, gain, heads,
        jnp.zeros((STRIDE, PAD), F32),
    )


def row_sums(count, idx, *refs):
    mix = Mix(count, idx, refs[1:-1])
    stats = refs[-1]
    heads = mix.att_v.shape[1] // HEAD_DIM
    rows_a = mix.att_a.shape[0] + 16
    tile = video_sums(
        (0, mix.chunks - 1), mix.video_att, mix.video_cot, mix.conv_v, mix.gain_v, heads,
        refs[0][...],
    )
    lane_a = lax.broadcasted_iota(jnp.int32, (rows_a, PAD), 1)
    square = jnp.zeros((rows_a, HEAD_DIM), F32)
    inner = jnp.zeros((rows_a, HEAD_DIM), F32)
    for h in range(heads):
        c = columns(h)
        mixed, cot, _, _, _ = mix.audio(c)
        square += mixed * mixed
        inner += cot * mix.gain_a[0:1, c] * mixed
    tile_a = jnp.where(
        lane_a == 0,
        jnp.sum(square, 1, keepdims=True),
        jnp.where(lane_a == 1, jnp.sum(inner, 1, keepdims=True), 0.0),
    )
    stats[0:STRIDE, :] = tile
    stats[STRIDE:, :] = tile_a


def norm_backward(count, width, idx, *refs):
    mix = Mix(count, idx, refs[2:12])
    mine, theirs = refs[0], refs[1]
    total_a = refs[12]
    grad_v, up_a, send_e, send_o, dots_a, parts = refs[13:19]
    scale_ref, shrink_ref = refs[19:21]
    heads = mix.att_v.shape[1] // HEAD_DIM
    sums = mine[...] + theirs[...]
    rows_a = mix.att_a.shape[0]
    ext = rows_a + 16
    for g in range(mix.chunks):
        inverse = lax.rsqrt(sums[0:STRIDE, g : g + 1] / width + EPSILON)
        inner = sums[0:STRIDE, g + 16 : g + 17]
        s = slice(g * STRIDE, (g + 1) * STRIDE)
        scale_ref[s, :] = jnp.broadcast_to(inverse, (STRIDE, HEAD_DIM))
        shrink_ref[s, :] = jnp.broadcast_to(
            inverse * inverse * inverse * inner / width, (STRIDE, HEAD_DIM)
        )
    row = lax.broadcasted_iota(jnp.int32, (ext, HEAD_DIM), 0)
    present = jnp.where(row < 8, mix.has_prev, jnp.where(row >= rows_a + 8, mix.has_next, 1.0))
    inverse = lax.rsqrt(sums[STRIDE:, 0:1] / width + EPSILON)
    scale_a = jnp.broadcast_to(inverse, (ext, HEAD_DIM)) * present
    shrink_a = (
        jnp.broadcast_to(
            inverse * inverse * inverse * sums[STRIDE:, 1:2] / width, (ext, HEAD_DIM)
        )
        * present
    )
    lane = lax.broadcasted_iota(jnp.int32, (rows_a, PAD), 1)
    dots = jnp.zeros((rows_a, PAD), F32)
    own = slice(8, 8 + rows_a)
    for h in range(heads):
        c = columns(h)
        taps = [mix.conv_v[k : k + 1, c] for k in range(3)]
        gain = mix.gain_v[0:1, c]
        sum_taps = [jnp.zeros((STRIDE, HEAD_DIM), F32) for _ in range(3)]
        sum_gain = jnp.zeros((STRIDE, HEAD_DIM), F32)
        atts = [mix.video_att(g, c) for g in (-1, 0, 1)]
        for g in range(mix.chunks):
            mixed = taps[0] * atts[0] + taps[1] * atts[1] + taps[2] * atts[2]
            s = slice(g * STRIDE, (g + 1) * STRIDE)
            scale = scale_ref[s, :]
            incoming = mix.video_cot(g, c)
            grad = scale * (incoming * gain) - mixed * shrink_ref[s, :]
            normed = mixed * scale
            grad_v[s, c] = grad
            sum_gain += incoming * normed
            for k in range(3):
                sum_taps[k] += grad * atts[k]
            if g + 1 < mix.chunks:
                atts = atts[1:] + [mix.video_att(g + 2, c)]
        for k in range(3):
            parts[k : k + 1, c] = jnp.sum(sum_taps[k], 0, keepdims=True)
        parts[3:4, c] = jnp.sum(sum_gain, 0, keepdims=True)

        mixed, cot, early, att, late = mix.audio(c)
        gain = mix.gain_a[0:1, c]
        taps = [mix.conv_a[k : k + 1, c] for k in range(3)]
        normed = mixed * scale_a
        grad = scale_a * (cot * gain) - mixed * shrink_a
        upstream = (
            taps[0] * pltpu.roll(grad, ext - 1, 0)
            + taps[1] * grad
            + taps[2] * pltpu.roll(grad, 1, 0)
        )[own].astype(BF)
        up_a[:, c] = upstream
        send_e[0:rows_a, c] = upstream
        send_o[0:rows_a, c] = upstream
        row_dot = jnp.sum(upstream.astype(F32) * att[own], 1, keepdims=True)
        dots = jnp.where(lane == h, row_dot, dots)
        for k, shifted in enumerate((early, att, late)):
            parts[4 + k : 5 + k, c] = jnp.sum((grad * shifted)[own], 0, keepdims=True)
        parts[7:8, c] = jnp.sum((cot * normed)[own], 0, keepdims=True)
    dots_a[...] = dots
    tail = slice(heads * HEAD_DIM, heads * HEAD_DIM + PAD)
    packed = pack_stats(jnp.where(lane < heads, total_a[...], 0.0)).astype(F32)
    packed_dots = pack_stats(dots).astype(F32)
    packed = (packed + pltpu.roll(packed_dots, 64, 1)).astype(BF)
    odd = idx[0] & 1
    body = slice(0, heads * HEAD_DIM)
    for send, side in ((send_e, 1 - odd), (send_o, odd)):
        start = pl.multiple_of(side * (mix.att_v.shape[0] - STRIDE), STRIDE)
        send[0:rows_a, tail] = packed
        send[rows_a:, body] = grad_v[pl.ds(start, STRIDE), :].astype(BF)
        send[rows_a:, tail] = jnp.zeros((STRIDE, PAD), BF)


def outputs(count, width, idx, *refs):
    mix = Mix(count, idx, refs[2:12])
    sums = refs[0][...] + refs[1][...]
    out_v, out_a, token = refs[13:16]
    token[...] = jnp.zeros(token.shape, F32)
    heads = mix.att_v.shape[1] // HEAD_DIM
    rows_a = mix.att_a.shape[0]
    scales = [
        jnp.broadcast_to(
            lax.rsqrt(sums[0:STRIDE, g : g + 1] / width + EPSILON), (STRIDE, HEAD_DIM)
        )
        for g in range(mix.chunks)
    ]
    scale_a = jnp.broadcast_to(
        lax.rsqrt(sums[STRIDE:, 0:1] / width + EPSILON), (rows_a + 16, HEAD_DIM)
    )
    for h in range(heads):
        c = columns(h)
        taps = [mix.conv_v[k : k + 1, c] for k in range(3)]
        gain = mix.gain_v[0:1, c]
        for g in range(mix.chunks):
            mixed = sum(taps[k] * mix.video_att(g + k - 1, c) for k in range(3))
            s = slice(g * STRIDE, (g + 1) * STRIDE)
            out_v[s, c] = (mixed * scales[g] * gain).astype(BF)
        normed = mix.audio(c)[0] * scale_a
        out_a[:, c] = (normed * mix.gain_a[0:1, c])[8 : 8 + rows_a].astype(BF)


def video_backward(
    count, idx, q, grad, re, ro, conv, kept, k, v, kve, kvo, _,
    dq_far, own, send_e, send_o, dq, sems_out,
):
    rows = q.shape[0]
    heads = q.shape[1] // HEAD_DIM
    back = Stream([(dq, dq_far)], sems_out, heads)
    near = k.shape[0]
    i = idx[0]
    even = (i & 1) == 0
    has_prev = (i > 0).astype(F32)
    has_next = (i < count - 1).astype(F32)
    halo = slice(near, near + STRIDE)
    for group in groups(heads, CHUNK):
        upstream, prob_grad, prob, score_grad = {}, {}, {}, {}
        for h in group:
            c = columns(h)
            first, second = re[halo, c].astype(F32), ro[halo, c].astype(F32)
            before = jnp.where(even, second, first) * has_prev
            after = jnp.where(even, first, second) * has_next
            own_grad = grad[:, c]
            wide = jnp.concatenate([before, own_grad, after], 0)
            upstream[h] = (
                conv[0:1, c] * wide[2 * STRIDE :]
                + conv[1:2, c] * own_grad
                + conv[2:3, c] * wide[0:rows]
            ).astype(BF)
            prob_grad[h] = dot(near_columns(v, kve, kvo, c, 1), upstream[h], 1, 1)
        for h in group:
            prob[h] = kept[h * 3 * near : (h + 1) * 3 * near, :]
            p = prob[h].astype(F32)
            row_dot = jnp.sum(p * prob_grad[h], 0, keepdims=True)
            score_grad[h] = (p * (prob_grad[h] - row_dot)).astype(BF)
        for h in group:
            c = columns(h)
            keys = near_columns(k, kve, kvo, c, 0)
            dq[:, c] = (dot(score_grad[h], keys, 0, 0) * FACTOR).astype(BF)
            dk = dot(score_grad[h], q[:, c], 1, 0) * FACTOR
            dv = dot(prob[h], upstream[h], 1, 0)
            for part, value in enumerate((dk, dv)):
                s = slice(part * near, (part + 1) * near)
                own[s, c] = value[0:near]
                send_e[s, c] = value[near : 2 * near].astype(BF)
                send_o[s, c] = value[2 * near :].astype(BF)
            back.after_head(h)
    back.wait_all()


def audio_backward(
    q, qe, qo, up, re, ro, total, dots, k, v, rows_lse, kept,
    dk_far, dv_far, own, send_e, send_o, dk, dv, sems_out,
):
    rows = q.shape[0]
    heads = q.shape[1] // HEAD_DIM
    back = Stream([(dk, dk_far), (dv, dv_far)], sems_out, heads)
    tail = slice(heads * HEAD_DIM, heads * HEAD_DIM + PAD)
    totals, row_dots = [total[...]], [dots[...]]
    for r in (re, ro):
        wide = unpack_stats(r[0:rows, tail])
        totals.append(wide)
        row_dots.append(pltpu.roll(wide, 64, 1))
    blank = jnp.zeros((PAD - 3 * rows, PAD), F32)
    totals = jnp.transpose(jnp.concatenate(totals + [blank], 0))
    share = jnp.exp(rows_lse[...] - totals)
    row_dots = jnp.transpose(jnp.concatenate(row_dots + [blank], 0))
    up_e, up_o = re.at[0:rows], ro.at[0:rows]
    for group in groups(heads, CHUNK):
        prob_grad, prob, score_grad = {}, {}, {}
        for h in group:
            c = columns(h)
            prob_grad[h] = dot(v[:, c], padded(up, up_e, up_o, c), 1, 1)
        for h in group:
            p = kept[h * k.shape[0] : (h + 1) * k.shape[0], :].astype(F32) * share[h : h + 1, :]
            score_grad[h] = (p * (prob_grad[h] - row_dots[h : h + 1, :])).astype(BF)
            prob[h] = p.astype(BF)
        for h in group:
            c = columns(h)
            grad = dot(score_grad[h], k[:, c], 0, 0) * FACTOR
            dk[:, c] = (dot(score_grad[h], padded(q, qe, qo, c), 1, 0) * FACTOR).astype(BF)
            dv[:, c] = dot(prob[h], padded(up, up_e, up_o, c), 1, 0).astype(BF)
            own[:, c] = grad[:rows]
            send_e[:, c] = grad[rows : 2 * rows].astype(BF)
            send_o[:, c] = grad[2 * rows : 3 * rows].astype(BF)
            back.after_head(h)
    back.wait_all()


def per_device(
    query_video,
    key_video,
    value_video,
    query_audio,
    key_audio,
    value_audio,
    conv_video,
    conv_audio,
    gain_video,
    gain_audio,
    video_window,
    audio_window,
    video_valid,
    audio_valid,
    cotangent_video,
    cotangent_audio,
):
    count = video_window.shape[0]
    block = lax.axis_index(BLOCKS)
    idx = block.astype(jnp.int32).reshape(1)
    rows_v, wide = query_video.shape
    rows_a = query_audio.shape[0]
    heads = wide // HEAD_DIM
    model = wide * lax.axis_size("tp")
    even_route = [(i, i ^ 1) for i in range(count)]
    odd_route = [(i, other(i, count)) for i in range(count)]

    def swap_e(x):
        return lax.ppermute(x, BLOCKS, even_route)

    def swap_o(x):
        return lax.ppermute(x, BLOCKS, odd_route)

    def bind(f, *extra):
        def kernel(*refs):
            return f(*extra, *refs)

        return kernel

    qe, qo = swap_e(query_audio), swap_o(query_audio)
    (both,) = call(
        pack_rows, [((2 * rows_a, wide), BF)], [key_audio, value_audio], (), 0.5,
        [pltpu.SemaphoreType.DMA((2,))], (0, 1),
    )
    kve, kvo = swap_e(both), swap_o(both)
    big = pltpu.VMEM((rows_v, wide), BF)

    def sems(count):
        return pltpu.SemaphoreType.DMA((count, heads // CHUNK))

    packed = ((rows_a, wide + PAD), BF)
    audio_info = (idx, audio_window.T, video_valid)
    video_info = (idx, video_window.T, audio_valid)
    rows_shape = ((PAD, PAD), F32)
    send_e, send_o, own_part, own_lse, rows_lse, kept_a = call(
        bind(audio_forward, count),
        [packed, packed, ((rows_a, wide), F32), ((rows_a, PAD), F32), rows_shape,
         ((heads * rows_v, 4 * rows_a), BF)],
        [query_audio, qe, qo, key_video, value_video],
        audio_info,
        1.6,
    )
    pe, po = swap_e(send_e), swap_o(send_o)
    keys_values = [key_audio, value_audio, kve, kvo]
    att_v, kept_v = call(
        bind(video_forward, count),
        [((rows_v, wide), BF), ((heads * 3 * rows_a, rows_v), BF)],
        [query_video] + keys_values + [own_lse],
        video_info,
        1.5,
        (),
        (),
        (),
        (5,),
    )
    halo = ((STRIDE, wide + 2 * PAD), BF)
    att_a, total_a, give_e, give_o = call(
        audio_combine,
        [((rows_a, wide), BF), ((rows_a, PAD), F32), halo, halo],
        [own_part, own_lse, pe, po, cotangent_audio, att_v],
        (idx,),
        0.5,
        [pltpu.VMEM((STRIDE, 2 * PAD), F32)] * 2,
    )
    he, ho = swap_e(give_e), swap_o(give_o)

    mix_args = [
        att_v, he, ho, cotangent_video, att_a, cotangent_audio,
        conv_video, conv_audio, gain_video.reshape(1, wide), gain_audio.reshape(1, wide),
    ]
    stats_rows = STRIDE + rows_a + 16
    (middle,) = call(
        middle_sums,
        [((STRIDE, PAD), F32)],
        [att_v, cotangent_video, conv_video, mix_args[8]],
        (),
        0.7,
    )
    (stats,) = call(
        bind(row_sums, count),
        [((stats_rows, PAD), F32)],
        [middle] + mix_args,
        (idx,),
        0.5,
    )
    tp_size = lax.axis_size("tp")
    stats_other = lax.ppermute(stats, "tp", [(i, i ^ 1) for i in range(tp_size)])
    chunks = rows_v // STRIDE
    both = ((rows_a + STRIDE, wide + PAD), BF)
    grad_v, up_a, back_e, back_o, dots_a, parts = call(
        bind(norm_backward, count, model),
        [
            ((rows_v, wide), F32),
            ((rows_a, wide), BF),
            both,
            both,
            ((rows_a, PAD), F32),
            ((8, wide), F32),
        ],
        [stats, stats_other] + mix_args + [total_a],
        (idx,),
        2.5,
        [pltpu.VMEM((rows_v, HEAD_DIM), F32)] * 2,
    )
    re, ro = swap_e(back_e), swap_o(back_o)

    def moved(x, bits):
        return lax.ppermute(x, BLOCKS, [(i, i ^ bits) for i in range(count)])

    def summed(x, bits, *after, micros=0.5):
        (y,) = call(
            plus, [((8, wide), F32)], [x, moved(x, bits)] + list(after), (), micros,
            (), (), (), range(2, 2 + len(after)),
        )
        return y

    total = summed(parts, 16)
    out_v, out_a, token = call(
        bind(outputs, count, model),
        [((rows_v, wide), BF), ((rows_a, wide), BF), ((8, PAD), F32)],
        [stats, stats_other] + mix_args + [total],
        (idx,),
        1.5,
        (),
        (),
        (),
        (12,),
    )
    total = summed(total, 32, token)
    total = summed(total, 2)

    two = ((2 * rows_a, wide), BF)
    dq_v, dkv_own, dkv_e, dkv_o = call(
        bind(video_backward, count),
        [((rows_v, wide), BF), ((2 * rows_a, wide), F32), two, two],
        [query_video, grad_v, re, ro, conv_video, kept_v] + keys_values + [total],
        (idx,),
        3.0,
        [big, sems(1)],
        (),
        (0,),
        (10,),
    )
    one = ((rows_a, wide), BF)
    dk_v, dv_v, dq_own, dq_e, dq_o = call(
        audio_backward,
        [((rows_v, wide), BF), ((rows_v, wide), BF), ((rows_a, wide), F32), one, one],
        [query_audio, qe, qo, up_a, re, ro, total_a, dots_a, key_video, value_video,
         rows_lse, kept_a],
        (),
        3.0,
        [big] * 2 + [sems(2)],
        (),
        (0, 1),
    )
    total = summed(total, 1, dq_own, dkv_own)
    three = ((3 * rows_a, wide), BF)
    give_e, give_o = call(
        join, [three, three], [dkv_e, dq_e, dkv_o, dq_o, total], (), 0.4,
        (), (), (), (4,),
    )
    got_e, got_o = swap_e(give_e), swap_o(give_o)
    total = summed(total, 96, micros=1.0)
    total = summed(total, 14, micros=1.0)
    one = ((rows_a, wide), BF)
    dk_a, dv_a, dq_a, token = call(
        settle,
        [one, one, one, ((8, PAD), F32)],
        [dkv_own, dq_own, got_e, got_o],
        (),
        0.5,
    )
    taps_v, taps_a, gain_v, gain_a = call(
        split_sums,
        [((3, wide), F32), ((3, wide), F32), ((wide,), F32), ((wide,), F32)],
        [total, moved(total, 4), token],
        (),
        0.5,
        (),
        (),
        (),
        (2,),
    )
    return (
        out_v,
        out_a,
        dq_v,
        dk_v,
        dv_v,
        dq_a,
        dk_a,
        dv_a,
        taps_v,
        taps_a,
        gain_v,
        gain_a,
    )


def solution(mesh):
    rows = P(BLOCKS, "tp")
    in_specs = (rows,) * 6 + (P(None, "tp"),) * 2 + (P("tp"),) * 2 + (P(),) * 4 + (rows,) * 2
    out_specs = (rows,) * 8 + (P(None, "tp"),) * 2 + (P("tp"),) * 2
    return jax.shard_map(
        per_device, mesh=mesh, in_specs=in_specs, out_specs=out_specs, check_vma=False
    )
```

```python
import jax
import jax.numpy as jnp
from jax import lax
from jax.experimental import pallas as pl
from jax.experimental.pallas import tpu as pltpu
from jax.sharding import PartitionSpec as P

HEAD_DIM = 128
STRIDE = 32
NEGATIVE = -1e30
EPSILON = 1e-06
FACTOR = HEAD_DIM ** (-0.5)
BLOCKS = ("video", "audio")
BF = jnp.bfloat16
F32 = jnp.float32
PAD = 128


def dot(a, b, over_a, over_b):
    return lax.dot_general(
        a, b, (((over_a,), (over_b,)), ((), ())), preferred_element_type=F32
    )


def call(kernel, outs, args, scalars, micros, scratch=(), far_args=(), far_outs=(), unread=()):
    vmem = pl.BlockSpec(memory_space=pltpu.VMEM)
    smem = pl.BlockSpec(memory_space=pltpu.SMEM)
    anywhere = pl.BlockSpec(memory_space=pl.ANY)
    far = pl.BlockSpec(memory_space=pltpu.HBM)
    size = sum(a.size * a.dtype.itemsize for a in args)
    return pl.pallas_call(
        kernel,
        out_shape=[jax.ShapeDtypeStruct(s, d) for s, d in outs],
        in_specs=[smem] * len(scalars)
        + [
            anywhere if n in unread else far if n in far_args else vmem
            for n in range(len(args))
        ],
        out_specs=[anywhere if n in far_outs else vmem for n in range(len(outs))],
        scratch_shapes=list(scratch),
        compiler_params=pltpu.CompilerParams(vmem_limit_bytes=48 * 1024 * 1024),
        cost_estimate=pl.CostEstimate(
            flops=int(micros * 1.1e9), bytes_accessed=size, transcendentals=0
        ),
    )(*scalars, *args)


CHUNK = 6


class Stream:
    def __init__(self, pairs, sems, heads):
        self.pairs, self.sems = pairs, sems
        self.parts = heads // CHUNK

    def copies(self, part):
        c = slice(part * CHUNK * HEAD_DIM, (part + 1) * CHUNK * HEAD_DIM)
        return [
            pltpu.make_async_copy(src.at[:, c], dst.at[:, c], self.sems.at[n, part])
            for n, (src, dst) in enumerate(self.pairs)
        ]

    def start(self, part):
        for copy in self.copies(part):
            copy.start()

    def wait(self, part):
        for copy in self.copies(part):
            copy.wait()

    def start_all(self):
        for part in range(self.parts):
            self.start(part)

    def wait_all(self):
        for part in range(self.parts):
            self.wait(part)

    def before_head(self, h):
        if h % CHUNK == 0:
            self.wait(h // CHUNK)

    def after_head(self, h):
        if h % CHUNK == CHUNK - 1:
            self.start(h // CHUNK)


def pack_rows(k, v, both, sems):
    rows = k.shape[0]
    copies = [
        pltpu.make_async_copy(k, both.at[0:rows], sems.at[0]),
        pltpu.make_async_copy(v, both.at[rows:], sems.at[1]),
    ]
    for copy in copies:
        copy.start()
    for copy in copies:
        copy.wait()


def plus(*refs):
    refs[-1][...] = refs[0][...] + refs[1][...]


def join(kv_e, q_e, kv_o, q_o, _, send_e, send_o):
    rows = kv_e.shape[0]
    for send, kv, q in ((send_e, kv_e, q_e), (send_o, kv_o, q_o)):
        send[0:rows, :] = kv[...]
        send[rows:, :] = q[...]


def settle(dkv, dq, e, o, dk_out, dv_out, dq_out, token):
    rows = dq.shape[0]
    token[...] = jnp.zeros(token.shape, F32)
    for n, out in enumerate((dk_out, dv_out, dq_out)):
        s = slice(n * rows, (n + 1) * rows)
        mine = dkv[s, :] if n < 2 else dq[...]
        out[...] = (mine + e[s, :].astype(F32) + o[s, :].astype(F32)).astype(BF)


def split_sums(mine, theirs, _, taps_v, taps_a, gain_v, gain_a):
    total = mine[...] + theirs[...]
    taps_v[...] = total[0:3]
    gain_v[...] = total[3]
    taps_a[...] = total[4:7]
    gain_a[...] = total[7]


def other(i, count):
    return (i + 2 * (i & 1) - 1 + count) & (count - 1)


def groups(heads, size):
    return [range(g, min(g + size, heads)) for g in range(0, heads, size)]


def columns(h):
    return slice(h * HEAD_DIM, (h + 1) * HEAD_DIM)


def pack_stats(tile):
    high = tile.astype(BF).astype(F32)
    rest = tile - high
    middle = rest.astype(BF).astype(F32)
    low = rest - middle
    return (high + pltpu.roll(middle, 16, 1) + pltpu.roll(low, 32, 1)).astype(BF)


def unpack_stats(packed):
    wide = packed.astype(F32)
    return wide + (pltpu.roll(wide, PAD - 16, 1) + pltpu.roll(wide, PAD - 32, 1))


def audio_bias(i, count, window, valid, rows_q, rows_k):
    row = lax.broadcasted_iota(jnp.int32, (rows_k, 4 * rows_q), 0)
    slot = lax.broadcasted_iota(jnp.int32, (rows_k, 4 * rows_q), 1) // rows_q
    position = i * rows_k + row
    blocks = (i, i ^ 1, other(i, count))
    lower, upper = [
        jnp.where(
            slot == 0,
            window[side, blocks[0]],
            jnp.where(slot == 1, window[side, blocks[1]], window[side, blocks[2]]),
        )
        for side in (0, 1)
    ]
    seen = (position >= lower) & (position < upper) & (row < valid[i]) & (slot < 3)
    return jnp.where(seen, 0.0, NEGATIVE)


def padded(own, e, o, c):
    return jnp.concatenate(
        [own[:, c], e[:, c], o[:, c], jnp.zeros((own.shape[0], HEAD_DIM), BF)], 0
    )


def video_bias(i, count, window, valid, rows_q, rows_k):
    row = lax.broadcasted_iota(jnp.int32, (rows_k, rows_q), 0)
    parts = []
    for c in (i, i ^ 1, other(i, count)):
        position = c * rows_k + row
        seen = (position >= window[0, i]) & (position < window[1, i]) & (row < valid[c])
        parts.append(jnp.where(seen, 0.0, NEGATIVE))
    return jnp.concatenate(parts, 0)


def audio_forward(
    count, idx, window, valid, q, qe, qo, k, v, send_e, send_o, own, own_lse, rows_lse, kept,
):
    rows = q.shape[0]
    heads = q.shape[1] // HEAD_DIM
    bias = audio_bias(idx[0], count, window, valid, rows, k.shape[0])
    rows_lse[...] = jnp.zeros(rows_lse.shape, F32)
    for group in groups(heads, heads):
        scores, probs = {}, {}
        for h in group:
            c = columns(h)
            scores[h] = dot(k[:, c], padded(q, qe, qo, c), 1, 1) * FACTOR + bias
        for h in group:
            peak = jnp.max(scores[h], 0, keepdims=True)
            weight = jnp.exp(scores[h] - peak)
            total = jnp.sum(weight, 0, keepdims=True)
            rows_lse[h : h + 1, :] = peak + jnp.log(total)
            probs[h] = (weight * (1.0 / total)).astype(BF)
        for h in group:
            c = columns(h)
            kept[h * k.shape[0] : (h + 1) * k.shape[0], :] = probs[h]
            part = dot(probs[h], v[:, c], 0, 0)
            own[:, c] = part[:rows]
            send_e[:, c] = part[rows : 2 * rows].astype(BF)
            send_o[:, c] = part[2 * rows : 3 * rows].astype(BF)
    tile = jnp.transpose(rows_lse[...])
    own_lse[...] = tile[:rows]
    tail = slice(heads * HEAD_DIM, heads * HEAD_DIM + PAD)
    send_e[:, tail] = pack_stats(tile[rows : 2 * rows])
    send_o[:, tail] = pack_stats(tile[2 * rows : 3 * rows])


def near_columns(own, e, o, c, part):
    rows = own.shape[0]
    s = slice(part * rows, (part + 1) * rows)
    return jnp.concatenate([own[:, c], e[s, c], o[s, c]], 0)


def video_forward(
    count, idx, window, valid, q, k, v, kve, kvo, _, att, kept
):
    rows = q.shape[0]
    heads = q.shape[1] // HEAD_DIM
    i = idx[0]
    bias = video_bias(i, count, window, valid, rows, k.shape[0])
    for group in groups(heads, heads):
        scores, probs = {}, {}
        for h in group:
            c = columns(h)
            keys = near_columns(k, kve, kvo, c, 0)
            scores[h] = dot(keys, q[:, c], 1, 1) * FACTOR + bias
        for h in group:
            peak = jnp.max(scores[h], 0, keepdims=True)
            weight = jnp.exp(scores[h] - peak)
            total = jnp.sum(weight, 0, keepdims=True)
            probs[h] = (weight * (1.0 / total)).astype(BF)
            kept[h * weight.shape[0] : (h + 1) * weight.shape[0], :] = probs[h]
        for h in group:
            c = columns(h)
            att[:, c] = dot(probs[h], near_columns(v, kve, kvo, c, 1), 0, 0).astype(BF)


def audio_combine(
    idx, own, own_lse, re, ro, cot, att_v, att, total, send_e, send_o, first, last
):
    rows = own.shape[0]
    heads = own.shape[1] // HEAD_DIM
    tail = slice(heads * HEAD_DIM, heads * HEAD_DIM + PAD)
    mine = own_lse[...]
    lse_e = unpack_stats(re[:, tail])
    lse_o = unpack_stats(ro[:, tail])
    peak = jnp.maximum(mine, jnp.maximum(lse_e, lse_o))
    whole = peak + jnp.log(
        jnp.exp(mine - peak) + jnp.exp(lse_e - peak) + jnp.exp(lse_o - peak)
    )
    total[...] = whole
    wm, we, wo = jnp.exp(mine - whole), jnp.exp(lse_e - whole), jnp.exp(lse_o - whole)
    first[...] = jnp.zeros(first.shape, F32)
    last[...] = jnp.zeros(last.shape, F32)
    for h in range(heads):
        c = columns(h)
        joined = (
            own[:, c] * wm[:, h : h + 1]
            + re[:, c].astype(F32) * we[:, h : h + 1]
            + ro[:, c].astype(F32) * wo[:, h : h + 1]
        )
        att[:, c] = joined.astype(BF)
        incoming = cot[:, c].astype(F32)
        for edge, pair, only in ((first, 0, 0), (last, rows - 2, rows - 1)):
            edge[h : h + 1, 0:PAD] = joined[pair : pair + 1]
            edge[16 + h : 17 + h, 0:PAD] = joined[pair + 1 : pair + 2]
            edge[h : h + 1, PAD:] = incoming[only : only + 1]
    odd = idx[0] & 1
    for send, side in ((send_e, 1 - odd), (send_o, odd)):
        start = pl.multiple_of(side * (att_v.shape[0] - STRIDE), STRIDE)
        send[:, 0 : heads * HEAD_DIM] = att_v[pl.ds(start, STRIDE), :]
        send[:, heads * HEAD_DIM :] = jnp.where(side == 1, last[...], first[...]).astype(BF)


class Mix:
    def __init__(self, count, idx, refs):
        self.i = idx[0]
        self.even = (self.i & 1) == 0
        self.has_prev = (self.i > 0).astype(F32)
        self.has_next = (self.i < count - 1).astype(F32)
        (self.att_v, self.he, self.ho, self.cot_v, self.att_a, self.cot_a,
         self.conv_v, self.conv_a, self.gain_v, self.gain_a) = refs
        self.chunks = self.att_v.shape[0] // STRIDE
        edges = slice(self.att_v.shape[1], self.att_v.shape[1] + 2 * PAD)
        self.low = self.before(self.he[:, edges], self.ho[:, edges])
        self.high = self.after(self.he[:, edges], self.ho[:, edges])
        self.row = lax.broadcasted_iota(jnp.int32, (8, HEAD_DIM), 0)

    def before(self, e, o):
        return jnp.where(self.even, o.astype(F32), e.astype(F32)) * self.has_prev

    def after(self, e, o):
        return jnp.where(self.even, e.astype(F32), o.astype(F32)) * self.has_next

    def video_att(self, g, c):
        if g < 0:
            return self.before(self.he[:, c], self.ho[:, c])
        if g >= self.chunks:
            return self.after(self.he[:, c], self.ho[:, c])
        return self.att_v[g * STRIDE : (g + 1) * STRIDE, c].astype(F32)

    def video_cot(self, g, c):
        return self.cot_v[g * STRIDE : (g + 1) * STRIDE, c].astype(F32)

    def placed(self, at, value):
        return jnp.where(self.row == at, value, 0.0)

    def audio_att(self, c):
        h = c.start // HEAD_DIM
        low, high = self.low[:, 0:PAD], self.high[:, 0:PAD]
        return jnp.concatenate(
            [
                self.placed(6, low[h : h + 1]) + self.placed(7, low[16 + h : 17 + h]),
                self.att_a[:, c].astype(F32),
                self.placed(0, high[h : h + 1]) + self.placed(1, high[16 + h : 17 + h]),
            ],
            0,
        )

    def audio_cot(self, c):
        h = c.start // HEAD_DIM
        return jnp.concatenate(
            [
                self.placed(7, self.low[h : h + 1, PAD:]),
                self.cot_a[:, c].astype(F32),
                self.placed(0, self.high[h : h + 1, PAD:]),
            ],
            0,
        )

    def audio(self, c):
        att = self.audio_att(c)
        rows = att.shape[0]
        early = pltpu.roll(att, 1, 0)
        late = pltpu.roll(att, rows - 1, 0)
        taps = self.conv_a
        mixed = taps[0:1, c] * early + taps[1:2, c] * att + taps[2:3, c] * late
        cot = self.audio_cot(c)
        return mixed, cot, early, att, late


def video_sums(chunks, att, cot, conv, gain, heads, tile):
    lane = lax.broadcasted_iota(jnp.int32, (STRIDE, PAD), 1)
    for g in chunks:
        square = jnp.zeros((STRIDE, HEAD_DIM), F32)
        inner = jnp.zeros((STRIDE, HEAD_DIM), F32)
        for h in range(heads):
            c = columns(h)
            mixed = (
                conv[0:1, c] * att(g - 1, c)
                + conv[1:2, c] * att(g, c)
                + conv[2:3, c] * att(g + 1, c)
            )
            square += mixed * mixed
            inner += cot(g, c) * gain[0:1, c] * mixed
        tile = jnp.where(lane == g, jnp.sum(square, 1, keepdims=True), tile)
        tile = jnp.where(lane == g + 16, jnp.sum(inner, 1, keepdims=True), tile)
    return tile


def middle_sums(att_v, cot_v, conv, gain, out):
    def chunk(ref):
        return lambda g, c: ref[g * STRIDE : (g + 1) * STRIDE, c].astype(F32)

    chunks = att_v.shape[0] // STRIDE
    heads = att_v.shape[1] // HEAD_DIM
    out[...] = video_sums(
        range(1, chunks - 1), chunk(att_v), chunk(cot_v), conv, gain, heads,
        jnp.zeros((STRIDE, PAD), F32),
    )


def row_sums(count, idx, *refs):
    mix = Mix(count, idx, refs[1:-1])
    stats = refs[-1]
    heads = mix.att_v.shape[1] // HEAD_DIM
    rows_a = mix.att_a.shape[0] + 16
    tile = video_sums(
        (0, mix.chunks - 1), mix.video_att, mix.video_cot, mix.conv_v, mix.gain_v, heads,
        refs[0][...],
    )
    lane_a = lax.broadcasted_iota(jnp.int32, (rows_a, PAD), 1)
    square = jnp.zeros((rows_a, HEAD_DIM), F32)
    inner = jnp.zeros((rows_a, HEAD_DIM), F32)
    for h in range(heads):
        c = columns(h)
        mixed, cot, _, _, _ = mix.audio(c)
        square += mixed * mixed
        inner += cot * mix.gain_a[0:1, c] * mixed
    tile_a = jnp.where(
        lane_a == 0,
        jnp.sum(square, 1, keepdims=True),
        jnp.where(lane_a == 1, jnp.sum(inner, 1, keepdims=True), 0.0),
    )
    stats[0:STRIDE, :] = tile
    stats[STRIDE:, :] = tile_a


def norm_backward(count, width, idx, *refs):
    mix = Mix(count, idx, refs[2:12])
    mine, theirs = refs[0], refs[1]
    total_a = refs[12]
    grad_v, up_a, send_e, send_o, dots_a, parts = refs[13:19]
    scale_ref, shrink_ref = refs[19:21]
    heads = mix.att_v.shape[1] // HEAD_DIM
    sums = mine[...] + theirs[...]
    rows_a = mix.att_a.shape[0]
    ext = rows_a + 16
    for g in range(mix.chunks):
        inverse = lax.rsqrt(sums[0:STRIDE, g : g + 1] / width + EPSILON)
        inner = sums[0:STRIDE, g + 16 : g + 17]
        s = slice(g * STRIDE, (g + 1) * STRIDE)
        scale_ref[s, :] = jnp.broadcast_to(inverse, (STRIDE, HEAD_DIM))
        shrink_ref[s, :] = jnp.broadcast_to(
            inverse * inverse * inverse * inner / width, (STRIDE, HEAD_DIM)
        )
    row = lax.broadcasted_iota(jnp.int32, (ext, HEAD_DIM), 0)
    present = jnp.where(row < 8, mix.has_prev, jnp.where(row >= rows_a + 8, mix.has_next, 1.0))
    inverse = lax.rsqrt(sums[STRIDE:, 0:1] / width + EPSILON)
    scale_a = jnp.broadcast_to(inverse, (ext, HEAD_DIM)) * present
    shrink_a = (
        jnp.broadcast_to(
            inverse * inverse * inverse * sums[STRIDE:, 1:2] / width, (ext, HEAD_DIM)
        )
        * present
    )
    lane = lax.broadcasted_iota(jnp.int32, (rows_a, PAD), 1)
    dots = jnp.zeros((rows_a, PAD), F32)
    own = slice(8, 8 + rows_a)
    for h in range(heads):
        c = columns(h)
        taps = [mix.conv_v[k : k + 1, c] for k in range(3)]
        gain = mix.gain_v[0:1, c]
        sum_taps = [jnp.zeros((STRIDE, HEAD_DIM), F32) for _ in range(3)]
        sum_gain = jnp.zeros((STRIDE, HEAD_DIM), F32)
        atts = [mix.video_att(g, c) for g in (-1, 0, 1)]
        for g in range(mix.chunks):
            mixed = taps[0] * atts[0] + taps[1] * atts[1] + taps[2] * atts[2]
            s = slice(g * STRIDE, (g + 1) * STRIDE)
            scale = scale_ref[s, :]
            incoming = mix.video_cot(g, c)
            grad = scale * (incoming * gain) - mixed * shrink_ref[s, :]
            normed = mixed * scale
            grad_v[s, c] = grad
            sum_gain += incoming * normed
            for k in range(3):
                sum_taps[k] += grad * atts[k]
            if g + 1 < mix.chunks:
                atts = atts[1:] + [mix.video_att(g + 2, c)]
        for k in range(3):
            parts[k : k + 1, c] = jnp.sum(sum_taps[k], 0, keepdims=True)
        parts[3:4, c] = jnp.sum(sum_gain, 0, keepdims=True)

        mixed, cot, early, att, late = mix.audio(c)
        gain = mix.gain_a[0:1, c]
        taps = [mix.conv_a[k : k + 1, c] for k in range(3)]
        normed = mixed * scale_a
        grad = scale_a * (cot * gain) - mixed * shrink_a
        upstream = (
            taps[0] * pltpu.roll(grad, ext - 1, 0)
            + taps[1] * grad
            + taps[2] * pltpu.roll(grad, 1, 0)
        )[own].astype(BF)
        up_a[:, c] = upstream
        send_e[0:rows_a, c] = upstream
        send_o[0:rows_a, c] = upstream
        row_dot = jnp.sum(upstream.astype(F32) * att[own], 1, keepdims=True)
        dots = jnp.where(lane == h, row_dot, dots)
        for k, shifted in enumerate((early, att, late)):
            parts[4 + k : 5 + k, c] = jnp.sum((grad * shifted)[own], 0, keepdims=True)
        parts[7:8, c] = jnp.sum((cot * normed)[own], 0, keepdims=True)
    dots_a[...] = dots
    tail = slice(heads * HEAD_DIM, heads * HEAD_DIM + PAD)
    packed = pack_stats(jnp.where(lane < heads, total_a[...], 0.0)).astype(F32)
    packed_dots = pack_stats(dots).astype(F32)
    packed = (packed + pltpu.roll(packed_dots, 64, 1)).astype(BF)
    odd = idx[0] & 1
    body = slice(0, heads * HEAD_DIM)
    for send, side in ((send_e, 1 - odd), (send_o, odd)):
        start = pl.multiple_of(side * (mix.att_v.shape[0] - STRIDE), STRIDE)
        send[0:rows_a, tail] = packed
        send[rows_a:, body] = grad_v[pl.ds(start, STRIDE), :].astype(BF)
        send[rows_a:, tail] = jnp.zeros((STRIDE, PAD), BF)


def outputs(count, width, idx, *refs):
    mix = Mix(count, idx, refs[2:12])
    sums = refs[0][...] + refs[1][...]
    out_v, out_a, token = refs[13:16]
    token[...] = jnp.zeros(token.shape, F32)
    heads = mix.att_v.shape[1] // HEAD_DIM
    rows_a = mix.att_a.shape[0]
    scales = [
        jnp.broadcast_to(
            lax.rsqrt(sums[0:STRIDE, g : g + 1] / width + EPSILON), (STRIDE, HEAD_DIM)
        )
        for g in range(mix.chunks)
    ]
    scale_a = jnp.broadcast_to(
        lax.rsqrt(sums[STRIDE:, 0:1] / width + EPSILON), (rows_a + 16, HEAD_DIM)
    )
    for h in range(heads):
        c = columns(h)
        taps = [mix.conv_v[k : k + 1, c] for k in range(3)]
        gain = mix.gain_v[0:1, c]
        for g in range(mix.chunks):
            mixed = sum(taps[k] * mix.video_att(g + k - 1, c) for k in range(3))
            s = slice(g * STRIDE, (g + 1) * STRIDE)
            out_v[s, c] = (mixed * scales[g] * gain).astype(BF)
        normed = mix.audio(c)[0] * scale_a
        out_a[:, c] = (normed * mix.gain_a[0:1, c])[8 : 8 + rows_a].astype(BF)


def video_backward(
    count, idx, q, grad, re, ro, conv, kept, k, v, kve, kvo, _,
    dq_far, own, send_e, send_o, dq, sems_out,
):
    rows = q.shape[0]
    heads = q.shape[1] // HEAD_DIM
    back = Stream([(dq, dq_far)], sems_out, heads)
    near = k.shape[0]
    i = idx[0]
    even = (i & 1) == 0
    has_prev = (i > 0).astype(F32)
    has_next = (i < count - 1).astype(F32)
    halo = slice(near, near + STRIDE)
    for group in groups(heads, CHUNK):
        upstream, prob_grad, prob, score_grad = {}, {}, {}, {}
        for h in group:
            c = columns(h)
            first, second = re[halo, c].astype(F32), ro[halo, c].astype(F32)
            before = jnp.where(even, second, first) * has_prev
            after = jnp.where(even, first, second) * has_next
            own_grad = grad[:, c]
            wide = jnp.concatenate([before, own_grad, after], 0)
            upstream[h] = (
                conv[0:1, c] * wide[2 * STRIDE :]
                + conv[1:2, c] * own_grad
                + conv[2:3, c] * wide[0:rows]
            ).astype(BF)
            prob_grad[h] = dot(near_columns(v, kve, kvo, c, 1), upstream[h], 1, 1)
        for h in group:
            prob[h] = kept[h * 3 * near : (h + 1) * 3 * near, :]
            p = prob[h].astype(F32)
            row_dot = jnp.sum(p * prob_grad[h], 0, keepdims=True)
            score_grad[h] = (p * (prob_grad[h] - row_dot)).astype(BF)
        for h in group:
            c = columns(h)
            keys = near_columns(k, kve, kvo, c, 0)
            dq[:, c] = (dot(score_grad[h], keys, 0, 0) * FACTOR).astype(BF)
            dk = dot(score_grad[h], q[:, c], 1, 0) * FACTOR
            dv = dot(prob[h], upstream[h], 1, 0)
            for part, value in enumerate((dk, dv)):
                s = slice(part * near, (part + 1) * near)
                own[s, c] = value[0:near]
                send_e[s, c] = value[near : 2 * near].astype(BF)
                send_o[s, c] = value[2 * near :].astype(BF)
            back.after_head(h)
    back.wait_all()


def audio_backward(
    q, qe, qo, up, re, ro, total, dots, k, v, rows_lse, kept,
    dk_far, dv_far, own, send_e, send_o, dk, dv, sems_out,
):
    rows = q.shape[0]
    heads = q.shape[1] // HEAD_DIM
    back = Stream([(dk, dk_far), (dv, dv_far)], sems_out, heads)
    tail = slice(heads * HEAD_DIM, heads * HEAD_DIM + PAD)
    totals, row_dots = [total[...]], [dots[...]]
    for r in (re, ro):
        wide = unpack_stats(r[0:rows, tail])
        totals.append(wide)
        row_dots.append(pltpu.roll(wide, 64, 1))
    blank = jnp.zeros((PAD - 3 * rows, PAD), F32)
    totals = jnp.transpose(jnp.concatenate(totals + [blank], 0))
    share = jnp.exp(rows_lse[...] - totals)
    row_dots = jnp.transpose(jnp.concatenate(row_dots + [blank], 0))
    up_e, up_o = re.at[0:rows], ro.at[0:rows]
    for group in groups(heads, CHUNK):
        prob_grad, prob, score_grad = {}, {}, {}
        for h in group:
            c = columns(h)
            prob_grad[h] = dot(v[:, c], padded(up, up_e, up_o, c), 1, 1)
        for h in group:
            p = kept[h * k.shape[0] : (h + 1) * k.shape[0], :].astype(F32) * share[h : h + 1, :]
            score_grad[h] = (p * (prob_grad[h] - row_dots[h : h + 1, :])).astype(BF)
            prob[h] = p.astype(BF)
        for h in group:
            c = columns(h)
            grad = dot(score_grad[h], k[:, c], 0, 0) * FACTOR
            dk[:, c] = (dot(score_grad[h], padded(q, qe, qo, c), 1, 0) * FACTOR).astype(BF)
            dv[:, c] = dot(prob[h], padded(up, up_e, up_o, c), 1, 0).astype(BF)
            own[:, c] = grad[:rows]
            send_e[:, c] = grad[rows : 2 * rows].astype(BF)
            send_o[:, c] = grad[2 * rows : 3 * rows].astype(BF)
            back.after_head(h)
    back.wait_all()


def per_device(
    query_video,
    key_video,
    value_video,
    query_audio,
    key_audio,
    value_audio,
    conv_video,
    conv_audio,
    gain_video,
    gain_audio,
    video_window,
    audio_window,
    video_valid,
    audio_valid,
    cotangent_video,
    cotangent_audio,
):
    count = video_window.shape[0]
    block = lax.axis_index(BLOCKS)
    idx = block.astype(jnp.int32).reshape(1)
    rows_v, wide = query_video.shape
    rows_a = query_audio.shape[0]
    heads = wide // HEAD_DIM
    model = wide * lax.axis_size("tp")
    even_route = [(i, i ^ 1) for i in range(count)]
    odd_route = [(i, other(i, count)) for i in range(count)]

    def swap_e(x):
        return lax.ppermute(x, BLOCKS, even_route)

    def swap_o(x):
        return lax.ppermute(x, BLOCKS, odd_route)

    def bind(f, *extra):
        def kernel(*refs):
            return f(*extra, *refs)

        return kernel

    qe, qo = swap_e(query_audio), swap_o(query_audio)
    (both,) = call(
        pack_rows, [((2 * rows_a, wide), BF)], [key_audio, value_audio], (), 0.5,
        [pltpu.SemaphoreType.DMA((2,))], (0, 1),
    )
    kve, kvo = swap_e(both), swap_o(both)
    big = pltpu.VMEM((rows_v, wide), BF)

    def sems(count):
        return pltpu.SemaphoreType.DMA((count, heads // CHUNK))

    packed = ((rows_a, wide + PAD), BF)
    audio_info = (idx, audio_window.T, video_valid)
    video_info = (idx, video_window.T, audio_valid)
    rows_shape = ((PAD, PAD), F32)
    send_e, send_o, own_part, own_lse, rows_lse, kept_a = call(
        bind(audio_forward, count),
        [packed, packed, ((rows_a, wide), F32), ((rows_a, PAD), F32), rows_shape,
         ((heads * rows_v, 4 * rows_a), BF)],
        [query_audio, qe, qo, key_video, value_video],
        audio_info,
        1.6,
    )
    pe, po = swap_e(send_e), swap_o(send_o)
    keys_values = [key_audio, value_audio, kve, kvo]
    att_v, kept_v = call(
        bind(video_forward, count),
        [((rows_v, wide), BF), ((heads * 3 * rows_a, rows_v), BF)],
        [query_video] + keys_values + [own_lse],
        video_info,
        1.5,
        (),
        (),
        (),
        (5,),
    )
    halo = ((STRIDE, wide + 2 * PAD), BF)
    att_a, total_a, give_e, give_o = call(
        audio_combine,
        [((rows_a, wide), BF), ((rows_a, PAD), F32), halo, halo],
        [own_part, own_lse, pe, po, cotangent_audio, att_v],
        (idx,),
        0.5,
        [pltpu.VMEM((STRIDE, 2 * PAD), F32)] * 2,
    )
    he, ho = swap_e(give_e), swap_o(give_o)

    mix_args = [
        att_v, he, ho, cotangent_video, att_a, cotangent_audio,
        conv_video, conv_audio, gain_video.reshape(1, wide), gain_audio.reshape(1, wide),
    ]
    stats_rows = STRIDE + rows_a + 16
    (middle,) = call(
        middle_sums,
        [((STRIDE, PAD), F32)],
        [att_v, cotangent_video, conv_video, mix_args[8]],
        (),
        0.7,
    )
    (stats,) = call(
        bind(row_sums, count),
        [((stats_rows, PAD), F32)],
        [middle] + mix_args,
        (idx,),
        0.5,
    )
    tp_size = lax.axis_size("tp")
    stats_other = lax.ppermute(stats, "tp", [(i, i ^ 1) for i in range(tp_size)])
    chunks = rows_v // STRIDE
    both = ((rows_a + STRIDE, wide + PAD), BF)
    grad_v, up_a, back_e, back_o, dots_a, parts = call(
        bind(norm_backward, count, model),
        [
            ((rows_v, wide), F32),
            ((rows_a, wide), BF),
            both,
            both,
            ((rows_a, PAD), F32),
            ((8, wide), F32),
        ],
        [stats, stats_other] + mix_args + [total_a],
        (idx,),
        2.5,
        [pltpu.VMEM((rows_v, HEAD_DIM), F32)] * 2,
    )
    re, ro = swap_e(back_e), swap_o(back_o)

    def moved(x, bits):
        return lax.ppermute(x, BLOCKS, [(i, i ^ bits) for i in range(count)])

    def summed(x, bits, *after, micros=0.5):
        (y,) = call(
            plus, [((8, wide), F32)], [x, moved(x, bits)] + list(after), (), micros,
            (), (), (), range(2, 2 + len(after)),
        )
        return y

    total = summed(parts, 16)
    out_v, out_a, token = call(
        bind(outputs, count, model),
        [((rows_v, wide), BF), ((rows_a, wide), BF), ((8, PAD), F32)],
        [stats, stats_other] + mix_args + [total],
        (idx,),
        1.5,
        (),
        (),
        (),
        (12,),
    )
    total = summed(total, 32, token)
    total = summed(total, 2)

    two = ((2 * rows_a, wide), BF)
    dq_v, dkv_own, dkv_e, dkv_o = call(
        bind(video_backward, count),
        [((rows_v, wide), BF), ((2 * rows_a, wide), F32), two, two],
        [query_video, grad_v, re, ro, conv_video, kept_v] + keys_values + [total],
        (idx,),
        3.0,
        [big, sems(1)],
        (),
        (0,),
        (10,),
    )
    one = ((rows_a, wide), BF)
    dk_v, dv_v, dq_own, dq_e, dq_o = call(
        audio_backward,
        [((rows_v, wide), BF), ((rows_v, wide), BF), ((rows_a, wide), F32), one, one],
        [query_audio, qe, qo, up_a, re, ro, total_a, dots_a, key_video, value_video,
         rows_lse, kept_a],
        (),
        3.0,
        [big] * 2 + [sems(2)],
        (),
        (0, 1),
    )
    total = summed(total, 1, dq_own, dkv_own)
    three = ((3 * rows_a, wide), BF)
    give_e, give_o = call(
        join, [three, three], [dkv_e, dq_e, dkv_o, dq_o, total], (), 0.4,
        (), (), (), (4,),
    )
    got_e, got_o = swap_e(give_e), swap_o(give_o)
    total = summed(total, 14, micros=1.0)
    total = summed(total, 96, micros=1.0)
    one = ((rows_a, wide), BF)
    dk_a, dv_a, dq_a, token = call(
        settle,
        [one, one, one, ((8, PAD), F32)],
        [dkv_own, dq_own, got_e, got_o],
        (),
        0.5,
    )
    taps_v, taps_a, gain_v, gain_a = call(
        split_sums,
        [((3, wide), F32), ((3, wide), F32), ((wide,), F32), ((wide,), F32)],
        [total, moved(total, 4), token],
        (),
        0.5,
        (),
        (),
        (),
        (2,),
    )
    return (
        out_v,
        out_a,
        dq_v,
        dk_v,
        dv_v,
        dq_a,
        dk_a,
        dv_a,
        taps_v,
        taps_a,
        gain_v,
        gain_a,
    )


def solution(mesh):
    rows = P(BLOCKS, "tp")
    in_specs = (rows,) * 6 + (P(None, "tp"),) * 2 + (P("tp"),) * 2 + (P(),) * 4 + (rows,) * 2
    out_specs = (rows,) * 8 + (P(None, "tp"),) * 2 + (P("tp"),) * 2
    return jax.shard_map(
        per_device, mesh=mesh, in_specs=in_specs, out_specs=out_specs, check_vma=False
    )
```
